128 devices in a mesh: row: 16 (over y, x_lo, core), col: 8 (over z, x_hi).
Axes of the slice: x: 4 (x_hi: 2, x_lo: 2; x = x_hi * 2 + x_lo), y: 4, z: 4, core: 2. Of those that a mesh axis runs over, the one named last changes fastest.
Arguments:
- pair: bfloat16 [2048, 2048, 128], P('row', 'col'), may hold values from -6 to 6
- counts: int32 [16, 128], replicated, may hold values from 1 to 24, 1024 in all within a row
- atom_single: bfloat16 [16384, 128], P(('row', 'col')), may hold values from -6 to 6
- w_bias: float32 [128, 4], replicated, may hold values from -24 to 24
- w_project: bfloat16 [128, 512], replicated, may hold values from -0.5 to 0.5
- w_out: bfloat16 [128, 128], replicated, may hold values from -0.5 to 0.5
- w_trans_in: bfloat16 [128, 512], replicated, may hold values from -0.5 to 0.5
- w_trans_out: bfloat16 [256, 128], replicated, may hold values from -0.375 to 0.375
- w_token: bfloat16 [128, 384], replicated, may hold values from -0.5 to 0.5
- w_row: bfloat16 [384, 128], replicated, may hold values from -0.3125 to 0.3125
- w_col: bfloat16 [384, 128], replicated, may hold values from -0.3125 to 0.3125
Outputs:
- atom_out: bfloat16 [16384, 128], P(('row', 'col'))
- token_single: bfloat16 [2048, 384], P('row')
- new_pair: bfloat16 [2048, 2048, 128], P('row', 'col')
The draws below stay inside these ranges and needn't reach their ends.
Inputs may be any that keep to these rules, and one draw needn't show every extreme that they name: Each row of counts sums to 1024, so the atoms of row group r belong to tokens r * 128 to r * 128 + 127.
All inputs are finite; a program needn't handle non-finite values.
Results may differ from the reference program's by a relative error of at most 0.017.
Values may be sent and summed in bfloat16 or wider, within the bound.
A program may use at most 64 MiB of HBM per device.

```python
import math
import jax
import jax.numpy as jnp
import numpy as np
from jax import lax

C_PAIR = 128
C_ATOM = 128
C_TOKEN = 384
HEADS = 4
Q_WIN = 32
K_WIN = 128
MOST = 24
TOK_ROW = 128
TOKENS = 2048
ATOMS = 16384
ROW_ATOMS = 1024
N_ROW = 16


def draw_w_bias(key, part):
    key = jax.random.fold_in(key, 7)
    base = jnp.clip(jax.random.normal(key, (C_PAIR, HEADS), jnp.float32), -4.0, 4.0)
    return jnp.clip(base * 1.5 / math.sqrt(C_PAIR), -24.0, 24.0)


def shard_levels(own_key, dims, split, least, top_value):
    def one(axis_at, shards_of):
        draws = jax.random.uniform(jax.random.fold_in(jax.random.fold_in(own_key, 6), axis_at), (shards_of,), jnp.float32, least / len(split), top_value / len(split))
        return jnp.repeat(jnp.exp(draws), dims[axis_at] // shards_of).reshape((-1,) + (1,) * (len(dims) - axis_at - 1))

    factor_of = one(*split[0])
    for cut in split[1:]:
        factor_of = factor_of * one(*cut)
    return factor_of


def profile(amount, total, bound, skew):
    weights = [(1 << 20) // math.isqrt(rank ** skew) + 1 for rank in range(2, amount + 1)]
    surplus, given = total - bound - (amount - 1), [1] * (amount - 1)
    while surplus > 0:
        free = [i for i in range(amount - 1) if given[i] < bound]
        pool, left = sum([weights[i] for i in free]), surplus
        for i in free:
            more = min(bound - given[i], max(1, left * weights[i] // pool), surplus)
            given[i] = given[i] + more
            surplus = surplus - more
    return np.array([bound] + given)


def ragged(key, amount, total, bound, slope):
    if amount == 2:
        one = jax.random.randint(key, (), max(1, total - bound), min(bound, total - 1) + 1)
        return jnp.stack([one, total - one])
    sizes = jnp.asarray(profile(amount, total, bound, slope), jnp.int32)
    couples = (amount - 1) // 2
    giver, sink = sizes[1:1 + 2 * couples:2], sizes[2:2 + 2 * couples:2]
    slack = jnp.minimum(giver - 1, bound - sink)
    shifted = jax.random.randint(jax.random.fold_in(key, 1), (couples,), 0, 1 << 20) % (slack + 1)
    sizes = sizes.at[1:1 + 2 * couples:2].set(giver - shifted).at[2:2 + 2 * couples:2].set(sink + shifted)
    return sizes[jax.random.permutation(jax.random.fold_in(key, 2), amount)]


def gaussian(own_key, shape, width, limit, pieces=(), held_as=jnp.bfloat16):
    level = shard_levels(own_key, shape, pieces, -0.22, 0.18) if pieces else 1.0
    result = jax.random.normal(own_key, shape, jnp.float32) * width * level
    return jnp.minimum(jnp.maximum(result, -limit), limit).astype(held_as)


def setup_inputs(seed: int = 0) -> dict:
    key_of = jax.random.split(jax.random.key(seed), 12)
    pair = gaussian(key_of[0], (TOKENS, TOKENS, C_PAIR), 1.0, 6.0, ((0, 16), (1, 8)))
    counts = jax.vmap(lambda own: ragged(own, TOK_ROW, ROW_ATOMS, MOST, 2))(jax.random.split(key_of[1], N_ROW)).reshape((N_ROW, TOK_ROW)).astype(jnp.int32)
    atom_single = gaussian(key_of[2], (ATOMS, C_ATOM), 1.0, 6.0, ((0, 128),))
    w_bias = draw_w_bias(jax.random.fold_in(key_of[11], 71), 0)
    w_project = gaussian(key_of[4], (C_ATOM, 4 * C_ATOM), C_ATOM ** -0.5, 0.5)
    w_out = gaussian(key_of[5], (C_ATOM, C_ATOM), C_ATOM ** -0.5, 0.5)
    w_trans_in = gaussian(key_of[6], (C_ATOM, 4 * C_ATOM), C_ATOM ** -0.5, 0.5)
    w_trans_out = gaussian(key_of[7], (2 * C_ATOM, C_ATOM), (2 * C_ATOM) ** -0.5, 0.375)
    w_token = gaussian(key_of[8], (C_ATOM, C_TOKEN), C_ATOM ** -0.5, 0.5)
    w_row = gaussian(key_of[9], (C_TOKEN, C_PAIR), C_TOKEN ** -0.5, 0.3125)
    w_col = gaussian(key_of[10], (C_TOKEN, C_PAIR), C_TOKEN ** -0.5, 0.3125)
    return dict(pair=pair, counts=counts, atom_single=atom_single, w_bias=w_bias, w_project=w_project, w_out=w_out, w_trans_in=w_trans_in, w_trans_out=w_trans_out, w_token=w_token, w_row=w_row, w_col=w_col)


def normalize(values):
    values = values.astype(jnp.float32)
    average = lax.optimization_barrier(jnp.mean(values, -1, keepdims=True))
    centred = values - average
    spread = lax.optimization_barrier(jnp.mean(centred * centred, -1, keepdims=True))
    return centred * lax.rsqrt(spread + 1e-05)

def window_keys(rimmed, windows):
    shaped = rimmed.reshape((windows + K_WIN // Q_WIN - 1, Q_WIN) + rimmed.shape[1:])
    return jnp.concatenate([shaped[offset:offset + windows] for offset in range(K_WIN // Q_WIN)], axis=1)

def reference(pair, counts, atom_single, w_bias, w_project, w_out, w_trans_in, w_trans_out, w_token, w_row, w_col):
    f32 = jnp.float32
    bf16 = jnp.bfloat16
    token_ends = jnp.cumsum(counts.reshape(-1)).astype(jnp.int32)
    margin = (K_WIN - Q_WIN) // 2
    windows = ATOMS // Q_WIN
    head_dim = C_ATOM // HEADS

    def bias_block(pair_rows):
        return jnp.einsum('ijc,ch->hij', normalize(pair_rows), w_bias.astype(f32), precision=lax.Precision.HIGHEST).astype(bf16)
    bias_full = lax.map(bias_block, pair.reshape(N_ROW, TOK_ROW, TOKENS, C_PAIR))
    bias_full = bias_full.transpose(1, 0, 2, 3).reshape(HEADS, TOKENS, TOKENS)
    positions = jnp.arange(ATOMS + 2 * margin, dtype=jnp.int32) - margin
    in_range = (positions >= 0) & (positions < ATOMS)
    token_ext = jnp.searchsorted(token_ends, jnp.clip(positions, 0, ATOMS - 1), side='right').astype(jnp.int32)
    token_of = token_ext[margin:margin + ATOMS]
    atom_norm = normalize(atom_single).astype(bf16)
    projected = jnp.dot(atom_norm, w_project, preferred_element_type=f32)
    queries = (projected[:, :C_ATOM] * head_dim ** (-0.5)).astype(bf16)
    keyval = projected[:, C_ATOM:3 * C_ATOM].astype(bf16)
    gate_part = projected[:, 3 * C_ATOM:].astype(bf16)
    rimmed = jnp.pad(keyval, ((margin, margin), (0, 0)))
    keys_win = window_keys(rimmed, windows)
    tokens_win = window_keys(token_ext, windows)
    range_win = window_keys(in_range, windows)
    query_tokens = token_of.reshape(windows, Q_WIN)
    picked = bias_full[:, query_tokens[:, :, None], tokens_win[:, None, :]].transpose(1, 0, 2, 3).astype(f32)
    q_heads = queries.reshape(windows, Q_WIN, HEADS, head_dim).astype(f32)
    k_heads = keys_win[..., :C_ATOM].reshape(windows, K_WIN, HEADS, head_dim).astype(f32)
    v_heads = keys_win[..., C_ATOM:].reshape(windows, K_WIN, HEADS, head_dim).astype(f32)
    scores = jnp.einsum('wqhd,wkhd->whqk', q_heads, k_heads, precision=lax.Precision.HIGHEST) + picked
    scores = jnp.where(range_win[:, None, None, :], scores, -jnp.inf)
    row_max = lax.optimization_barrier(jnp.max(scores, -1, keepdims=True))
    exponent = jnp.exp(scores - row_max)
    weights = (exponent / lax.optimization_barrier(jnp.sum(exponent, -1, keepdims=True))).astype(bf16)
    attended = jnp.einsum('whqk,wkhd->wqhd', weights.astype(f32), v_heads, precision=lax.Precision.HIGHEST)
    gated = (attended.reshape(ATOMS, C_ATOM) * jax.nn.sigmoid(gate_part.astype(f32))).astype(bf16)
    residual = (atom_single.astype(f32) + jnp.dot(gated, w_out, preferred_element_type=f32)).astype(bf16)
    second = normalize(residual).astype(bf16)
    doubled = jnp.dot(second, w_trans_in, preferred_element_type=f32)
    hidden = (jax.nn.silu(doubled[:, :2 * C_ATOM]) * doubled[:, 2 * C_ATOM:]).astype(bf16)
    atom_out = (residual.astype(f32) + jnp.dot(hidden, w_trans_out, preferred_element_type=f32)).astype(bf16)
    emitted = jax.nn.relu(jnp.dot(atom_out, w_token, preferred_element_type=f32)).astype(bf16)
    sums = jax.ops.segment_sum(emitted.astype(f32), token_of, TOKENS)
    token_single = (sums / counts.reshape(-1)[:, None].astype(f32)).astype(bf16)
    row_term = jnp.dot(token_single, w_row, preferred_element_type=f32)
    col_term = jnp.dot(token_single, w_col, preferred_element_type=f32)

    def update(inputs_pair):
        pair_rows, row_terms = inputs_pair
        return (pair_rows.astype(f32) + row_terms[:, None, :] + col_term[None, :, :]).astype(bf16)
    new_pair = lax.map(update, (pair.reshape(N_ROW, TOK_ROW, TOKENS, C_PAIR), row_term.reshape(N_ROW, TOK_ROW, C_PAIR)))
    return (atom_out, token_single, new_pair.reshape(TOKENS, TOKENS, C_PAIR))
```

```python
import functools

import jax
import jax.numpy as jnp
from jax import lax
from jax.experimental import pallas as pl
from jax.experimental.pallas import tpu as pltpu
from jax.sharding import PartitionSpec as P

MESH = pl.DeviceIdType.MESH
F32 = jnp.float32
BF16 = jnp.bfloat16
N_ROW, N_COL = 16, 8
TOK = 128
CH = 128
HEADS = 4
WIN = 32
KEYS = 128
ATOMS = 1024
MARGIN = (KEYS - WIN) // 2
EXT = ATOMS + 2 * MARGIN
OWN = ATOMS // N_COL
STEP = 16
MASK_LANE = 56
SPLIT = 64


def nt(a, b):
    return lax.dot_general(a, b, (((1,), (1,)), ((), ())), preferred_element_type=F32)


def mm(a, b):
    return jnp.dot(a, b, preferred_element_type=F32)


def layer_norm(x):
    average = jnp.mean(x, -1, keepdims=True)
    centred = x - average
    spread = jnp.mean(centred * centred, -1, keepdims=True)
    return centred * lax.rsqrt(spread + 1e-05)


def iota(shape, axis):
    return lax.broadcasted_iota(jnp.int32, shape, axis)


def exchange_kernel(
    pair_hbm,
    atom_hbm,
    counts_hbm,
    wb_hbm,
    wp_hbm,
    wo_hbm,
    wi_hbm,
    wt_hbm,
    wk_hbm,
    wr_hbm,
    wc_hbm,
    atom_out,
    single_out,
    row_out,
    col_out,
    pair_buf,
    counts,
    wb,
    wp,
    wo,
    wi,
    wt,
    wk,
    wr,
    wc,
    stat,
    diag,
    side,
    side_in,
    atoms,
    lhs,
    rhs,
    vals,
    gate,
    gated,
    emitted,
    atom_res,
    single_buf,
    row_buf,
    col_buf,
    pair_sem,
    w_sem,
    local_sem,
    send_sem,
    recv_sem,
    side_sem,
):
    r, c = lax.axis_index("row"), lax.axis_index("col")
    odd = lax.rem(r, 2)
    home = r // 2
    is_main = c == home
    helper_col = home - 1 + 2 * odd
    has_helper = (helper_col >= 0) & (helper_col < N_COL)
    is_helper = c == helper_col
    has_prev, has_next = r > 0, r < N_ROW - 1
    side_start = pl.multiple_of((1 - odd) * TOK, TOK)
    own_start = pl.multiple_of(odd * TOK, TOK)

    def pair_copy(k):
        rows = pl.ds(k * STEP, STEP)
        return pltpu.make_async_copy(pair_hbm.at[rows], pair_buf.at[rows], pair_sem.at[k])

    def half_copy(k):
        rows = pl.ds(k * STEP, STEP)
        cols = pl.ds(side_start, TOK)
        return pltpu.make_async_copy(
            pair_hbm.at[rows, cols], pair_buf.at[rows, cols], pair_sem.at[k]
        )

    weights = [
        pltpu.make_async_copy(a, b, w_sem.at[i])
        for i, (a, b) in enumerate(
            [
                (wb_hbm, wb),
                (counts_hbm, counts),
                (wp_hbm, wp),
                (wo_hbm, wo),
                (wi_hbm, wi),
                (wt_hbm, wt),
                (wk_hbm, wk),
                (wr_hbm, wr),
                (wc_hbm, wc),
            ]
        )
    ]
    steps = TOK // STEP

    @pl.when(is_main)
    def _():
        weights[0].start()
        for k in range(steps):
            pair_copy(k).start()
        for w in weights[1:]:
            w.start()

    @pl.when(is_helper)
    def _():
        weights[0].start()
        for k in range(steps):
            half_copy(k).start()

    barrier = pltpu.get_barrier_semaphore()

    def hello(row, col):
        pl.semaphore_signal(barrier, inc=1, device_id=(row, col), device_id_type=MESH)

    @pl.when(is_main)
    def _():
        for p in range(1, N_COL):
            hello(r, lax.rem(c + p, N_COL))
        for p in range(1, N_ROW):
            hello(lax.rem(r + p, N_ROW), c)

        @pl.when(has_prev)
        def _():
            hello(r - 1, N_COL - 1)

        @pl.when(has_next)
        def _():
            hello(r + 1, 0)

    @pl.when(jnp.logical_not(is_main))
    def _():
        hello(r, home)

    @pl.when(r != 2 * c)
    def _():
        hello(2 * c, c)

    @pl.when(r != 2 * c + 1)
    def _():
        hello(2 * c + 1, c)

    to_next = (c == N_COL - 1) & has_next
    to_prev = (c == 0) & has_prev

    @pl.when(to_next)
    def _():
        hello(r + 1, (r + 1) // 2)

    @pl.when(to_prev)
    def _():
        hello(r - 1, (r - 1) // 2)

    one = lambda flag: jnp.where(flag, 1, 0)
    greetings = (
        one(is_main) * (N_COL - 1 + N_ROW - 1 + one(has_prev) + one(has_next))
        + one(jnp.logical_not(is_main))
        + one(r != 2 * c)
        + one(r != 2 * c + 1)
        + one(to_next)
        + one(to_prev)
    )
    pl.semaphore_wait(barrier, greetings)

    def atom_copy(col):
        return pltpu.make_async_remote_copy(
            src_ref=atom_hbm,
            dst_ref=atoms.at[pl.ds(MARGIN + col * OWN, OWN)],
            send_sem=send_sem.at[0],
            recv_sem=recv_sem.at[col],
            device_id=(r, home),
            device_id_type=MESH,
        )

    def edge_copy(forward, row):
        start = OWN - MARGIN if forward else 0
        return pltpu.make_async_remote_copy(
            src_ref=atom_hbm.at[pl.ds(start, MARGIN)],
            dst_ref=atoms.at[pl.ds(0 if forward else MARGIN + ATOMS, MARGIN)],
            send_sem=send_sem.at[1 if forward else 2],
            recv_sem=recv_sem.at[N_COL + (0 if forward else 1)],
            device_id=(row, row // 2),
            device_id_type=MESH,
        )

    def side_copy():
        return pltpu.make_async_remote_copy(
            src_ref=side,
            dst_ref=side_in,
            send_sem=send_sem.at[3],
            recv_sem=side_sem,
            device_id=(r, home),
            device_id_type=MESH,
        )

    @pl.when(jnp.logical_not(is_main))
    def _():
        atom_copy(c).start()

    @pl.when(to_next)
    def _():
        edge_copy(True, r + 1).start()

    @pl.when(to_prev)
    def _():
        edge_copy(False, r - 1).start()

    own_atoms = pltpu.make_async_copy(
        atom_hbm, atoms.at[pl.ds(MARGIN + c * OWN, OWN)], local_sem.at[0]
    )

    @pl.when(is_main)
    def _():
        own_atoms.start()

    lane = iota((8, TOK), 1)
    sub = iota((8, TOK), 0)
    block_of = lane // 8
    on_diag = lax.rem(lane, 8) == sub

    def bias_weights():
        w = wb[...]
        w = w - jnp.mean(w, -1, keepdims=True)
        high = w.astype(BF16)
        rest = w - high.astype(F32)
        mid = rest.astype(BF16)
        low = (rest - mid.astype(F32)).astype(BF16)
        ones = jnp.ones((1, CH), BF16)
        zeros = jnp.zeros((4, CH), BF16)
        return jnp.concatenate(
            [high, ones, zeros[:3], mid, zeros, low, zeros], axis=0
        )

    def moments(i, start, seg, w24):
        x = pair_buf[i, pl.ds(start, TOK), :]
        t = nt(w24, x)
        gram = nt(x, x)
        d = jnp.zeros((8, TOK), F32)
        for k in range(TOK // 8):
            d = jnp.where(block_of == k, gram[8 * k : 8 * k + 8], d)
        rows = pl.ds(pl.multiple_of(i * 8, 8), 8)
        stat[seg, rows, :] = t[0:8] + t[8:16] + t[16:24]
        diag[seg, rows, :] = jnp.where(on_diag, d, 0.0)

    def head_bias(seg):
        def part(ref, s):
            return ref[seg, pl.ds(s, TOK, stride=8), :]

        s1 = part(stat, 4)
        s2 = part(diag, 0)
        for s in range(1, 8):
            s2 = s2 + part(diag, s)
        near = (s1 * (1 / CH)).astype(BF16).astype(F32)
        offset = s1 * (1 / CH) - near
        moment = (s2 - 2 * near * s1) + CH * (near * near)
        spread = jnp.maximum(moment * (1 / CH) - offset * offset, 0.0)
        scale = lax.rsqrt(spread + 1e-05)
        return [(part(stat, h) * scale).astype(BF16) for h in range(HEADS)]

    @pl.when(is_helper)
    def _():
        weights[0].wait()
        w24 = bias_weights()

        @pl.loop(0, steps)
        def _(k):
            half_copy(k).wait()

            @pl.loop(0, STEP, unroll=8)
            def _(u):
                moments(k * STEP + u, side_start, 1, w24)

        for h, value in enumerate(head_bias(1)):
            side[h] = value
        side_copy().start()
        side_copy().wait_send()

    @pl.when(is_main)
    def _():
        weights[0].wait()
        w24 = bias_weights()

        @pl.loop(0, steps)
        def _(k):
            pair_copy(k).wait()

            @pl.loop(0, STEP, unroll=4)
            def _(u):
                moments(k * STEP + u, own_start, 0, w24)
                moments(k * STEP + u, side_start, 1, w24)

        for w in weights[1:]:
            w.wait()

        own_counts = counts[pl.ds(r, 1), :].astype(F32)
        prev_counts = counts[pl.ds(jnp.maximum(r - 1, 0), 1), :].astype(F32)
        next_counts = counts[pl.ds(jnp.minimum(r + 1, N_ROW - 1), 1), :].astype(F32)
        stacked = jnp.concatenate(
            [own_counts, prev_counts, next_counts, jnp.zeros((5, TOK), F32)], axis=0
        )
        upper = (iota((TOK, TOK), 0) <= iota((TOK, TOK), 1)).astype(F32).astype(BF16)
        lower = (iota((TOK, TOK), 0) >= iota((TOK, TOK), 1)).astype(F32).astype(BF16)
        stacked_low = stacked.astype(BF16)
        ends = mm(stacked_low, upper)
        starts = ends - stacked
        ends_column = nt(lower, stacked_low)[:, 0:1]
        eye = (iota((TOK, TOK), 0) == iota((TOK, TOK), 1)).astype(F32).astype(BF16)
        counts_column = nt(eye, stacked_low)[:, 0:1]
        starts_column = ends_column - counts_column
        far = 1e9
        one_lane = iota((1, TOK), 1)
        after = one_lane < SPLIT
        side_from = jnp.where(
            after,
            jnp.where(has_next, starts[2:3] + ATOMS, far),
            jnp.where(has_prev, starts[1:2] - ATOMS, far),
        )
        side_to = jnp.where(
            after,
            jnp.where(has_next, ends[2:3] + ATOMS, far),
            jnp.where(has_prev, ends[1:2] - ATOMS, far),
        )
        masked = one_lane == MASK_LANE
        low_mask = jnp.where(has_prev, far, -float(MARGIN))
        mask_from = jnp.where(has_next, low_mask, float(ATOMS))
        mask_to = jnp.where(
            has_next, jnp.where(has_prev, far, 0.0), float(ATOMS + MARGIN)
        )
        side_from = jnp.where(masked, mask_from, side_from)
        side_to = jnp.where(masked, mask_to, side_to)

        def onehot(first, count, lo, hi):
            at = (iota((count, TOK), 0) + first).astype(F32)
            return jnp.where((at >= lo) & (at < hi), 1.0, 0.0).astype(BF16)

        rhs[:, CH : CH + TOK] = onehot(-MARGIN, EXT, starts[0:1], ends[0:1])
        rhs[:, CH + TOK :] = onehot(-MARGIN, EXT, side_from, side_to)
        vals[:, CH:] = jnp.ones((EXT, CH), BF16)

        own_atoms.wait()
        for p in range(1, N_COL):
            atom_copy(lax.rem(c + p, N_COL)).wait_recv()

        @pl.when(has_prev)
        def _():
            edge_copy(True, r).wait_recv()

        @pl.when(jnp.logical_not(has_prev))
        def _():
            atoms[0:MARGIN, :] = jnp.zeros((MARGIN, CH), BF16)

        @pl.when(has_next)
        def _():
            edge_copy(False, r).wait_recv()

        @pl.when(jnp.logical_not(has_next))
        def _():
            atoms[MARGIN + ATOMS :, :] = jnp.zeros((MARGIN, CH), BF16)

        head_of = iota((WIN, CH), 1) // (CH // HEADS)
        pieces = [(0, MARGIN, False)]
        pieces += [(MARGIN + 256 * k, 256, True) for k in range(ATOMS // 256)]
        pieces += [(MARGIN + ATOMS, MARGIN, False)]
        for start, count, inside in pieces:
            span = slice(start, start + count)
            norm = layer_norm(atoms[span, :].astype(F32)).astype(BF16)
            projected = mm(norm, wp[...])
            rhs[span, 0:CH] = projected[:, CH : 2 * CH].astype(BF16)
            vals[span, 0:CH] = projected[:, 2 * CH : 3 * CH].astype(BF16)
            if inside:
                first = start - MARGIN
                gate[first : first + count, :] = projected[:, 3 * CH :]
                queries = projected[:, 0:CH] * (CH // HEADS) ** -0.5
                for w in range(count // WIN):
                    window = queries[w * WIN : (w + 1) * WIN]
                    base = (first + w * WIN) * HEADS
                    for h in range(HEADS):
                        lhs[base + h * WIN : base + (h + 1) * WIN, 0:CH] = jnp.where(
                            head_of == h, window, 0.0
                        ).astype(BF16)

        own_bias = head_bias(0)
        main_side = head_bias(1)

        @pl.when(has_helper)
        def _():
            side_copy().wait_recv()

        @pl.when(jnp.logical_not(has_helper))
        def _():
            side_in[...] = jnp.zeros((HEADS, TOK, TOK), BF16)

        side_lane = iota((TOK, TOK), 1)
        mine = (side_lane < SPLIT) == (odd == 0)
        for h in range(HEADS):
            joined = jnp.where(
                mine, main_side[h].astype(F32), side_in[h].astype(F32)
            )
            joined = jnp.where(side_lane == MASK_LANE, -1e30, joined).astype(BF16)
            both = jnp.concatenate([own_bias[h], joined], axis=1)
            for k in range(ATOMS // 256):
                first = k * 256
                picked = mm(
                    rhs[MARGIN + first : MARGIN + first + 256, CH : CH + TOK], both
                ).astype(BF16)
                for w in range(256 // WIN):
                    base = (first + w * WIN) * HEADS + h * WIN
                    lhs[base : base + WIN, CH:] = picked[w * WIN : (w + 1) * WIN]

        @pl.loop(0, ATOMS // WIN, unroll=4)
        def _(w):
            keys = pl.ds(pl.multiple_of(w * WIN, WIN), KEYS)
            rows = pl.ds(pl.multiple_of(w * WIN * HEADS, WIN * HEADS), WIN * HEADS)
            scores = nt(lhs[rows, :], rhs[keys, :])
            top = jnp.max(scores, -1, keepdims=True)
            weight = jnp.exp(scores - top).astype(BF16)
            total = mm(weight, vals[keys, :])
            above = total[0:WIN, 0:CH]
            below = total[0:WIN, CH:]
            for h in range(1, HEADS):
                here = head_of == h
                above = jnp.where(here, total[h * WIN : (h + 1) * WIN, 0:CH], above)
                below = jnp.where(here, total[h * WIN : (h + 1) * WIN, CH:], below)
            span = pl.ds(pl.multiple_of(w * WIN, WIN), WIN)
            opened = 1.0 + jnp.exp(-gate[span, :])
            gated[span, :] = (above / (below * opened)).astype(BF16)

        for k in range(ATOMS // 256):
            span = slice(k * 256, (k + 1) * 256)
            ext = slice(MARGIN + k * 256, MARGIN + (k + 1) * 256)
            residual = (atoms[ext, :].astype(F32) + mm(gated[span, :], wo[...])).astype(BF16)
            residual = residual.astype(F32)
            second = layer_norm(residual).astype(BF16)
            doubled = mm(second, wi[...])
            swish = doubled[:, 0 : 2 * CH]
            hidden = (swish / (1.0 + jnp.exp(-swish)) * doubled[:, 2 * CH :]).astype(BF16)
            out = (residual + mm(hidden, wt[...])).astype(BF16)
            atom_res[span, :] = out
            emitted[span, :] = jnp.maximum(mm(out, wk[...]), 0.0).astype(BF16)

        at = iota((TOK, ATOMS), 1).astype(F32)
        member = jnp.where((at >= starts_column) & (at < ends_column), 1.0, 0.0)
        totals = mm(member.astype(BF16), emitted[...])
        single = (totals / counts_column).astype(BF16)
        single_buf[...] = single
        row_buf[...] = mm(single, wr[...]).astype(BF16)
        col_buf[...] = mm(single, wc[...]).astype(BF16)

    def send(src, dst, slot, recv, row, col):
        return pltpu.make_async_remote_copy(
            src_ref=src,
            dst_ref=dst,
            send_sem=send_sem.at[slot],
            recv_sem=recv_sem.at[recv],
            device_id=(row, col),
            device_id_type=MESH,
        )

    base = N_COL + 2

    def row_send(p):
        return send(row_buf, row_out, 4 + p, base, r, lax.rem(c + p, N_COL))

    def single_send(p):
        return send(
            single_buf, single_out, 4 + N_COL + p, base + 1, r, lax.rem(c + p, N_COL)
        )

    def atom_send(p):
        col = lax.rem(c + p, N_COL)
        return send(
            atom_res.at[pl.ds(col * OWN, OWN)],
            atom_out,
            4 + 2 * N_COL + p,
            base + 2,
            r,
            col,
        )

    def col_send(p, parity):
        return send(
            col_buf,
            col_out.at[pl.ds(parity * TOK, TOK)],
            4 + 3 * N_COL + p,
            base + 3 + parity,
            lax.rem(r + p, N_ROW),
            c,
        )

    @pl.when(is_main)
    def _():
        for p in range(1, N_ROW):
            col_send(p, odd).start()
        for p in range(1, N_COL):
            row_send(p).start()
        for p in range(1, N_COL):
            atom_send(p).start()
        for p in range(1, N_COL):
            single_send(p).start()
        locals_ = [
            pltpu.make_async_copy(row_buf, row_out, local_sem.at[1]),
            pltpu.make_async_copy(single_buf, single_out, local_sem.at[2]),
            pltpu.make_async_copy(
                atom_res.at[pl.ds(c * OWN, OWN)], atom_out, local_sem.at[3]
            ),
            pltpu.make_async_copy(
                col_buf, col_out.at[pl.ds(odd * TOK, TOK)], local_sem.at[4]
            ),
        ]
        for copy in locals_:
            copy.start()
        for copy in locals_:
            copy.wait()
        for p in range(1, N_ROW):
            col_send(p, odd).wait_send()
        for p in range(1, N_COL):
            row_send(p).wait_send()
            atom_send(p).wait_send()
            single_send(p).wait_send()

    @pl.when(jnp.logical_not(is_main))
    def _():
        atom_copy(c).wait_send()
        row_send(1).wait_recv()
        atom_send(1).wait_recv()
        single_send(1).wait_recv()

    @pl.when(to_next)
    def _():
        edge_copy(True, r + 1).wait_send()

    @pl.when(to_prev)
    def _():
        edge_copy(False, r - 1).wait_send()

    @pl.when(r != 2 * c)
    def _():
        col_send(1, 0).wait_recv()

    @pl.when(r != 2 * c + 1)
    def _():
        col_send(1, 1).wait_recv()


def update_kernel(pair, row, col, atom, single, new_pair, atom_out, single_out):
    @pl.when(pl.program_id(0) == 0)
    def _():
        atom_out[...] = atom[...]
        single_out[...] = single[...]

    rows = pair.shape[0]
    column = col[...].astype(F32)
    for i in range(rows):
        term = row[i : i + 1, :].astype(F32)
        new_pair[i] = (pair[i].astype(F32) + (column + term)).astype(BF16)


def shards(
    pair, counts, atom_single, w_bias, w_project, w_out, w_trans_in, w_trans_out, w_token, w_row, w_col
):
    any_ = pl.BlockSpec(memory_space=pl.ANY)
    vmem = pltpu.VMEM
    weights = (w_bias.T, w_project, w_out, w_trans_in, w_trans_out, w_token, w_row, w_col)
    atom, single, row, col = pl.pallas_call(
        exchange_kernel,
        out_shape=(
            jax.ShapeDtypeStruct((OWN, CH), BF16),
            jax.ShapeDtypeStruct((TOK, 3 * CH), BF16),
            jax.ShapeDtypeStruct((TOK, CH), BF16),
            jax.ShapeDtypeStruct((2 * TOK, CH), BF16),
        ),
        in_specs=[any_] * (3 + len(weights)),
        out_specs=(any_,) * 4,
        scratch_shapes=[
            vmem((TOK, 2 * TOK, CH), BF16),
            vmem(counts.shape, jnp.int32),
            *[vmem(w.shape, w.dtype) for w in weights],
            vmem((2, 8 * TOK, TOK), F32),
            vmem((2, 8 * TOK, TOK), F32),
            vmem((HEADS, TOK, TOK), BF16),
            vmem((HEADS, TOK, TOK), BF16),
            vmem((EXT, CH), BF16),
            vmem((ATOMS * HEADS, CH + 2 * TOK), BF16),
            vmem((EXT, CH + 2 * TOK), BF16),
            vmem((EXT, 2 * CH), BF16),
            vmem((ATOMS, CH), F32),
            vmem((ATOMS, CH), BF16),
            vmem((ATOMS, 3 * CH), BF16),
            vmem((ATOMS, CH), BF16),
            vmem((TOK, 3 * CH), BF16),
            vmem((TOK, CH), BF16),
            vmem((TOK, CH), BF16),
            pltpu.SemaphoreType.DMA((TOK // STEP,)),
            pltpu.SemaphoreType.DMA((1 + len(weights),)),
            pltpu.SemaphoreType.DMA((5,)),
            pltpu.SemaphoreType.DMA((4 + 3 * N_COL + N_ROW,)),
            pltpu.SemaphoreType.DMA((N_COL + 7,)),
            pltpu.SemaphoreType.DMA,
        ],
        compiler_params=pltpu.CompilerParams(
            collective_id=0, has_side_effects=True, vmem_limit_bytes=40 * 2**20
        ),
    )(pair, atom_single, counts, *weights)
    rows = 16
    whole = lambda a: pl.BlockSpec(a.shape, lambda i: (0,) * a.ndim)
    block = pl.BlockSpec((rows,) + pair.shape[1:], lambda i: (i, 0, 0))
    new_pair, atom_out, token_single = pl.pallas_call(
        update_kernel,
        grid=(pair.shape[0] // rows,),
        out_shape=(
            jax.ShapeDtypeStruct(pair.shape, BF16),
            jax.ShapeDtypeStruct(atom.shape, BF16),
            jax.ShapeDtypeStruct(single.shape, BF16),
        ),
        in_specs=[
            block,
            pl.BlockSpec((rows, CH), lambda i: (i, 0)),
            whole(col),
            whole(atom),
            whole(single),
        ],
        out_specs=(block, whole(atom), whole(single)),
        compiler_params=pltpu.CompilerParams(vmem_limit_bytes=16 * 2**20),
    )(pair, row, col, atom, single)
    return atom_out, token_single, new_pair


def solution(mesh):
    return jax.shard_map(
        shards,
        mesh=mesh,
        in_specs=(P("row", "col", None), P(), P(("row", "col"), None)) + (P(),) * 8,
        out_specs=(P(("row", "col"), None), P("row", None), P("row", "col", None)),
        check_vma=False,
    )
```

```python
import functools

import jax
import jax.numpy as jnp
from jax import lax
from jax.experimental import pallas as pl
from jax.experimental.pallas import tpu as pltpu
from jax.sharding import PartitionSpec as P

MESH = pl.DeviceIdType.MESH
F32 = jnp.float32
BF16 = jnp.bfloat16
N_ROW, N_COL = 16, 8
TOK = 128
CH = 128
HEADS = 4
WIN = 32
KEYS = 128
ATOMS = 1024
MARGIN = (KEYS - WIN) // 2
EXT = ATOMS + 2 * MARGIN
OWN = ATOMS // N_COL
STEP = 16
REACH = 80
HALF = REACH // 2
EDGES = (0, 1, 30, 31)
MASK_LANE = 56
ATTEND_UNROLL = 14
SPLIT = 64


def nt(a, b):
    return lax.dot_general(a, b, (((1,), (1,)), ((), ())), preferred_element_type=F32)


def mm(a, b):
    return jnp.dot(a, b, preferred_element_type=F32)


def layer_norm(x):
    average = jnp.mean(x, -1, keepdims=True)
    centred = x - average
    spread = jnp.mean(centred * centred, -1, keepdims=True)
    return centred * lax.rsqrt(spread + 1e-05)


def iota(shape, axis):
    return lax.broadcasted_iota(jnp.int32, shape, axis)


def exchange_kernel(
    pair_hbm,
    atom_hbm,
    counts_hbm,
    wb_hbm,
    wp_hbm,
    wo_hbm,
    wi_hbm,
    wt_hbm,
    wk_hbm,
    wr_hbm,
    wc_hbm,
    atom_out,
    single_out,
    row_out,
    col_out,
    own_pair,
    side_pair,
    counts,
    wb,
    wp,
    wo,
    wi,
    wt,
    wk,
    wr,
    wc,
    stat,
    diag,
    side,
    side_in,
    atoms,
    queries,
    picked,
    picked_side,
    rhs,
    vals,
    gate,
    gated,
    resid,
    resid_in,
    emitted,
    member,
    own_sem,
    side_pair_sem,
    w_sem,
    local_sem,
    send_sem,
    recv_sem,
):
    r, c = lax.axis_index("row"), lax.axis_index("col")
    odd = lax.rem(r, 2)
    home = r // 2
    is_main = c == home
    not_main = jnp.logical_not(is_main)
    helper_col = home - 1 + 2 * odd
    has_helper = (helper_col >= 0) & (helper_col < N_COL)
    is_helper = c == helper_col
    has_prev, has_next = r > 0, r < N_ROW - 1
    z, x_hi = c // 2, lax.rem(c, 2)
    y, x_lo = r // 4, lax.rem(r // 2, 2)
    sibling = r + 1 - 2 * odd
    col_main = 2 * c + odd
    fed_by_main = r != col_main
    row_peers = [
        (lax.rem(z + dz, 4) * 2 + (1 - x_hi if dx else x_hi))
        for dz, dx in ((2, 1), (1, 1), (3, 1), (2, 0), (0, 1), (1, 0), (3, 0))
    ]
    col_peers = [
        (lax.rem(y + dy, 4) * 2 + (1 - x_lo if dx else x_lo)) * 2 + odd
        for dy, dx in ((2, 1), (1, 1), (3, 1), (2, 0), (1, 0), (3, 0), (0, 1))
    ]
    own_start = pl.multiple_of(odd * TOK, TOK)
    on_main_next = odd == 0
    side_is_next = on_main_next == is_main
    side_rows = jnp.where(side_is_next, TOK - REACH, 0)
    side_start = pl.multiple_of((1 - odd) * TOK + jnp.where(side_is_next, 0, SPLIT), SPLIT)

    def own_copy(k):
        rows = pl.ds(k * STEP, STEP)
        return pltpu.make_async_copy(
            pair_hbm.at[rows, pl.ds(own_start, TOK)], own_pair.at[rows], own_sem.at[k]
        )

    def side_pair_copy(k):
        return pltpu.make_async_copy(
            pair_hbm.at[pl.ds(side_rows + k * HALF, HALF), pl.ds(side_start, SPLIT)],
            side_pair.at[:, pl.ds(k * SPLIT, SPLIT)],
            side_pair_sem.at[k],
        )

    weights = [
        pltpu.make_async_copy(a, b, w_sem.at[i])
        for i, (a, b) in enumerate(
            [
                (wb_hbm, wb),
                (counts_hbm, counts),
                (wp_hbm, wp),
                (wo_hbm, wo),
                (wi_hbm, wi),
                (wt_hbm, wt),
                (wk_hbm, wk),
                (wr_hbm, wr),
                (wc_hbm, wc),
            ]
        )
    ]
    receiver_weights = [weights[4], weights[5], weights[7]]
    steps = TOK // STEP

    barrier = pltpu.get_barrier_semaphore()

    def hello(row, col):
        pl.semaphore_signal(barrier, inc=1, device_id=(row, col), device_id_type=MESH)

    to_next = (c == N_COL - 1) & has_next
    to_prev = (c == 0) & has_prev

    @pl.when(is_main)
    def _():
        for col in row_peers:
            hello(r, col)

        @pl.when(has_prev)
        def _():
            hello(r - 1, N_COL - 1)

        @pl.when(has_next)
        def _():
            hello(r + 1, 0)

        for row in col_peers:
            hello(row, c)

    @pl.when(not_main)
    def _():
        hello(r, home)

    @pl.when(fed_by_main)
    def _():
        hello(col_main, c)

    hello(sibling, c)

    @pl.when(to_next)
    def _():
        hello(r + 1, (r + 1) // 2)

    @pl.when(to_prev)
    def _():
        hello(r - 1, (r - 1) // 2)

    def one(flag):
        return jnp.where(flag, 1, 0)

    greetings = (
        1
        + one(is_main) * (2 * 7 + one(has_prev) + one(has_next))
        + one(not_main)
        + one(fed_by_main)
        + one(to_next)
        + one(to_prev)
    )

    @pl.when(is_main)
    def _():
        weights[1].start()
        weights[0].start()
        for k in range(2):
            side_pair_copy(k).start()
        for k in range(steps):
            own_copy(k).start()
        for w in weights[2:]:
            w.start()

    @pl.when(not_main)
    def _():
        @pl.when(is_helper)
        def _():
            weights[0].start()
            for k in range(2):
                side_pair_copy(k).start()

        for w in receiver_weights:
            w.start()

    def atom_copy(col):
        return pltpu.make_async_remote_copy(
            src_ref=atom_hbm,
            dst_ref=atoms.at[pl.ds(MARGIN + col * OWN, OWN)],
            send_sem=send_sem.at[0],
            recv_sem=recv_sem.at[col],
            device_id=(r, home),
            device_id_type=MESH,
        )

    def edge_copy(forward, row):
        start = OWN - MARGIN if forward else 0
        return pltpu.make_async_remote_copy(
            src_ref=atom_hbm.at[pl.ds(start, MARGIN)],
            dst_ref=atoms.at[pl.ds(0 if forward else MARGIN + ATOMS, MARGIN)],
            send_sem=send_sem.at[1 if forward else 2],
            recv_sem=recv_sem.at[N_COL + (0 if forward else 1)],
            device_id=(row, row // 2),
            device_id_type=MESH,
        )

    def side_copy():
        return pltpu.make_async_remote_copy(
            src_ref=side,
            dst_ref=side_in,
            send_sem=send_sem.at[3],
            recv_sem=recv_sem.at[N_COL + 2],
            device_id=(r, home),
            device_id_type=MESH,
        )

    own_atoms = pltpu.make_async_copy(
        atom_hbm, atoms.at[pl.ds(MARGIN + c * OWN, OWN)], local_sem.at[0]
    )

    @pl.when(is_main)
    def _():
        own_atoms.start()

    @pl.when(not_main)
    def _():
        pl.semaphore_wait(barrier, greetings)
        atom_copy(c).start()

    @pl.when(to_next & not_main)
    def _():
        edge_copy(True, r + 1).start()

    @pl.when(to_prev & not_main)
    def _():
        edge_copy(False, r - 1).start()

    lane = iota((8, TOK), 1)
    sub = iota((8, TOK), 0)
    block_of = lane // 8
    on_diag = lax.rem(lane, 8) == sub

    def bias_weights():
        w = wb[...]
        w = w - jnp.mean(w, -1, keepdims=True)
        high = w.astype(BF16)
        rest = w - high.astype(F32)
        mid = rest.astype(BF16)
        low = (rest - mid.astype(F32)).astype(BF16)
        ones = jnp.ones((1, CH), BF16)
        zeros = jnp.zeros((12, CH), BF16)
        return jnp.concatenate(
            [high, ones, zeros[:3], mid, zeros[:4], low, zeros], axis=0
        )

    def moments(x, i, first, w32):
        t = nt(jnp.concatenate([w32, x], axis=0), x)
        d = jnp.zeros((8, TOK), F32)
        for k in range(TOK // 8):
            d = jnp.where(block_of == k, t[32 + 8 * k : 40 + 8 * k], d)
        rows = pl.ds(pl.multiple_of(first + i * 8, 8), 8)
        stat[rows, :] = t[0:8] + t[8:16] + t[16:24]
        diag[rows, :] = jnp.where(on_diag, d, 0.0)

    def side_moments(w32):
        for k in range(2):
            side_pair_copy(k).wait()

        @pl.loop(0, HALF, unroll=8)
        def _(i):
            moments(side_pair[i], i, 8 * TOK, w32)

    def head_bias(first, count):
        def part(ref, s):
            return ref[pl.ds(first + s, count, stride=8), :]

        s1 = part(stat, 4)
        s2 = part(diag, 0)
        for s in range(1, 8):
            s2 = s2 + part(diag, s)
        near = (s1 * (1 / CH)).astype(BF16).astype(F32)
        offset = s1 * (1 / CH) - near
        moment = (s2 - 2 * near * s1) + CH * (near * near)
        spread = jnp.maximum(moment * (1 / CH) - offset * offset, 0.0)
        scale = lax.rsqrt(spread + 1e-05)
        return [part(stat, h) * scale for h in range(HEADS)]

    def transition(x):
        residual = x.astype(F32)
        second = layer_norm(residual).astype(BF16)
        doubled = mm(second, wi[...])
        swish = doubled[:, 0 : 2 * CH]
        hidden = swish * (0.5 + 0.5 * jnp.tanh(0.5 * swish)) * doubled[:, 2 * CH :]
        return (residual + mm(hidden.astype(BF16), wt[...])).astype(BF16)

    @pl.when(is_helper)
    def _():
        weights[0].wait()
        side_moments(bias_weights())
        for h, value in enumerate(head_bias(8 * TOK, HALF)):
            side[h] = value
        side_copy().start()
        side_copy().wait_send()

    def send(src, dst, slot, recv, row, col):
        return pltpu.make_async_remote_copy(
            src_ref=src,
            dst_ref=dst,
            send_sem=send_sem.at[slot],
            recv_sem=recv_sem.at[recv],
            device_id=(row, col),
            device_id_type=MESH,
        )

    base = N_COL + 3

    def resid_send(p):
        col = row_peers[p]
        return send(resid.at[pl.ds(col * OWN, OWN)], resid_in, 4 + p, base, r, col)

    def single_send(p):
        return send(single_out, single_out, 12 + p, base + 1, r, row_peers[p])

    own_half = col_out.at[pl.ds(pl.multiple_of(odd * TOK, TOK), TOK)]

    def col_send(p):
        return send(own_half, own_half, 20 + p, base + 2, col_peers[p], c)

    def col_forward():
        return send(own_half, own_half, 28, base + 3, sibling, c)

    @pl.when(is_main)
    def _():
        weights[1].wait()
        own_counts = counts[pl.ds(r, 1), :].astype(F32)
        prev_counts = counts[pl.ds(jnp.maximum(r - 1, 0), 1), :].astype(F32)
        next_counts = counts[pl.ds(jnp.minimum(r + 1, N_ROW - 1), 1), :].astype(F32)
        stacked = jnp.concatenate(
            [own_counts, prev_counts, next_counts, jnp.zeros((5, TOK), F32)], axis=0
        )
        upper = (iota((TOK, TOK), 0) <= iota((TOK, TOK), 1)).astype(F32).astype(BF16)
        lower = (iota((TOK, TOK), 0) >= iota((TOK, TOK), 1)).astype(F32).astype(BF16)
        stacked_low = stacked.astype(BF16)
        ends = mm(stacked_low, upper)
        starts = ends - stacked
        ends_column = nt(lower, stacked_low)[:, 0:1]
        eye = (iota((TOK, TOK), 0) == iota((TOK, TOK), 1)).astype(F32).astype(BF16)
        counts_column = nt(eye, stacked_low)[:, 0:1]
        starts_column = ends_column - counts_column
        far = 1e9
        one_lane = iota((1, TOK), 1)
        after = one_lane < SPLIT
        side_from = jnp.where(
            after,
            jnp.where(has_next, starts[2:3] + ATOMS, far),
            jnp.where(has_prev, starts[1:2] - ATOMS, far),
        )
        side_to = jnp.where(
            after,
            jnp.where(has_next, ends[2:3] + ATOMS, far),
            jnp.where(has_prev, ends[1:2] - ATOMS, far),
        )
        masked = one_lane == MASK_LANE
        low_mask = jnp.where(has_prev, far, -float(MARGIN))
        mask_from = jnp.where(has_next, low_mask, float(ATOMS))
        mask_to = jnp.where(
            has_next, jnp.where(has_prev, far, 0.0), float(ATOMS + MARGIN)
        )
        side_from = jnp.where(masked, mask_from, side_from)
        side_to = jnp.where(masked, mask_to, side_to)

        def onehot(first, count, lo, hi):
            at = (iota((count, TOK), 0) + first).astype(F32)
            return jnp.where((at >= lo) & (at < hi), 1.0, 0.0).astype(BF16)

        rhs[:, CH : CH + TOK] = onehot(-MARGIN, EXT, starts[0:1], ends[0:1])
        for first in (0, ATOMS - 2 * MARGIN + WIN):
            rhs[first : first + KEYS + WIN, CH + TOK :] = onehot(
                first - MARGIN, KEYS + WIN, side_from, side_to
            )
        vals[:, CH:] = jnp.ones((EXT, CH), BF16)
        at = iota((TOK, ATOMS), 1).astype(F32)
        member[...] = jnp.where(
            (at >= starts_column) & (at < ends_column), 1.0, 0.0
        ).astype(BF16)

        weights[0].wait()
        w32 = bias_weights()
        side_moments(w32)

        @pl.loop(0, steps)
        def _(k):
            own_copy(k).wait()

            @pl.loop(0, STEP, unroll=8)
            def _(u):
                i = k * STEP + u
                moments(own_pair[i], i, 0, w32)

        for w in weights[2:]:
            w.wait()
        pl.semaphore_wait(barrier, greetings)

        @pl.when(to_next)
        def _():
            edge_copy(True, r + 1).start()

        @pl.when(to_prev)
        def _():
            edge_copy(False, r - 1).start()

        own_bias = [value.astype(BF16) for value in head_bias(0, TOK)]
        main_side = head_bias(8 * TOK, HALF)
        for h in range(HEADS):
            for k in range(ATOMS // 256):
                first = k * 256
                rows = mm(
                    rhs[MARGIN + first : MARGIN + first + 256, CH : CH + TOK], own_bias[h]
                ).astype(BF16)
                for w in range(256 // WIN):
                    start = (first + w * WIN) * HEADS + h * WIN
                    picked[start : start + WIN, :] = rows[w * WIN : (w + 1) * WIN]

        own_atoms.wait()
        for col in reversed(row_peers):
            atom_copy(col).wait_recv()

        @pl.when(has_prev)
        def _():
            edge_copy(True, r).wait_recv()

        @pl.when(jnp.logical_not(has_prev))
        def _():
            atoms[0:MARGIN, :] = jnp.zeros((MARGIN, CH), BF16)

        @pl.when(has_next)
        def _():
            edge_copy(False, r).wait_recv()

        @pl.when(jnp.logical_not(has_next))
        def _():
            atoms[MARGIN + ATOMS :, :] = jnp.zeros((MARGIN, CH), BF16)

        pieces = [(0, MARGIN, False)]
        pieces += [(MARGIN + 256 * k, 256, True) for k in range(ATOMS // 256)]
        pieces += [(MARGIN + ATOMS, MARGIN, False)]
        for start, count, inside in pieces:
            span = slice(start, start + count)
            norm = layer_norm(atoms[span, :].astype(F32)).astype(BF16)
            projected = mm(norm, wp[...])
            rhs[span, 0:CH] = projected[:, CH : 2 * CH].astype(BF16)
            vals[span, 0:CH] = projected[:, 2 * CH : 3 * CH].astype(BF16)
            if inside:
                first = slice(start - MARGIN, start - MARGIN + count)
                gate[first, :] = 0.5 + 0.5 * jnp.tanh(0.5 * projected[:, 3 * CH :])
                queries[first, :] = (projected[:, 0:CH] * (CH // HEADS) ** -0.5).astype(BF16)

        @pl.when(has_helper)
        def _():
            side_copy().wait_recv()

        @pl.when(jnp.logical_not(has_helper))
        def _():
            side_in[...] = jnp.zeros(side_in.shape, F32)

        low_lanes = iota((HALF, TOK), 1) < SPLIT
        mask_lane = iota((TOK, TOK), 1) == MASK_LANE
        for h in range(HEADS):
            theirs = side_in[h]
            ahead = jnp.where(on_main_next, main_side[h], theirs)
            behind = jnp.where(on_main_next, theirs, main_side[h])
            ahead_rolled = pltpu.roll(ahead, SPLIT, 1)
            behind_rolled = pltpu.roll(behind, SPLIT, 1)
            none = jnp.zeros((HALF, TOK), F32)
            gap = TOK - REACH - HALF
            upper_rows = jnp.concatenate([none, none[:gap], ahead, ahead_rolled], axis=0)
            lower_rows = jnp.concatenate([behind_rolled, behind, none, none[:gap]], axis=0)
            both = jnp.where(iota((TOK, TOK), 1) < SPLIT, upper_rows, lower_rows)
            both = jnp.where(mask_lane, -1e30, both).astype(BF16)
            for k, first in enumerate((0, ATOMS - 2 * WIN)):
                rows = mm(
                    rhs[MARGIN + first : MARGIN + first + 2 * WIN, CH : CH + TOK], both
                ).astype(BF16)
                for w in range(2):
                    start = ((2 * k + w) * HEADS + h) * WIN
                    picked_side[start : start + WIN, :] = rows[w * WIN : (w + 1) * WIN]

        head_of = iota((WIN, CH), 1) // (CH // HEADS)

        def attend(q, bias, keys, extra, values, opened):
            split = [jnp.where(head_of == h, q, jnp.zeros_like(q)) for h in range(HEADS)]
            parts = [jnp.concatenate(split, axis=0), bias]
            if extra is not None:
                parts.append(extra)
            scores = nt(jnp.concatenate(parts, axis=1), keys)
            top = jnp.max(scores, -1, keepdims=True)
            weight = jnp.exp(scores - top).astype(BF16)
            total = mm(weight, values)
            above = total[0:WIN, 0:CH]
            below = total[0:WIN, CH:]
            for h in range(1, HEADS):
                here = head_of == h
                above = jnp.where(here, total[h * WIN : (h + 1) * WIN, 0:CH], above)
                below = jnp.where(here, total[h * WIN : (h + 1) * WIN, CH:], below)
            return (above * opened / below).astype(BF16)

        for n, w in enumerate(EDGES):
            span = slice(w * WIN, (w + 1) * WIN)
            keys = slice(w * WIN, w * WIN + KEYS)
            block = slice(w * WIN * HEADS, (w + 1) * WIN * HEADS)
            gated[span, :] = attend(
                queries[span, :],
                picked[block, :],
                rhs[keys, :],
                picked_side[n * WIN * HEADS : (n + 1) * WIN * HEADS, :],
                vals[keys, :],
                gate[span, :],
            )

        @pl.loop(2, ATOMS // WIN - 2, unroll=ATTEND_UNROLL)
        def _(w):
            start = pl.multiple_of(w * WIN, WIN)
            span = pl.ds(start, WIN)
            keys = pl.ds(start, KEYS)
            block = pl.ds(pl.multiple_of(w * WIN * HEADS, WIN * HEADS), WIN * HEADS)
            gated[span, :] = attend(
                queries[span, :],
                picked[block, :],
                rhs[keys, 0 : CH + TOK],
                None,
                vals[keys, :],
                gate[span, :],
            )

        for k in range(ATOMS // 256):
            span = slice(k * 256, (k + 1) * 256)
            ext = slice(MARGIN + k * 256, MARGIN + (k + 1) * 256)
            resid[span, :] = (atoms[ext, :].astype(F32) + mm(gated[span, :], wo[...])).astype(BF16)
        for p in range(7):
            resid_send(p).start()
        for k in range(ATOMS // 256):
            span = slice(k * 256, (k + 1) * 256)
            out = transition(resid[span, :])
            emitted[span, :] = jnp.maximum(mm(out, wk[...]), 0.0).astype(BF16)
        totals = mm(member[...], emitted[...])
        single = (totals / counts_column).astype(BF16)
        col_out[pl.ds(pl.multiple_of(odd * TOK, TOK), TOK), :] = mm(single, wc[...]).astype(BF16)
        for p in range(7):
            col_send(p).start()
        single_out[...] = single
        for p in range(7):
            single_send(p).start()
        resid_in[...] = resid[pl.ds(pl.multiple_of(c * OWN, OWN), OWN), :]

    @pl.when(not_main)
    def _():
        for w in receiver_weights:
            w.wait()
        resid_send(0).wait_recv()

    atom_out[...] = transition(resid_in[...])

    @pl.when(fed_by_main)
    def _():
        col_send(0).wait_recv()

    col_forward().start()

    @pl.when(not_main)
    def _():
        single_send(0).wait_recv()

    row_out[...] = mm(single_out[...], wr[...])
    col_forward().wait_recv()
    col_forward().wait_send()

    @pl.when(is_main)
    def _():
        for p in range(7):
            resid_send(p).wait_send()
            col_send(p).wait_send()
            single_send(p).wait_send()

    @pl.when(not_main)
    def _():
        atom_copy(c).wait_send()

    @pl.when(to_next)
    def _():
        edge_copy(True, r + 1).wait_send()

    @pl.when(to_prev)
    def _():
        edge_copy(False, r - 1).wait_send()


def update_kernel(pair, row, col, atom, single, new_pair, atom_out, single_out):
    @pl.when(pl.program_id(0) == 0)
    def _():
        atom_out[...] = atom[...]
        single_out[...] = single[...]

    column = col[...]
    for i in range(pair.shape[0]):
        term = jnp.broadcast_to(row[i : i + 1, :], (16, CH)).astype(BF16)
        term = jnp.concatenate([term] * (column.shape[0] // 16), axis=0)
        new_pair[i] = pair[i] + (column + term)


def shards(
    pair, counts, atom_single, w_bias, w_project, w_out, w_trans_in, w_trans_out, w_token, w_row, w_col
):
    any_ = pl.BlockSpec(memory_space=pl.ANY)
    vmem = pltpu.VMEM
    in_hbm = lambda a: pltpu.with_memory_space_constraint(a, pltpu.HBM)
    weights = (w_bias.T, w_project, w_out, w_trans_in, w_trans_out, w_token, w_row, w_col)
    in_vmem = pl.BlockSpec(memory_space=vmem)
    atom, single, row, col = pl.pallas_call(
        exchange_kernel,
        out_shape=(
            jax.ShapeDtypeStruct((OWN, CH), BF16),
            jax.ShapeDtypeStruct((TOK, 3 * CH), BF16),
            jax.ShapeDtypeStruct((TOK, CH), F32),
            jax.ShapeDtypeStruct((2 * TOK, CH), BF16),
        ),
        in_specs=[any_] * (3 + len(weights)),
        out_specs=(in_vmem,) * 4,
        scratch_shapes=[
            vmem((TOK, TOK, CH), BF16),
            vmem((HALF, TOK, CH), BF16),
            vmem(counts.shape, jnp.int32),
            *[vmem(w.shape, w.dtype) for w in weights],
            vmem((8 * (TOK + HALF), TOK), F32),
            vmem((8 * (TOK + HALF), TOK), F32),
            vmem((HEADS, HALF, TOK), F32),
            vmem((HEADS, HALF, TOK), F32),
            vmem((EXT, CH), BF16),
            vmem((ATOMS, CH), BF16),
            vmem((ATOMS * HEADS, TOK), BF16),
            vmem((len(EDGES) * WIN * HEADS, TOK), BF16),
            vmem((EXT, CH + 2 * TOK), BF16),
            vmem((EXT, 2 * CH), BF16),
            vmem((ATOMS, CH), F32),
            vmem((ATOMS, CH), BF16),
            vmem((ATOMS, CH), BF16),
            vmem((OWN, CH), BF16),
            vmem((ATOMS, 3 * CH), BF16),
            vmem((TOK, ATOMS), BF16),
            pltpu.SemaphoreType.DMA((TOK // STEP,)),
            pltpu.SemaphoreType.DMA((2,)),
            pltpu.SemaphoreType.DMA((1 + len(weights),)),
            pltpu.SemaphoreType.DMA((1,)),
            pltpu.SemaphoreType.DMA((29,)),
            pltpu.SemaphoreType.DMA((N_COL + 7,)),
        ],
        compiler_params=pltpu.CompilerParams(
            collective_id=0, has_side_effects=True, vmem_limit_bytes=40 * 2**20
        ),
    )(*[in_hbm(a) for a in (pair, atom_single, counts, *weights)])
    rows = 16
    whole = lambda a: pl.BlockSpec(a.shape, lambda i: (0,) * a.ndim)
    block = pl.BlockSpec((rows,) + pair.shape[1:], lambda i: (i, 0, 0))
    new_pair, atom_out, token_single = pl.pallas_call(
        update_kernel,
        grid=(pair.shape[0] // rows,),
        out_shape=(
            jax.ShapeDtypeStruct(pair.shape, BF16),
            jax.ShapeDtypeStruct(atom.shape, BF16),
            jax.ShapeDtypeStruct(single.shape, BF16),
        ),
        in_specs=[
            block,
            pl.BlockSpec((rows, CH), lambda i: (i, 0)),
            whole(col),
            whole(atom),
            whole(single),
        ],
        out_specs=(block, whole(atom), whole(single)),
        compiler_params=pltpu.CompilerParams(vmem_limit_bytes=16 * 2**20),
    )(pair, row, col, atom, single)
    return atom_out, token_single, new_pair


def solution(mesh):
    return jax.shard_map(
        shards,
        mesh=mesh,
        in_specs=(P("row", "col", None), P(), P(("row", "col"), None)) + (P(),) * 8,
        out_specs=(P(("row", "col"), None), P("row", None), P("row", "col", None)),
        check_vma=False,
    )
```

```python
import functools

import jax
import jax.numpy as jnp
from jax import lax
from jax.experimental import pallas as pl
from jax.experimental.pallas import tpu as pltpu
from jax.sharding import PartitionSpec as P

MESH = pl.DeviceIdType.MESH
F32 = jnp.float32
BF16 = jnp.bfloat16
N_ROW, N_COL = 16, 8
TOK = 128
CH = 128
HEADS = 4
WIN = 32
KEYS = 128
ATOMS = 1024
MARGIN = (KEYS - WIN) // 2
EXT = ATOMS + 2 * MARGIN
OWN = ATOMS // N_COL
STEP = 16
BLOCK = 8
UPDATE_VMEM = 20
REACH = 80
HALF = REACH // 2
EARLY = 4
EDGES = (0, 1, 30, 31)
MASK_LANE = 56
ATTEND_UNROLL = 28
SPLIT = 64


def nt(a, b):
    return lax.dot_general(a, b, (((1,), (1,)), ((), ())), preferred_element_type=F32)


def mm(a, b):
    return jnp.dot(a, b, preferred_element_type=F32)


def layer_norm(x):
    average = jnp.mean(x, -1, keepdims=True)
    centred = x - average
    spread = jnp.mean(centred * centred, -1, keepdims=True)
    return centred * lax.rsqrt(spread + 1e-05)


def iota(shape, axis):
    return lax.broadcasted_iota(jnp.int32, shape, axis)


def exchange_kernel(
    pair_hbm,
    atom_hbm,
    counts_hbm,
    wb_hbm,
    wp_hbm,
    wo_hbm,
    wi_hbm,
    wt_hbm,
    wk_hbm,
    wr_hbm,
    wc_hbm,
    atom_out,
    single_out,
    row_out,
    col_out,
    own_pair,
    side_pair,
    counts,
    wb,
    wp,
    wo,
    wi,
    wt,
    wk,
    wr,
    wc,
    stat,
    diag,
    side,
    side_in,
    atoms,
    queries,
    picked,
    picked_side,
    rhs,
    vals,
    gate,
    gated,
    resid,
    resid_in,
    final,
    emitted,
    member,
    own_sem,
    side_pair_sem,
    w_sem,
    local_sem,
    send_sem,
    recv_sem,
):
    r, c = lax.axis_index("row"), lax.axis_index("col")
    odd = lax.rem(r, 2)
    home = r // 2
    is_main = c == home
    not_main = jnp.logical_not(is_main)
    helper_col = home - 1 + 2 * odd
    has_helper = (helper_col >= 0) & (helper_col < N_COL)
    is_helper = c == helper_col
    has_prev, has_next = r > 0, r < N_ROW - 1
    z, x_hi = c // 2, lax.rem(c, 2)
    y, x_lo = r // 4, lax.rem(r // 2, 2)
    sibling = r + 1 - 2 * odd
    partner = c + 1 - 2 * x_hi
    home_side = x_hi == x_lo
    col_main = 2 * c + odd
    row_peers = [
        (lax.rem(z + dz, 4) * 2 + (1 - x_hi if dx else x_hi))
        for dz, dx in ((2, 1), (1, 1), (3, 1), (2, 0), (0, 1), (1, 0), (3, 0))
    ]
    col_peers = [
        (lax.rem(y + dy, 4) * 2 + (1 - x_lo if dx else x_lo)) * 2 + odd
        for dy, dx in ((2, 1), (1, 1), (3, 1), (2, 0), (1, 0), (3, 0), (0, 1))
    ]
    own_start = pl.multiple_of(odd * TOK, TOK)
    on_main_next = odd == 0
    side_is_next = on_main_next == is_main
    side_rows = jnp.where(side_is_next, TOK - REACH, 0)
    side_start = pl.multiple_of((1 - odd) * TOK + jnp.where(side_is_next, 0, SPLIT), SPLIT)

    def own_copy(k):
        rows = pl.ds(k * STEP, STEP)
        return pltpu.make_async_copy(
            pair_hbm.at[rows, pl.ds(own_start, TOK)], own_pair.at[rows], own_sem.at[k]
        )

    def side_pair_copy(k):
        return pltpu.make_async_copy(
            pair_hbm.at[pl.ds(side_rows + k * HALF, HALF), pl.ds(side_start, SPLIT)],
            side_pair.at[:, pl.ds(k * SPLIT, SPLIT)],
            side_pair_sem.at[k],
        )

    weights = [
        pltpu.make_async_copy(a, b, w_sem.at[i])
        for i, (a, b) in enumerate(
            [
                (wb_hbm, wb),
                (counts_hbm, counts),
                (wp_hbm, wp),
                (wo_hbm, wo),
                (wi_hbm, wi),
                (wt_hbm, wt),
                (wk_hbm, wk),
                (wr_hbm, wr),
                (wc_hbm, wc),
            ]
        )
    ]
    receiver_weights = [weights[4], weights[5], weights[7]]
    steps = TOK // STEP

    barrier = pltpu.get_barrier_semaphore()

    def hello(row, col):
        pl.semaphore_signal(barrier, inc=1, device_id=(row, col), device_id_type=MESH)

    to_next = (c == N_COL - 1) & has_next
    to_prev = (c == 0) & has_prev

    relays = not_main & home_side

    @pl.when(is_main)
    def _():
        for col in row_peers:
            hello(r, col)

        @pl.when(has_prev)
        def _():
            hello(r - 1, N_COL - 1)

        @pl.when(has_next)
        def _():
            hello(r + 1, 0)

    @pl.when(not_main)
    def _():
        hello(r, home)
        hello(col_main, c)

    hello(sibling, c)

    @pl.when(jnp.logical_not(home_side) & (partner != home))
    def _():
        hello(r, partner)

    def one(flag):
        return jnp.where(flag, 1, 0)

    greetings = (
        1
        + one(is_main) * 2 * 7
        + one(not_main)
        + one(relays)
        + one(to_next)
        + one(to_prev)
    )

    @pl.when(is_main)
    def _():
        weights[1].start()
        weights[0].start()
        for k in range(2):
            side_pair_copy(k).start()
        for k in range(steps):
            own_copy(k).start()
        for w in weights[2:]:
            w.start()

    @pl.when(not_main)
    def _():
        @pl.when(is_helper)
        def _():
            weights[0].start()
            for k in range(2):
                side_pair_copy(k).start()

        for w in receiver_weights:
            w.start()

    def atom_copy(col):
        return pltpu.make_async_remote_copy(
            src_ref=atom_hbm,
            dst_ref=atoms.at[pl.ds(MARGIN + col * OWN, OWN)],
            send_sem=send_sem.at[0],
            recv_sem=recv_sem.at[col],
            device_id=(r, home),
            device_id_type=MESH,
        )

    def edge_copy(forward, row):
        start = OWN - MARGIN if forward else 0
        return pltpu.make_async_remote_copy(
            src_ref=atom_hbm.at[pl.ds(start, MARGIN)],
            dst_ref=atoms.at[pl.ds(0 if forward else MARGIN + ATOMS, MARGIN)],
            send_sem=send_sem.at[1 if forward else 2],
            recv_sem=recv_sem.at[N_COL + (0 if forward else 1)],
            device_id=(row, row // 2),
            device_id_type=MESH,
        )

    def side_copy():
        return pltpu.make_async_remote_copy(
            src_ref=side,
            dst_ref=side_in,
            send_sem=send_sem.at[3],
            recv_sem=recv_sem.at[N_COL + 2],
            device_id=(r, home),
            device_id_type=MESH,
        )

    own_atoms = pltpu.make_async_copy(
        atom_hbm, atoms.at[pl.ds(MARGIN + c * OWN, OWN)], local_sem.at[0]
    )

    @pl.when(is_main)
    def _():
        own_atoms.start()

    lane = iota((8, TOK), 1)
    sub = iota((8, TOK), 0)
    block_of = lane // 8
    on_diag = lax.rem(lane, 8) == sub

    def bias_weights():
        w = wb[...]
        w = w - jnp.mean(w, -1, keepdims=True)
        high = w.astype(BF16)
        rest = w - high.astype(F32)
        mid = rest.astype(BF16)
        low = (rest - mid.astype(F32)).astype(BF16)
        ones = jnp.ones((1, CH), BF16)
        zeros = jnp.zeros((12, CH), BF16)
        return jnp.concatenate(
            [high, ones, zeros[:3], mid, zeros[:4], low, zeros], axis=0
        )

    def moments(x, i, first, w32):
        t = nt(jnp.concatenate([w32, x], axis=0), x)
        d = jnp.zeros((8, TOK), F32)
        for k in range(TOK // 8):
            d = jnp.where(block_of == k, t[32 + 8 * k : 40 + 8 * k], d)
        rows = pl.ds(pl.multiple_of(first + i * 8, 8), 8)
        stat[rows, :] = t[0:8] + t[8:16] + t[16:24]
        diag[rows, :] = jnp.where(on_diag, d, 0.0)

    def side_moments(w32):
        for k in range(2):
            side_pair_copy(k).wait()

        @pl.loop(0, HALF, unroll=8)
        def _(i):
            moments(side_pair[i], i, 8 * TOK, w32)

    def head_bias(first, count):
        def part(ref, s):
            return ref[pl.ds(first + s, count, stride=8), :]

        s1 = part(stat, 4)
        s2 = part(diag, 0)
        for s in range(1, 8):
            s2 = s2 + part(diag, s)
        near = (s1 * (1 / CH)).astype(BF16).astype(F32)
        offset = s1 * (1 / CH) - near
        moment = (s2 - 2 * near * s1) + CH * (near * near)
        spread = jnp.maximum(moment * (1 / CH) - offset * offset, 0.0)
        scale = lax.rsqrt(spread + 1e-05)
        return [part(stat, h) * scale for h in range(HEADS)]

    def transition(x):
        residual = x.astype(F32)
        second = layer_norm(residual).astype(BF16)
        doubled = mm(second, wi[...])
        swish = doubled[:, 0 : 2 * CH]
        hidden = swish * (0.5 + 0.5 * jnp.tanh(0.5 * swish)) * doubled[:, 2 * CH :]
        return (residual + mm(hidden.astype(BF16), wt[...])).astype(BF16)

    @pl.when(is_helper)
    def _():
        weights[0].wait()
        side_moments(bias_weights())
        for h, value in enumerate(head_bias(8 * TOK, HALF)):
            side[h] = value

    @pl.when(not_main)
    def _():
        pl.semaphore_wait(barrier, greetings)
        atom_copy(c).start()

    @pl.when(to_next & not_main)
    def _():
        edge_copy(True, r + 1).start()

    @pl.when(to_prev & not_main)
    def _():
        edge_copy(False, r - 1).start()

    @pl.when(is_helper)
    def _():
        side_copy().start()
        side_copy().wait_send()

    def send(src, dst, slot, recv, row, col):
        return pltpu.make_async_remote_copy(
            src_ref=src,
            dst_ref=dst,
            send_sem=send_sem.at[slot],
            recv_sem=recv_sem.at[recv],
            device_id=(row, col),
            device_id_type=MESH,
        )

    base = N_COL + 3

    def resid_send(p):
        col = row_peers[p]
        return send(resid.at[pl.ds(col * OWN, OWN)], resid_in, 4 + p, base, r, col)

    def single_send(p, k):
        piece = single_out.at[:, pl.ds(k * CH, CH)]
        col = (row_peers[3], row_peers[5], row_peers[6], partner)[p]
        return send(piece, piece, 12 + 4 * k + p, base + (1, 4, 5)[k], r, col)

    own_half = col_out.at[pl.ds(pl.multiple_of(odd * TOK, TOK), TOK)]

    def col_send(p):
        return send(own_half, own_half, 24 + p, base + 2, col_peers[p], c)

    def col_forward():
        return send(own_half, own_half, 31, base + 3, sibling, c)

    @pl.when(is_main)
    def _():
        weights[1].wait()
        own_counts = counts[pl.ds(r, 1), :].astype(F32)
        prev_counts = counts[pl.ds(jnp.maximum(r - 1, 0), 1), :].astype(F32)
        next_counts = counts[pl.ds(jnp.minimum(r + 1, N_ROW - 1), 1), :].astype(F32)
        stacked = jnp.concatenate(
            [own_counts, prev_counts, next_counts, jnp.zeros((5, TOK), F32)], axis=0
        )
        upper = (iota((TOK, TOK), 0) <= iota((TOK, TOK), 1)).astype(F32).astype(BF16)
        lower = (iota((TOK, TOK), 0) >= iota((TOK, TOK), 1)).astype(F32).astype(BF16)
        stacked_low = stacked.astype(BF16)
        ends = mm(stacked_low, upper)
        starts = ends - stacked
        ends_column = nt(lower, stacked_low)[:, 0:1]
        eye = (iota((TOK, TOK), 0) == iota((TOK, TOK), 1)).astype(F32).astype(BF16)
        counts_column = nt(eye, stacked_low)[:, 0:1]
        starts_column = ends_column - counts_column
        far = 1e9
        one_lane = iota((1, TOK), 1)
        after = one_lane < SPLIT
        side_from = jnp.where(
            after,
            jnp.where(has_next, starts[2:3] + ATOMS, far),
            jnp.where(has_prev, starts[1:2] - ATOMS, far),
        )
        side_to = jnp.where(
            after,
            jnp.where(has_next, ends[2:3] + ATOMS, far),
            jnp.where(has_prev, ends[1:2] - ATOMS, far),
        )
        masked = one_lane == MASK_LANE
        low_mask = jnp.where(has_prev, far, -float(MARGIN))
        mask_from = jnp.where(has_next, low_mask, float(ATOMS))
        mask_to = jnp.where(
            has_next, jnp.where(has_prev, far, 0.0), float(ATOMS + MARGIN)
        )
        side_from = jnp.where(masked, mask_from, side_from)
        side_to = jnp.where(masked, mask_to, side_to)

        def onehot(first, count, lo, hi):
            at = (iota((count, TOK), 0) + first).astype(F32)
            return jnp.where((at >= lo) & (at < hi), 1.0, 0.0).astype(BF16)

        rhs[:, CH : CH + TOK] = onehot(-MARGIN, EXT, starts[0:1], ends[0:1])
        for first in (0, ATOMS - 2 * MARGIN + WIN):
            rhs[first : first + KEYS + WIN, CH + TOK :] = onehot(
                first - MARGIN, KEYS + WIN, side_from, side_to
            )
        vals[:, CH:] = jnp.ones((EXT, CH), BF16)
        at = iota((TOK, ATOMS), 1).astype(F32)
        member[...] = jnp.where(
            (at >= starts_column) & (at < ends_column), 1.0, 0.0
        ).astype(BF16)

        weights[0].wait()
        w32 = bias_weights()
        side_moments(w32)

        @pl.loop(0, steps)
        def _(k):
            own_copy(k).wait()

            @pl.loop(0, STEP, unroll=8)
            def _(u):
                i = k * STEP + u
                moments(own_pair[i], i, 0, w32)

        for w in weights[2:]:
            w.wait()
        pl.semaphore_wait(barrier, greetings)

        @pl.when(to_next)
        def _():
            edge_copy(True, r + 1).start()

        @pl.when(to_prev)
        def _():
            edge_copy(False, r - 1).start()

        own_bias = [value.astype(BF16) for value in head_bias(0, TOK)]
        main_side = head_bias(8 * TOK, HALF)
        for h in range(HEADS):
            for k in range(ATOMS // 256):
                first = k * 256
                rows = mm(
                    rhs[MARGIN + first : MARGIN + first + 256, CH : CH + TOK], own_bias[h]
                ).astype(BF16)
                for w in range(256 // WIN):
                    start = (first + w * WIN) * HEADS + h * WIN
                    picked[start : start + WIN, :] = rows[w * WIN : (w + 1) * WIN]

        def keys_values(start, count):
            span = pl.ds(start, count)
            norm = layer_norm(atoms[span, :].astype(F32)).astype(BF16)
            projected = mm(norm, wp[...])
            rhs[span, 0:CH] = projected[:, CH : 2 * CH].astype(BF16)
            vals[span, 0:CH] = projected[:, 2 * CH : 3 * CH].astype(BF16)
            return projected

        def project(col):
            projected = keys_values(pl.multiple_of(MARGIN + col * OWN, 16), OWN)
            span = pl.ds(pl.multiple_of(col * OWN, OWN), OWN)
            gate[span, :] = 0.5 + 0.5 * jnp.tanh(0.5 * projected[:, 3 * CH :])
            queries[span, :] = (projected[:, 0:CH] * (CH // HEADS) ** -0.5).astype(BF16)

        own_atoms.wait()
        near_first = row_peers[::-1]
        for col in near_first[:EARLY]:
            atom_copy(col).wait_recv()
        for col in [c] + near_first[:EARLY]:
            project(col)

        @pl.when(has_helper)
        def _():
            side_copy().wait_recv()

        @pl.when(jnp.logical_not(has_helper))
        def _():
            side_in[...] = jnp.zeros(side_in.shape, F32)

        low_lanes = iota((HALF, TOK), 1) < SPLIT
        mask_lane = iota((TOK, TOK), 1) == MASK_LANE
        for h in range(HEADS):
            theirs = side_in[h]
            ahead = jnp.where(on_main_next, main_side[h], theirs)
            behind = jnp.where(on_main_next, theirs, main_side[h])
            ahead_rolled = pltpu.roll(ahead, SPLIT, 1)
            behind_rolled = pltpu.roll(behind, SPLIT, 1)
            none = jnp.zeros((HALF, TOK), F32)
            gap = TOK - REACH - HALF
            upper_rows = jnp.concatenate([none, none[:gap], ahead, ahead_rolled], axis=0)
            lower_rows = jnp.concatenate([behind_rolled, behind, none, none[:gap]], axis=0)
            both = jnp.where(iota((TOK, TOK), 1) < SPLIT, upper_rows, lower_rows)
            both = jnp.where(mask_lane, -1e30, both).astype(BF16)
            for k, first in enumerate((0, ATOMS - 2 * WIN)):
                rows = mm(
                    rhs[MARGIN + first : MARGIN + first + 2 * WIN, CH : CH + TOK], both
                ).astype(BF16)
                for w in range(2):
                    start = ((2 * k + w) * HEADS + h) * WIN
                    picked_side[start : start + WIN, :] = rows[w * WIN : (w + 1) * WIN]

        for col in near_first[EARLY:]:
            atom_copy(col).wait_recv()

        @pl.when(has_prev)
        def _():
            edge_copy(True, r).wait_recv()

        @pl.when(jnp.logical_not(has_prev))
        def _():
            atoms[0:MARGIN, :] = jnp.zeros((MARGIN, CH), BF16)

        @pl.when(has_next)
        def _():
            edge_copy(False, r).wait_recv()

        @pl.when(jnp.logical_not(has_next))
        def _():
            atoms[MARGIN + ATOMS :, :] = jnp.zeros((MARGIN, CH), BF16)

        for col in near_first[EARLY:]:
            project(col)
        keys_values(0, MARGIN)
        keys_values(MARGIN + ATOMS, MARGIN)

        head_of = iota((WIN, CH), 1) // (CH // HEADS)

        def attend(q, bias, keys, extra, values, opened):
            split = [jnp.where(head_of == h, q, jnp.zeros_like(q)) for h in range(HEADS)]
            parts = [jnp.concatenate(split, axis=0), bias]
            if extra is not None:
                parts.append(extra)
            scores = nt(jnp.concatenate(parts, axis=1), keys)
            top = jnp.max(scores, -1, keepdims=True)
            weight = jnp.exp(scores - top).astype(BF16)
            total = mm(weight, values)
            above = total[0:WIN, 0:CH]
            below = total[0:WIN, CH:]
            for h in range(1, HEADS):
                here = head_of == h
                above = jnp.where(here, total[h * WIN : (h + 1) * WIN, 0:CH], above)
                below = jnp.where(here, total[h * WIN : (h + 1) * WIN, CH:], below)
            return (above * opened / below).astype(BF16)

        for n, w in enumerate(EDGES):
            span = slice(w * WIN, (w + 1) * WIN)
            keys = slice(w * WIN, w * WIN + KEYS)
            block = slice(w * WIN * HEADS, (w + 1) * WIN * HEADS)
            gated[span, :] = attend(
                queries[span, :],
                picked[block, :],
                rhs[keys, :],
                picked_side[n * WIN * HEADS : (n + 1) * WIN * HEADS, :],
                vals[keys, :],
                gate[span, :],
            )

        @pl.loop(2, ATOMS // WIN - 2, unroll=ATTEND_UNROLL)
        def _(w):
            start = pl.multiple_of(w * WIN, WIN)
            span = pl.ds(start, WIN)
            keys = pl.ds(start, KEYS)
            block = pl.ds(pl.multiple_of(w * WIN * HEADS, WIN * HEADS), WIN * HEADS)
            gated[span, :] = attend(
                queries[span, :],
                picked[block, :],
                rhs[keys, 0 : CH + TOK],
                None,
                vals[keys, :],
                gate[span, :],
            )

        for k in range(ATOMS // 256):
            span = slice(k * 256, (k + 1) * 256)
            ext = slice(MARGIN + k * 256, MARGIN + (k + 1) * 256)
            resid[span, :] = (atoms[ext, :].astype(F32) + mm(gated[span, :], wo[...])).astype(BF16)
        for p in range(7):
            resid_send(p).start()
        for k in range(ATOMS // 256):
            span = slice(k * 256, (k + 1) * 256)
            final[span, :] = transition(resid[span, :])
        terms = jnp.zeros((TOK, CH), F32)
        for q in range(3):
            part = slice(q * CH, (q + 1) * CH)
            for k in range(ATOMS // 256):
                span = slice(k * 256, (k + 1) * 256)
                emitted[span, part] = jnp.maximum(mm(final[span, :], wk[:, part]), 0.0).astype(BF16)
            totals = mm(member[...], emitted[:, part])
            single = (totals / counts_column).astype(BF16)
            single_out[:, part] = single
            for p in range(4):
                single_send(p, q).start()
            terms = terms + mm(single, wc[part, :])
        col_out[pl.ds(pl.multiple_of(odd * TOK, TOK), TOK), :] = terms.astype(BF16)
        for p in range(7):
            col_send(p).start()
        resid_in[...] = resid[pl.ds(pl.multiple_of(c * OWN, OWN), OWN), :]

    @pl.when(not_main)
    def _():
        for w in receiver_weights:
            w.wait()
        resid_send(0).wait_recv()

    atom_out[...] = transition(resid_in[...])

    @pl.when(relays)
    def _():
        for k in range(3):
            single_send(0, k).wait_recv()
            single_send(3, k).start()

    @pl.when(not_main)
    def _():
        col_send(0).wait_recv()

    col_forward().start()

    @pl.when(jnp.logical_not(home_side))
    def _():
        for k in range(3):
            single_send(0, k).wait_recv()

    row_out[...] = mm(single_out[...], wr[...])
    col_forward().wait_recv()
    col_forward().wait_send()

    @pl.when(is_main)
    def _():
        for p in range(7):
            resid_send(p).wait_send()
            col_send(p).wait_send()
        for k in range(3):
            for p in range(4):
                single_send(p, k).wait_send()

    @pl.when(relays)
    def _():
        for k in range(3):
            single_send(3, k).wait_send()

    @pl.when(not_main)
    def _():
        atom_copy(c).wait_send()

    @pl.when(to_next)
    def _():
        edge_copy(True, r + 1).wait_send()

    @pl.when(to_prev)
    def _():
        edge_copy(False, r - 1).wait_send()


def update_kernel(pair, row, col, atom, single, new_pair, atom_out, single_out, result, sem):
    small = [
        pltpu.make_async_copy(atom, atom_out, sem.at[0]),
        pltpu.make_async_copy(single, single_out, sem.at[1]),
    ]
    for copy in small:
        copy.start()
    width = col.shape[0]
    column = col[...]

    def out_copy(k):
        rows = pl.ds(k * BLOCK, BLOCK)
        return pltpu.make_async_copy(result.at[rows], new_pair.at[rows], sem.at[2 + k])

    @pl.loop(0, TOK // BLOCK)
    def _(k):
        terms = row[pl.ds(pl.multiple_of(k * BLOCK, BLOCK), BLOCK), :]
        for u in range(BLOCK):
            term = jnp.broadcast_to(terms[u : u + 1], (16, CH)).astype(BF16)
            term = jnp.concatenate([term] * (width // 16), axis=0)
            i = k * BLOCK + u
            result[i] = pair[i] + (column + term)
        out_copy(k).start()

    for copy in small:
        copy.wait()
    for k in range(TOK // BLOCK):
        out_copy(k).wait()


def shards(
    pair, counts, atom_single, w_bias, w_project, w_out, w_trans_in, w_trans_out, w_token, w_row, w_col
):
    any_ = pl.BlockSpec(memory_space=pl.ANY)
    vmem = pltpu.VMEM
    in_hbm = lambda a: pltpu.with_memory_space_constraint(a, pltpu.HBM)
    weights = (w_bias.T, w_project, w_out, w_trans_in, w_trans_out, w_token, w_row, w_col)
    in_vmem = pl.BlockSpec(memory_space=vmem)
    atom, single, row, col = pl.pallas_call(
        exchange_kernel,
        out_shape=(
            jax.ShapeDtypeStruct((OWN, CH), BF16),
            jax.ShapeDtypeStruct((TOK, 3 * CH), BF16),
            jax.ShapeDtypeStruct((TOK, CH), F32),
            jax.ShapeDtypeStruct((2 * TOK, CH), BF16),
        ),
        in_specs=[any_] * (3 + len(weights)),
        out_specs=(in_vmem,) * 4,
        scratch_shapes=[
            vmem((TOK, TOK, CH), BF16),
            vmem((HALF, TOK, CH), BF16),
            vmem(counts.shape, jnp.int32),
            *[vmem(w.shape, w.dtype) for w in weights],
            vmem((8 * (TOK + HALF), TOK), F32),
            vmem((8 * (TOK + HALF), TOK), F32),
            vmem((HEADS, HALF, TOK), F32),
            vmem((HEADS, HALF, TOK), F32),
            vmem((EXT, CH), BF16),
            vmem((ATOMS, CH), BF16),
            vmem((ATOMS * HEADS, TOK), BF16),
            vmem((len(EDGES) * WIN * HEADS, TOK), BF16),
            vmem((EXT, CH + 2 * TOK), BF16),
            vmem((EXT, 2 * CH), BF16),
            vmem((ATOMS, CH), F32),
            vmem((ATOMS, CH), BF16),
            vmem((ATOMS, CH), BF16),
            vmem((OWN, CH), BF16),
            vmem((ATOMS, CH), BF16),
            vmem((ATOMS, 3 * CH), BF16),
            vmem((TOK, ATOMS), BF16),
            pltpu.SemaphoreType.DMA((TOK // STEP,)),
            pltpu.SemaphoreType.DMA((2,)),
            pltpu.SemaphoreType.DMA((1 + len(weights),)),
            pltpu.SemaphoreType.DMA((1,)),
            pltpu.SemaphoreType.DMA((32,)),
            pltpu.SemaphoreType.DMA((N_COL + 9,)),
        ],
        compiler_params=pltpu.CompilerParams(
            collective_id=0, has_side_effects=True, vmem_limit_bytes=40 * 2**20
        ),
    )(*[in_hbm(a) for a in (pair, atom_single, counts, *weights)])
    new_pair, atom_out, token_single = pl.pallas_call(
        update_kernel,
        out_shape=(
            jax.ShapeDtypeStruct(pair.shape, BF16),
            jax.ShapeDtypeStruct(atom.shape, BF16),
            jax.ShapeDtypeStruct(single.shape, BF16),
        ),
        in_specs=[in_vmem] * 5,
        out_specs=(any_,) * 3,
        scratch_shapes=[
            vmem(pair.shape, BF16),
            pltpu.SemaphoreType.DMA((2 + TOK // BLOCK,)),
        ],
        compiler_params=pltpu.CompilerParams(vmem_limit_bytes=UPDATE_VMEM * 2**20),
    )(pltpu.with_memory_space_constraint(pair, pltpu.VMEM), row, col, atom, single)
    return atom_out, token_single, new_pair


def solution(mesh):
    return jax.shard_map(
        shards,
        mesh=mesh,
        in_specs=(P("row", "col", None), P(), P(("row", "col"), None)) + (P(),) * 8,
        out_specs=(P(("row", "col"), None), P("row", None), P("row", "col", None)),
        check_vma=False,
    )
```

```python
import functools

import jax
import jax.numpy as jnp
from jax import lax
from jax.experimental import pallas as pl
from jax.experimental.pallas import tpu as pltpu
from jax.sharding import PartitionSpec as P

MESH = pl.DeviceIdType.MESH
F32 = jnp.float32
BF16 = jnp.bfloat16
N_ROW, N_COL = 16, 8
TOK = 128
CH = 128
HEADS = 4
WIN = 32
KEYS = 128
ATOMS = 1024
MARGIN = (KEYS - WIN) // 2
EXT = ATOMS + 2 * MARGIN
OWN = ATOMS // N_COL
STEP = 16
BLOCK = 8
UPDATE_VMEM = 20
REACH = 80
HALF = REACH // 2
EARLY = 4
EDGES = (0, 1, 30, 31)
MASK_LANE = 56
ATTEND_UNROLL = 28
OWN_UNROLL = 64
SIDE_UNROLL = 40
PART = 256
SPLIT = 64


def nt(a, b):
    return lax.dot_general(a, b, (((1,), (1,)), ((), ())), preferred_element_type=F32)


def mm(a, b):
    return jnp.dot(a, b, preferred_element_type=F32)


def layer_norm(x):
    average = jnp.mean(x, -1, keepdims=True)
    centred = x - average
    spread = jnp.mean(centred * centred, -1, keepdims=True)
    return centred * lax.rsqrt(spread + 1e-05)


def iota(shape, axis):
    return lax.broadcasted_iota(jnp.int32, shape, axis)


def exchange_kernel(
    pair_hbm,
    atom_hbm,
    counts_hbm,
    wb_hbm,
    wp_hbm,
    wo_hbm,
    wi_hbm,
    wt_hbm,
    wk_hbm,
    wr_hbm,
    wc_hbm,
    atom_out,
    single_out,
    row_out,
    col_out,
    own_pair,
    side_pair,
    counts,
    wb,
    wp,
    wo,
    wi,
    wt,
    wk,
    wr,
    wc,
    stat,
    diag,
    side,
    side_in,
    atoms,
    queries,
    picked,
    picked_side,
    rhs,
    vals,
    gate,
    gated,
    resid,
    resid_in,
    mine_in,
    final,
    emitted,
    member,
    own_sem,
    side_pair_sem,
    w_sem,
    local_sem,
    send_sem,
    recv_sem,
):
    r, c = lax.axis_index("row"), lax.axis_index("col")
    odd = lax.rem(r, 2)
    home = r // 2
    is_main = c == home
    not_main = jnp.logical_not(is_main)
    helper_col = home - 1 + 2 * odd
    has_helper = (helper_col >= 0) & (helper_col < N_COL)
    is_helper = c == helper_col
    has_prev, has_next = r > 0, r < N_ROW - 1
    z, x_hi = c // 2, lax.rem(c, 2)
    y, x_lo = r // 4, lax.rem(r // 2, 2)
    sibling = r + 1 - 2 * odd
    partner = c + 1 - 2 * x_hi
    home_side = x_hi == x_lo
    col_main = 2 * c + odd
    row_peers = [
        (lax.rem(z + dz, 4) * 2 + (1 - x_hi if dx else x_hi))
        for dz, dx in ((2, 1), (1, 1), (3, 1), (2, 0), (0, 1), (1, 0), (3, 0))
    ]
    col_peers = [
        (lax.rem(y + dy, 4) * 2 + (1 - x_lo if dx else x_lo)) * 2 + odd
        for dy, dx in ((2, 1), (1, 1), (3, 1), (2, 0), (1, 0), (3, 0), (0, 1))
    ]
    own_start = pl.multiple_of(odd * TOK, TOK)
    on_main_next = odd == 0
    side_is_next = on_main_next == is_main
    side_rows = jnp.where(side_is_next, TOK - REACH, 0)
    side_start = pl.multiple_of((1 - odd) * TOK + jnp.where(side_is_next, 0, SPLIT), SPLIT)

    def own_copy(k):
        rows = pl.ds(k * STEP, STEP)
        return pltpu.make_async_copy(
            pair_hbm.at[rows, pl.ds(own_start, TOK)], own_pair.at[rows], own_sem.at[k]
        )

    def side_pair_copy(k):
        return pltpu.make_async_copy(
            pair_hbm.at[pl.ds(side_rows + k * HALF, HALF), pl.ds(side_start, SPLIT)],
            side_pair.at[:, pl.ds(k * SPLIT, SPLIT)],
            side_pair_sem.at[k],
        )

    weights = [
        pltpu.make_async_copy(a, b, w_sem.at[i])
        for i, (a, b) in enumerate(
            [
                (wb_hbm, wb),
                (counts_hbm, counts),
                (wp_hbm, wp),
                (wo_hbm, wo),
                (wi_hbm, wi),
                (wt_hbm, wt),
                (wk_hbm, wk),
                (wr_hbm, wr),
                (wc_hbm, wc),
            ]
        )
    ]
    receiver_weights = [weights[4], weights[5], weights[7]]
    steps = TOK // STEP

    own_atoms = pltpu.make_async_copy(
        atom_hbm, atoms.at[pl.ds(MARGIN + c * OWN, OWN)], local_sem.at[0]
    )
    mine = pltpu.make_async_copy(atom_hbm, mine_in, local_sem.at[1])
    mine.start()
    barrier = pltpu.get_barrier_semaphore()

    def hello(row, col):
        pl.semaphore_signal(barrier, inc=1, device_id=(row, col), device_id_type=MESH)

    to_next = (c == N_COL - 1) & has_next
    to_prev = (c == 0) & has_prev

    across = jnp.logical_not(home_side)
    ahead_of_home = lax.rem(z - y + 4, 4)
    relays = not_main & ((home_side & (ahead_of_home != 2)) | (across & (ahead_of_home == 0)))
    passes_atoms = not_main & home_side
    feeder = jnp.where(home_side, lax.rem(z + 3, 4), lax.rem(z + 2, 4)) * 2 + x_hi

    @pl.when(is_main)
    def _():
        for col in row_peers:
            hello(r, col)

        @pl.when(has_prev)
        def _():
            hello(r - 1, N_COL - 1)

        @pl.when(has_next)
        def _():
            hello(r + 1, 0)

    @pl.when(not_main)
    def _():
        hello(r, home)
        hello(col_main, c)

    hello(sibling, c)

    @pl.when(across & (ahead_of_home != 0))
    def _():
        hello(r, partner)

    @pl.when(ahead_of_home == 2)
    def _():
        hello(r, feeder)

    def one(flag):
        return jnp.where(flag, 1, 0)

    greetings = (
        1
        + one(is_main) * 2 * 7
        + one(not_main)
        + one(passes_atoms)
        + one(ahead_of_home == 1) * one(home_side)
        + one(ahead_of_home == 0) * one(across)
        + one(to_next)
        + one(to_prev)
    )

    @pl.when(is_main)
    def _():
        weights[1].start()
        own_atoms.start()
        weights[0].start()
        for k in range(2):
            side_pair_copy(k).start()
        for k in range(steps):
            own_copy(k).start()
        for w in weights[2:]:
            w.start()

    @pl.when(not_main)
    def _():
        @pl.when(is_helper)
        def _():
            weights[0].start()
            for k in range(2):
                side_pair_copy(k).start()

        for w in receiver_weights:
            w.start()

    def atom_copy(col):
        return pltpu.make_async_remote_copy(
            src_ref=mine_in,
            dst_ref=atoms.at[pl.ds(MARGIN + col * OWN, OWN)],
            send_sem=send_sem.at[0],
            recv_sem=recv_sem.at[col],
            device_id=(r, home),
            device_id_type=MESH,
        )

    def edge_copy(forward, row):
        start = OWN - MARGIN if forward else 0
        return pltpu.make_async_remote_copy(
            src_ref=mine_in.at[pl.ds(start, MARGIN)],
            dst_ref=atoms.at[pl.ds(0 if forward else MARGIN + ATOMS, MARGIN)],
            send_sem=send_sem.at[1 if forward else 2],
            recv_sem=recv_sem.at[N_COL + (0 if forward else 1)],
            device_id=(row, row // 2),
            device_id_type=MESH,
        )

    def side_copy():
        return pltpu.make_async_remote_copy(
            src_ref=side,
            dst_ref=side_in,
            send_sem=send_sem.at[3],
            recv_sem=recv_sem.at[N_COL + 2],
            device_id=(r, home),
            device_id_type=MESH,
        )


    lane = iota((8, TOK), 1)
    sub = iota((8, TOK), 0)
    block_of = lane // 8
    on_diag = lax.rem(lane, 8) == sub

    def bias_weights():
        w = wb[...]
        w = w - jnp.mean(w, -1, keepdims=True)
        high = w.astype(BF16)
        rest = w - high.astype(F32)
        mid = rest.astype(BF16)
        low = (rest - mid.astype(F32)).astype(BF16)
        ones = jnp.ones((1, CH), BF16)
        zeros = jnp.zeros((12, CH), BF16)
        return jnp.concatenate(
            [high, ones, zeros[:3], mid, zeros[:4], low, zeros], axis=0
        )

    def moments(x, i, first, w32):
        t = nt(jnp.concatenate([w32, x], axis=0), x)
        d = jnp.zeros((8, TOK), F32)
        for k in range(TOK // 8):
            d = jnp.where(block_of == k, t[32 + 8 * k : 40 + 8 * k], d)
        rows = pl.ds(pl.multiple_of(first + i * 8, 8), 8)
        stat[rows, :] = t[0:8] + t[8:16] + t[16:24]
        diag[rows, :] = jnp.where(on_diag, d, 0.0)

    def side_moments(w32):
        for k in range(2):
            side_pair_copy(k).wait()

        @pl.loop(0, HALF, unroll=SIDE_UNROLL)
        def _(i):
            moments(side_pair[i], i, 8 * TOK, w32)

    def head_bias(first, count):
        def part(ref, s):
            return ref[pl.ds(first + s, count, stride=8), :]

        s1 = part(stat, 4)
        s2 = part(diag, 0)
        for s in range(1, 8):
            s2 = s2 + part(diag, s)
        near = (s1 * (1 / CH)).astype(BF16).astype(F32)
        offset = s1 * (1 / CH) - near
        moment = (s2 - 2 * near * s1) + CH * (near * near)
        spread = jnp.maximum(moment * (1 / CH) - offset * offset, 0.0)
        scale = lax.rsqrt(spread + 1e-05)
        return [part(stat, h) * scale for h in range(HEADS)]

    def transition(x):
        residual = x.astype(F32)
        second = layer_norm(residual).astype(BF16)
        doubled = mm(second, wi[...])
        swish = doubled[:, 0 : 2 * CH]
        hidden = swish * (0.5 + 0.5 * jnp.tanh(0.5 * swish)) * doubled[:, 2 * CH :]
        return (residual + mm(hidden.astype(BF16), wt[...])).astype(BF16)

    @pl.when(is_helper)
    def _():
        weights[0].wait()
        side_moments(bias_weights())
        for h, value in enumerate(head_bias(8 * TOK, HALF)):
            side[h] = value

    @pl.when(not_main)
    def _():
        mine.wait()
        pl.semaphore_wait(barrier, greetings)
        atom_copy(c).start()

    @pl.when(to_next & not_main)
    def _():
        edge_copy(True, r + 1).start()

    @pl.when(to_prev & not_main)
    def _():
        edge_copy(False, r - 1).start()

    @pl.when(is_helper)
    def _():
        side_copy().start()
        side_copy().wait_send()

    def send(src, dst, slot, recv, row, col):
        return pltpu.make_async_remote_copy(
            src_ref=src,
            dst_ref=dst,
            send_sem=send_sem.at[slot],
            recv_sem=recv_sem.at[recv],
            device_id=(row, col),
            device_id_type=MESH,
        )

    base = N_COL + 3

    def resid_send(p):
        col = (partner, row_peers[5], row_peers[6], row_peers[3])[p]
        count = OWN if p == 0 else 2 * OWN
        first = col if p == 0 else col // 2 * 2
        return send(
            resid.at[pl.ds(pl.multiple_of(first * OWN, OWN), count)],
            resid_in.at[pl.ds(0, count)],
            4 + p,
            base,
            r,
            col,
        )

    def atom_pass():
        return send(
            resid_in.at[pl.ds(pl.multiple_of((1 - x_hi) * OWN, OWN), OWN)],
            atom_out,
            8,
            base + 6,
            r,
            partner,
        )

    def single_send(p, k):
        piece = single_out.at[k]
        col = (row_peers[5], row_peers[6], partner, row_peers[3])[p]
        return send(piece, piece, 12 + 4 * k + p, base + (1, 4, 5)[k], r, col)

    tree = (
        (is_main, (0, 1, 2)),
        (home_side & (ahead_of_home == 1), (0, 2)),
        (home_side & (ahead_of_home == 3), (2,)),
        (across & (ahead_of_home == 0), (3,)),
    )

    own_half = col_out.at[pl.ds(pl.multiple_of(odd * TOK, TOK), TOK)]

    def col_send(p):
        return send(own_half, own_half, 24 + p, base + 2, col_peers[p], c)

    def col_forward():
        return send(own_half, own_half, 31, base + 3, sibling, c)

    @pl.when(is_main)
    def _():
        weights[1].wait()
        own_counts = counts[pl.ds(r, 1), :].astype(F32)
        prev_counts = counts[pl.ds(jnp.maximum(r - 1, 0), 1), :].astype(F32)
        next_counts = counts[pl.ds(jnp.minimum(r + 1, N_ROW - 1), 1), :].astype(F32)
        stacked = jnp.concatenate(
            [own_counts, prev_counts, next_counts, jnp.zeros((5, TOK), F32)], axis=0
        )
        upper = (iota((TOK, TOK), 0) <= iota((TOK, TOK), 1)).astype(F32).astype(BF16)
        lower = (iota((TOK, TOK), 0) >= iota((TOK, TOK), 1)).astype(F32).astype(BF16)
        stacked_low = stacked.astype(BF16)
        ends = mm(stacked_low, upper)
        starts = ends - stacked
        ends_column = nt(lower, stacked_low)[:, 0:1]
        eye = (iota((TOK, TOK), 0) == iota((TOK, TOK), 1)).astype(F32).astype(BF16)
        counts_column = nt(eye, stacked_low)[:, 0:1]
        starts_column = ends_column - counts_column
        far = 1e9
        one_lane = iota((1, TOK), 1)
        after = one_lane < SPLIT
        side_from = jnp.where(
            after,
            jnp.where(has_next, starts[2:3] + ATOMS, far),
            jnp.where(has_prev, starts[1:2] - ATOMS, far),
        )
        side_to = jnp.where(
            after,
            jnp.where(has_next, ends[2:3] + ATOMS, far),
            jnp.where(has_prev, ends[1:2] - ATOMS, far),
        )
        masked = one_lane == MASK_LANE
        low_mask = jnp.where(has_prev, far, -float(MARGIN))
        mask_from = jnp.where(has_next, low_mask, float(ATOMS))
        mask_to = jnp.where(
            has_next, jnp.where(has_prev, far, 0.0), float(ATOMS + MARGIN)
        )
        side_from = jnp.where(masked, mask_from, side_from)
        side_to = jnp.where(masked, mask_to, side_to)

        def onehot(first, count, lo, hi):
            at = (iota((count, TOK), 0) + first).astype(F32)
            return jnp.where((at >= lo) & (at < hi), 1.0, 0.0).astype(BF16)

        rhs[:, CH : CH + TOK] = onehot(-MARGIN, EXT, starts[0:1], ends[0:1])
        for first in (0, ATOMS - 2 * MARGIN + WIN):
            rhs[first : first + KEYS + WIN, CH + TOK :] = onehot(
                first - MARGIN, KEYS + WIN, side_from, side_to
            )
        vals[:, CH:] = jnp.ones((EXT, CH), BF16)
        at = iota((TOK, ATOMS), 1).astype(F32)
        member[...] = jnp.where(
            (at >= starts_column) & (at < ends_column), 1.0, 0.0
        ).astype(BF16)

        weights[0].wait()
        w32 = bias_weights()
        side_moments(w32)

        @pl.loop(0, TOK // OWN_UNROLL)
        def _(k):
            for u in range(OWN_UNROLL // STEP):
                own_copy(k * (OWN_UNROLL // STEP) + u).wait()
            for u in range(OWN_UNROLL):
                i = k * OWN_UNROLL + u
                moments(own_pair[i], i, 0, w32)

        for w in weights[2:]:
            w.wait()
        mine.wait()
        pl.semaphore_wait(barrier, greetings)

        @pl.when(to_next)
        def _():
            edge_copy(True, r + 1).start()

        @pl.when(to_prev)
        def _():
            edge_copy(False, r - 1).start()

        own_atoms.wait()
        near_first = row_peers[::-1]
        for col in near_first[:EARLY]:
            atom_copy(col).wait_recv()
        own_bias = [value.astype(BF16) for value in head_bias(0, TOK)]
        main_side = head_bias(8 * TOK, HALF)
        for h in range(HEADS):
            for k in range(ATOMS // 256):
                first = k * 256
                rows = mm(
                    rhs[MARGIN + first : MARGIN + first + 256, CH : CH + TOK], own_bias[h]
                ).astype(BF16)
                for w in range(256 // WIN):
                    start = (first + w * WIN) * HEADS + h * WIN
                    picked[start : start + WIN, :] = rows[w * WIN : (w + 1) * WIN]

        def keys_values(start, count):
            span = pl.ds(start, count)
            norm = layer_norm(atoms[span, :].astype(F32)).astype(BF16)
            projected = mm(norm, wp[...])
            rhs[span, 0:CH] = projected[:, CH : 2 * CH].astype(BF16)
            vals[span, 0:CH] = projected[:, 2 * CH : 3 * CH].astype(BF16)
            return projected

        def project(col):
            projected = keys_values(pl.multiple_of(MARGIN + col * OWN, 16), OWN)
            span = pl.ds(pl.multiple_of(col * OWN, OWN), OWN)
            gate[span, :] = 0.5 + 0.5 * jnp.tanh(0.5 * projected[:, 3 * CH :])
            queries[span, :] = (projected[:, 0:CH] * (CH // HEADS) ** -0.5).astype(BF16)

        for col in [c] + near_first[:EARLY]:
            project(col)

        @pl.when(has_helper)
        def _():
            side_copy().wait_recv()

        @pl.when(jnp.logical_not(has_helper))
        def _():
            side_in[...] = jnp.zeros(side_in.shape, F32)

        low_lanes = iota((HALF, TOK), 1) < SPLIT
        mask_lane = iota((TOK, TOK), 1) == MASK_LANE
        for h in range(HEADS):
            theirs = side_in[h]
            ahead = jnp.where(on_main_next, main_side[h], theirs)
            behind = jnp.where(on_main_next, theirs, main_side[h])
            ahead_rolled = pltpu.roll(ahead, SPLIT, 1)
            behind_rolled = pltpu.roll(behind, SPLIT, 1)
            none = jnp.zeros((HALF, TOK), F32)
            gap = TOK - REACH - HALF
            upper_rows = jnp.concatenate([none, none[:gap], ahead, ahead_rolled], axis=0)
            lower_rows = jnp.concatenate([behind_rolled, behind, none, none[:gap]], axis=0)
            both = jnp.where(iota((TOK, TOK), 1) < SPLIT, upper_rows, lower_rows)
            both = jnp.where(mask_lane, -1e30, both).astype(BF16)
            for k, first in enumerate((0, ATOMS - 2 * WIN)):
                rows = mm(
                    rhs[MARGIN + first : MARGIN + first + 2 * WIN, CH : CH + TOK], both
                ).astype(BF16)
                for w in range(2):
                    start = ((2 * k + w) * HEADS + h) * WIN
                    picked_side[start : start + WIN, :] = rows[w * WIN : (w + 1) * WIN]

        for col in near_first[EARLY:]:
            atom_copy(col).wait_recv()

        @pl.when(has_prev)
        def _():
            edge_copy(True, r).wait_recv()

        @pl.when(jnp.logical_not(has_prev))
        def _():
            atoms[0:MARGIN, :] = jnp.zeros((MARGIN, CH), BF16)

        @pl.when(has_next)
        def _():
            edge_copy(False, r).wait_recv()

        @pl.when(jnp.logical_not(has_next))
        def _():
            atoms[MARGIN + ATOMS :, :] = jnp.zeros((MARGIN, CH), BF16)

        for col in near_first[EARLY:]:
            project(col)
        keys_values(0, MARGIN)
        keys_values(MARGIN + ATOMS, MARGIN)

        head_of = iota((WIN, CH), 1) // (CH // HEADS)

        def attend(q, bias, keys, extra, values, opened):
            split = [jnp.where(head_of == h, q, jnp.zeros_like(q)) for h in range(HEADS)]
            parts = [jnp.concatenate(split, axis=0), bias]
            if extra is not None:
                parts.append(extra)
            scores = nt(jnp.concatenate(parts, axis=1), keys)
            top = jnp.max(scores, -1, keepdims=True)
            weight = jnp.exp(scores - top).astype(BF16)
            total = mm(weight, values)
            above = total[0:WIN, 0:CH]
            below = total[0:WIN, CH:]
            for h in range(1, HEADS):
                here = head_of == h
                above = jnp.where(here, total[h * WIN : (h + 1) * WIN, 0:CH], above)
                below = jnp.where(here, total[h * WIN : (h + 1) * WIN, CH:], below)
            return (above * opened / below).astype(BF16)

        for n, w in enumerate(EDGES):
            span = slice(w * WIN, (w + 1) * WIN)
            keys = slice(w * WIN, w * WIN + KEYS)
            block = slice(w * WIN * HEADS, (w + 1) * WIN * HEADS)
            gated[span, :] = attend(
                queries[span, :],
                picked[block, :],
                rhs[keys, :],
                picked_side[n * WIN * HEADS : (n + 1) * WIN * HEADS, :],
                vals[keys, :],
                gate[span, :],
            )

        @pl.loop(2, ATOMS // WIN - 2, unroll=ATTEND_UNROLL)
        def _(w):
            start = pl.multiple_of(w * WIN, WIN)
            span = pl.ds(start, WIN)
            keys = pl.ds(start, KEYS)
            block = pl.ds(pl.multiple_of(w * WIN * HEADS, WIN * HEADS), WIN * HEADS)
            gated[span, :] = attend(
                queries[span, :],
                picked[block, :],
                rhs[keys, 0 : CH + TOK],
                None,
                vals[keys, :],
                gate[span, :],
            )

        for k in range(ATOMS // 256):
            span = slice(k * 256, (k + 1) * 256)
            ext = slice(MARGIN + k * 256, MARGIN + (k + 1) * 256)
            resid[span, :] = (atoms[ext, :].astype(F32) + mm(gated[span, :], wo[...])).astype(BF16)
        for p in range(4):
            resid_send(p).start()
        for k in range(ATOMS // PART):
            span = slice(k * PART, (k + 1) * PART)
            final[span, :] = transition(resid[span, :])
        terms = jnp.zeros((TOK, CH), F32)
        for q in range(3):
            part = slice(q * CH, (q + 1) * CH)
            for k in range(ATOMS // 256):
                span = slice(k * 256, (k + 1) * 256)
                emitted[span, part] = jnp.maximum(mm(final[span, :], wk[:, part]), 0.0).astype(BF16)
            totals = mm(member[...], emitted[:, part])
            single = (totals / counts_column).astype(BF16)
            single_out[q] = single
            for p in tree[0][1]:
                single_send(p, q).start()
            terms = terms + mm(single, wc[part, :])
        col_out[pl.ds(pl.multiple_of(odd * TOK, TOK), TOK), :] = terms.astype(BF16)
        for p in range(7):
            col_send(p).start()
        resid_in[0:OWN, :] = resid[pl.ds(pl.multiple_of(c * OWN, OWN), OWN), :]

    @pl.when(not_main)
    def _():
        for w in receiver_weights:
            w.wait()

    @pl.when(passes_atoms)
    def _():
        resid_send(1).wait_recv()
        resid_in[...] = transition(resid_in[...])
        atom_pass().start()
        atom_out[...] = resid_in[pl.ds(pl.multiple_of(x_hi * OWN, OWN), OWN), :]

    @pl.when(across & (ahead_of_home == 0))
    def _():
        resid_send(0).wait_recv()

    @pl.when(ahead_of_home == 0)
    def _():
        atom_out[...] = transition(resid_in[0:OWN, :])

    for role, copies in tree[1:]:

        @pl.when(role)
        def _():
            for k in range(3):
                single_send(0, k).wait_recv()
                for p in copies:
                    single_send(p, k).start()

    @pl.when(not_main)
    def _():
        col_send(0).wait_recv()

    col_forward().start()

    @pl.when(not_main & jnp.logical_not(relays))
    def _():
        for k in range(3):
            single_send(0, k).wait_recv()

    row_out[...] = sum(mm(single_out[q], wr[q * CH : (q + 1) * CH, :]) for q in range(3))
    col_forward().wait_recv()
    col_forward().wait_send()

    @pl.when(passes_atoms)
    def _():
        atom_pass().wait_send()

    @pl.when(across & (ahead_of_home != 0))
    def _():
        atom_pass().wait_recv()

    @pl.when(is_main)
    def _():
        for p in range(4):
            resid_send(p).wait_send()
        for p in range(7):
            col_send(p).wait_send()

    for role, copies in tree:

        @pl.when(role)
        def _():
            for k in range(3):
                for p in copies:
                    single_send(p, k).wait_send()

    @pl.when(not_main)
    def _():
        atom_copy(c).wait_send()

    @pl.when(to_next)
    def _():
        edge_copy(True, r + 1).wait_send()

    @pl.when(to_prev)
    def _():
        edge_copy(False, r - 1).wait_send()


def update_kernel(pair, row, col, atom, single, new_pair, atom_out, single_out, result, sem):
    small = [
        pltpu.make_async_copy(atom, atom_out, sem.at[0]),
    ] + [
        pltpu.make_async_copy(single.at[q], single_out.at[:, pl.ds(q * CH, CH)], sem.at[1 + q])
        for q in range(3)
    ]
    for copy in small:
        copy.start()
    width = col.shape[0]
    column = col[...]

    def out_copy(k):
        rows = pl.ds(k * BLOCK, BLOCK)
        return pltpu.make_async_copy(result.at[rows], new_pair.at[rows], sem.at[4 + k])

    @pl.loop(0, TOK // BLOCK)
    def _(k):
        terms = row[pl.ds(pl.multiple_of(k * BLOCK, BLOCK), BLOCK), :]
        for u in range(BLOCK):
            term = jnp.broadcast_to(terms[u : u + 1], (16, CH)).astype(BF16)
            term = jnp.concatenate([term] * (width // 16), axis=0)
            i = k * BLOCK + u
            result[i] = pair[i] + (column + term)
        out_copy(k).start()

    for copy in small:
        copy.wait()
    for k in range(TOK // BLOCK):
        out_copy(k).wait()


def shards(
    pair, counts, atom_single, w_bias, w_project, w_out, w_trans_in, w_trans_out, w_token, w_row, w_col
):
    any_ = pl.BlockSpec(memory_space=pl.ANY)
    vmem = pltpu.VMEM
    in_hbm = lambda a: pltpu.with_memory_space_constraint(a, pltpu.HBM)
    weights = (w_bias.T, w_project, w_out, w_trans_in, w_trans_out, w_token, w_row, w_col)
    in_vmem = pl.BlockSpec(memory_space=vmem)
    atom, single, row, col = pl.pallas_call(
        exchange_kernel,
        out_shape=(
            jax.ShapeDtypeStruct((OWN, CH), BF16),
            jax.ShapeDtypeStruct((3, TOK, CH), BF16),
            jax.ShapeDtypeStruct((TOK, CH), F32),
            jax.ShapeDtypeStruct((2 * TOK, CH), BF16),
        ),
        in_specs=[any_] * (3 + len(weights)),
        out_specs=(in_vmem,) * 4,
        scratch_shapes=[
            vmem((TOK, TOK, CH), BF16),
            vmem((HALF, TOK, CH), BF16),
            vmem(counts.shape, jnp.int32),
            *[vmem(w.shape, w.dtype) for w in weights],
            vmem((8 * (TOK + HALF), TOK), F32),
            vmem((8 * (TOK + HALF), TOK), F32),
            vmem((HEADS, HALF, TOK), F32),
            vmem((HEADS, HALF, TOK), F32),
            vmem((EXT, CH), BF16),
            vmem((ATOMS, CH), BF16),
            vmem((ATOMS * HEADS, TOK), BF16),
            vmem((len(EDGES) * WIN * HEADS, TOK), BF16),
            vmem((EXT, CH + 2 * TOK), BF16),
            vmem((EXT, 2 * CH), BF16),
            vmem((ATOMS, CH), F32),
            vmem((ATOMS, CH), BF16),
            vmem((ATOMS, CH), BF16),
            vmem((2 * OWN, CH), BF16),
            vmem((OWN, CH), BF16),
            vmem((ATOMS, CH), BF16),
            vmem((ATOMS, 3 * CH), BF16),
            vmem((TOK, ATOMS), BF16),
            pltpu.SemaphoreType.DMA((TOK // STEP,)),
            pltpu.SemaphoreType.DMA((2,)),
            pltpu.SemaphoreType.DMA((1 + len(weights),)),
            pltpu.SemaphoreType.DMA((2,)),
            pltpu.SemaphoreType.DMA((32,)),
            pltpu.SemaphoreType.DMA((N_COL + 10,)),
        ],
        compiler_params=pltpu.CompilerParams(
            collective_id=0, has_side_effects=True, vmem_limit_bytes=40 * 2**20
        ),
    )(*[in_hbm(a) for a in (pair, atom_single, counts, *weights)])
    new_pair, atom_out, token_single = pl.pallas_call(
        update_kernel,
        out_shape=(
            jax.ShapeDtypeStruct(pair.shape, BF16),
            jax.ShapeDtypeStruct(atom.shape, BF16),
            jax.ShapeDtypeStruct((TOK, 3 * CH), BF16),
        ),
        in_specs=[in_vmem] * 5,
        out_specs=(any_,) * 3,
        scratch_shapes=[
            vmem(pair.shape, BF16),
            pltpu.SemaphoreType.DMA((4 + TOK // BLOCK,)),
        ],
        compiler_params=pltpu.CompilerParams(vmem_limit_bytes=UPDATE_VMEM * 2**20),
    )(pltpu.with_memory_space_constraint(pair, pltpu.VMEM), row, col, atom, single)
    return atom_out, token_single, new_pair


def solution(mesh):
    return jax.shard_map(
        shards,
        mesh=mesh,
        in_specs=(P("row", "col", None), P(), P(("row", "col"), None)) + (P(),) * 8,
        out_specs=(P(("row", "col"), None), P("row", None), P("row", "col", None)),
        check_vma=False,
    )
```

```python
import functools

import jax
import jax.numpy as jnp
from jax import lax
from jax.experimental import pallas as pl
from jax.experimental.pallas import tpu as pltpu
from jax.sharding import PartitionSpec as P

MESH = pl.DeviceIdType.MESH
F32 = jnp.float32
BF16 = jnp.bfloat16
N_ROW, N_COL = 16, 8
TOK = 128
CH = 128
HEADS = 4
WIN = 32
KEYS = 128
ATOMS = 1024
MARGIN = (KEYS - WIN) // 2
EXT = ATOMS + 2 * MARGIN
OWN = ATOMS // N_COL
STEP = 16
BLOCK = 8
UPDATE_VMEM = 20
REACH = 80
HALF = REACH // 2
EARLY = 4
EDGES = (0, 1, 30, 31)
MASK_LANE = 56
ATTEND_UNROLL = 28
OWN_UNROLL = 64
SIDE_UNROLL = 40
PART = 256
SPLIT = 64


def nt(a, b):
    return lax.dot_general(a, b, (((1,), (1,)), ((), ())), preferred_element_type=F32)


def mm(a, b):
    return jnp.dot(a, b, preferred_element_type=F32)


def layer_norm(x):
    average = jnp.mean(x, -1, keepdims=True)
    centred = x - average
    spread = jnp.mean(centred * centred, -1, keepdims=True)
    return centred * lax.rsqrt(spread + 1e-05)


def iota(shape, axis):
    return lax.broadcasted_iota(jnp.int32, shape, axis)


def exchange_kernel(
    pair_hbm,
    atom_hbm,
    counts_hbm,
    wb_hbm,
    wp_hbm,
    wo_hbm,
    wi_hbm,
    wt_hbm,
    wk_hbm,
    wr_hbm,
    wc_hbm,
    atom_out,
    single_out,
    row_out,
    col_out,
    own_pair,
    side_pair,
    counts,
    wb,
    wp,
    wo,
    wi,
    wt,
    wk,
    wr,
    wc,
    stat,
    diag,
    side,
    side_in,
    atoms,
    queries,
    picked,
    picked_side,
    rhs,
    vals,
    gate,
    gated,
    resid,
    resid_in,
    mine_in,
    final,
    emitted,
    member,
    own_sem,
    side_pair_sem,
    w_sem,
    local_sem,
    send_sem,
    recv_sem,
):
    r, c = lax.axis_index("row"), lax.axis_index("col")
    odd = lax.rem(r, 2)
    home = r // 2
    is_main = c == home
    not_main = jnp.logical_not(is_main)
    helper_col = home - 1 + 2 * odd
    has_helper = (helper_col >= 0) & (helper_col < N_COL)
    is_helper = c == helper_col
    has_prev, has_next = r > 0, r < N_ROW - 1
    z, x_hi = c // 2, lax.rem(c, 2)
    y, x_lo = r // 4, lax.rem(r // 2, 2)
    sibling = r + 1 - 2 * odd
    partner = c + 1 - 2 * x_hi
    home_side = x_hi == x_lo
    row_peers = [
        (lax.rem(z + dz, 4) * 2 + (1 - x_hi if dx else x_hi))
        for dz, dx in ((2, 1), (1, 1), (3, 1), (2, 0), (0, 1), (1, 0), (3, 0))
    ]
    col_peers = [
        (lax.rem(y + dy, 4) * 2 + (1 - x_lo if dx else x_lo)) * 2 + odd
        for dy, dx in ((2, 1), (1, 1), (3, 1), (2, 0), (1, 0), (3, 0), (0, 1))
    ]
    own_start = pl.multiple_of(odd * TOK, TOK)
    on_main_next = odd == 0
    side_is_next = on_main_next == is_main
    side_rows = jnp.where(side_is_next, TOK - REACH, 0)
    side_start = pl.multiple_of((1 - odd) * TOK + jnp.where(side_is_next, 0, SPLIT), SPLIT)

    def own_copy(k):
        rows = pl.ds(k * STEP, STEP)
        return pltpu.make_async_copy(
            pair_hbm.at[rows, pl.ds(own_start, TOK)], own_pair.at[rows], own_sem.at[k]
        )

    def side_pair_copy(k):
        return pltpu.make_async_copy(
            pair_hbm.at[pl.ds(side_rows + k * HALF, HALF), pl.ds(side_start, SPLIT)],
            side_pair.at[:, pl.ds(k * SPLIT, SPLIT)],
            side_pair_sem.at[k],
        )

    weights = [
        pltpu.make_async_copy(a, b, w_sem.at[i])
        for i, (a, b) in enumerate(
            [
                (wb_hbm, wb),
                (counts_hbm, counts),
                (wp_hbm, wp),
                (wo_hbm, wo),
                (wi_hbm, wi),
                (wt_hbm, wt),
                (wk_hbm, wk),
                (wr_hbm, wr),
                (wc_hbm, wc),
            ]
        )
    ]
    receiver_weights = [weights[4], weights[5], weights[7]]
    steps = TOK // STEP

    own_atoms = pltpu.make_async_copy(
        atom_hbm, atoms.at[pl.ds(MARGIN + c * OWN, OWN)], local_sem.at[0]
    )
    mine = pltpu.make_async_copy(atom_hbm, mine_in, local_sem.at[1])
    mine.start()
    barrier = pltpu.get_barrier_semaphore()

    def hello(row, col):
        pl.semaphore_signal(barrier, inc=1, device_id=(row, col), device_id_type=MESH)

    to_next = (c == N_COL - 1) & has_next
    to_prev = (c == 0) & has_prev

    across = jnp.logical_not(home_side)
    ahead_of_home = lax.rem(z - y + 4, 4)
    relays = not_main & ((home_side & (ahead_of_home != 2)) | (across & (ahead_of_home == 0)))
    passes_atoms = not_main & home_side
    @pl.when(is_main)
    def _():
        for col in row_peers:
            hello(r, col)

        @pl.when(has_prev)
        def _():
            hello(r - 1, N_COL - 1)

        @pl.when(has_next)
        def _():
            hello(r + 1, 0)

    @pl.when(not_main)
    def _():
        hello(r, home)

    for n in range(2):

        @pl.when(r != 2 * c + n)
        def _():
            hello(2 * c + n, c)

    def one(flag):
        return jnp.where(flag, 1, 0)

    greetings = (
        one(is_main) * (N_COL - 1 + N_ROW - 1)
        + one(not_main)
        + one(to_next)
        + one(to_prev)
    )

    @pl.when(is_main)
    def _():
        weights[1].start()
        own_atoms.start()
        weights[0].start()
        for k in range(2):
            side_pair_copy(k).start()
        for k in range(steps):
            own_copy(k).start()
        for w in weights[2:]:
            w.start()

    @pl.when(not_main)
    def _():
        @pl.when(is_helper)
        def _():
            weights[0].start()
            for k in range(2):
                side_pair_copy(k).start()

        for w in receiver_weights:
            w.start()

    def atom_copy(col):
        return pltpu.make_async_remote_copy(
            src_ref=mine_in,
            dst_ref=atoms.at[pl.ds(MARGIN + col * OWN, OWN)],
            send_sem=send_sem.at[0],
            recv_sem=recv_sem.at[col],
            device_id=(r, home),
            device_id_type=MESH,
        )

    def edge_copy(forward, row):
        start = OWN - MARGIN if forward else 0
        return pltpu.make_async_remote_copy(
            src_ref=mine_in.at[pl.ds(start, MARGIN)],
            dst_ref=atoms.at[pl.ds(0 if forward else MARGIN + ATOMS, MARGIN)],
            send_sem=send_sem.at[1 if forward else 2],
            recv_sem=recv_sem.at[N_COL + (0 if forward else 1)],
            device_id=(row, row // 2),
            device_id_type=MESH,
        )

    def side_copy():
        return pltpu.make_async_remote_copy(
            src_ref=side,
            dst_ref=side_in,
            send_sem=send_sem.at[3],
            recv_sem=recv_sem.at[N_COL + 2],
            device_id=(r, home),
            device_id_type=MESH,
        )


    lane = iota((8, TOK), 1)
    sub = iota((8, TOK), 0)
    block_of = lane // 8
    on_diag = lax.rem(lane, 8) == sub

    def bias_weights():
        w = wb[...]
        w = w - jnp.mean(w, -1, keepdims=True)
        high = w.astype(BF16)
        rest = w - high.astype(F32)
        mid = rest.astype(BF16)
        low = (rest - mid.astype(F32)).astype(BF16)
        ones = jnp.ones((1, CH), BF16)
        zeros = jnp.zeros((12, CH), BF16)
        return jnp.concatenate(
            [high, ones, zeros[:3], mid, zeros[:4], low, zeros], axis=0
        )

    def moments(x, i, first, w32):
        t = nt(jnp.concatenate([w32, x], axis=0), x)
        d = jnp.zeros((8, TOK), F32)
        for k in range(TOK // 8):
            d = jnp.where(block_of == k, t[32 + 8 * k : 40 + 8 * k], d)
        rows = pl.ds(pl.multiple_of(first + i * 8, 8), 8)
        stat[rows, :] = t[0:8] + t[8:16] + t[16:24]
        diag[rows, :] = jnp.where(on_diag, d, 0.0)

    def side_moments(w32):
        for k in range(2):
            side_pair_copy(k).wait()

        @pl.loop(0, HALF, unroll=SIDE_UNROLL)
        def _(i):
            moments(side_pair[i], i, 8 * TOK, w32)

    def head_bias(first, count):
        def part(ref, s):
            return ref[pl.ds(first + s, count, stride=8), :]

        s1 = part(stat, 4)
        s2 = part(diag, 0)
        for s in range(1, 8):
            s2 = s2 + part(diag, s)
        near = (s1 * (1 / CH)).astype(BF16).astype(F32)
        offset = s1 * (1 / CH) - near
        moment = (s2 - 2 * near * s1) + CH * (near * near)
        spread = jnp.maximum(moment * (1 / CH) - offset * offset, 0.0)
        scale = lax.rsqrt(spread + 1e-05)
        return [part(stat, h) * scale for h in range(HEADS)]

    def transition(x):
        residual = x.astype(F32)
        second = layer_norm(residual).astype(BF16)
        doubled = mm(second, wi[...])
        swish = doubled[:, 0 : 2 * CH]
        hidden = swish * (0.5 + 0.5 * jnp.tanh(0.5 * swish)) * doubled[:, 2 * CH :]
        return (residual + mm(hidden.astype(BF16), wt[...])).astype(BF16)

    @pl.when(is_helper)
    def _():
        weights[0].wait()
        side_moments(bias_weights())
        for h, value in enumerate(head_bias(8 * TOK, HALF)):
            side[h] = value

    @pl.when(not_main)
    def _():
        mine.wait()
        pl.semaphore_wait(barrier, greetings)
        atom_copy(c).start()

    @pl.when(to_next & not_main)
    def _():
        edge_copy(True, r + 1).start()

    @pl.when(to_prev & not_main)
    def _():
        edge_copy(False, r - 1).start()

    @pl.when(is_helper)
    def _():
        side_copy().start()
        side_copy().wait_send()

    def send(src, dst, slot, recv, row, col):
        return pltpu.make_async_remote_copy(
            src_ref=src,
            dst_ref=dst,
            send_sem=send_sem.at[slot],
            recv_sem=recv_sem.at[recv],
            device_id=(row, col),
            device_id_type=MESH,
        )

    base = N_COL + 3

    def resid_send(p):
        col = (partner, row_peers[5], row_peers[6], row_peers[3])[p]
        count = OWN if p == 0 else 2 * OWN
        first = col if p == 0 else col // 2 * 2
        return send(
            resid.at[pl.ds(pl.multiple_of(first * OWN, OWN), count)],
            resid_in.at[pl.ds(0, count)],
            4 + p,
            base,
            r,
            col,
        )

    def atom_pass():
        return send(
            resid_in.at[pl.ds(pl.multiple_of((1 - x_hi) * OWN, OWN), OWN)],
            atom_out,
            8,
            base + 6,
            r,
            partner,
        )

    def single_send(p, k):
        piece = single_out.at[k]
        col = (row_peers[5], row_peers[6], partner, row_peers[3])[p]
        return send(piece, piece, 12 + 4 * k + p, base + (1, 4, 5)[k], r, col)

    tree = (
        (is_main, (0, 1, 2)),
        (home_side & (ahead_of_home == 1), (0, 2)),
        (home_side & (ahead_of_home == 3), (2,)),
        (across & (ahead_of_home == 0), (3,)),
    )

    own_half = col_out.at[pl.ds(pl.multiple_of(odd * TOK, TOK), TOK)]

    def col_send(p):
        return send(own_half, own_half, 24 + p, base + 2, col_peers[p], c)

    def col_forward():
        return send(own_half, own_half, 31, base + 3, sibling, c)

    @pl.when(is_main)
    def _():
        weights[1].wait()
        own_counts = counts[pl.ds(r, 1), :].astype(F32)
        prev_counts = counts[pl.ds(jnp.maximum(r - 1, 0), 1), :].astype(F32)
        next_counts = counts[pl.ds(jnp.minimum(r + 1, N_ROW - 1), 1), :].astype(F32)
        stacked = jnp.concatenate(
            [own_counts, prev_counts, next_counts, jnp.zeros((5, TOK), F32)], axis=0
        )
        upper = (iota((TOK, TOK), 0) <= iota((TOK, TOK), 1)).astype(F32).astype(BF16)
        lower = (iota((TOK, TOK), 0) >= iota((TOK, TOK), 1)).astype(F32).astype(BF16)
        stacked_low = stacked.astype(BF16)
        ends = mm(stacked_low, upper)
        starts = ends - stacked
        ends_column = nt(lower, stacked_low)[:, 0:1]
        eye = (iota((TOK, TOK), 0) == iota((TOK, TOK), 1)).astype(F32).astype(BF16)
        counts_column = nt(eye, stacked_low)[:, 0:1]
        starts_column = ends_column - counts_column
        far = 1e9
        one_lane = iota((1, TOK), 1)
        after = one_lane < SPLIT
        side_from = jnp.where(
            after,
            jnp.where(has_next, starts[2:3] + ATOMS, far),
            jnp.where(has_prev, starts[1:2] - ATOMS, far),
        )
        side_to = jnp.where(
            after,
            jnp.where(has_next, ends[2:3] + ATOMS, far),
            jnp.where(has_prev, ends[1:2] - ATOMS, far),
        )
        masked = one_lane == MASK_LANE
        low_mask = jnp.where(has_prev, far, -float(MARGIN))
        mask_from = jnp.where(has_next, low_mask, float(ATOMS))
        mask_to = jnp.where(
            has_next, jnp.where(has_prev, far, 0.0), float(ATOMS + MARGIN)
        )
        side_from = jnp.where(masked, mask_from, side_from)
        side_to = jnp.where(masked, mask_to, side_to)

        def onehot(first, count, lo, hi):
            at = (iota((count, TOK), 0) + first).astype(F32)
            return jnp.where((at >= lo) & (at < hi), 1.0, 0.0).astype(BF16)

        rhs[:, CH : CH + TOK] = onehot(-MARGIN, EXT, starts[0:1], ends[0:1])
        for first in (0, ATOMS - 2 * MARGIN + WIN):
            rhs[first : first + KEYS + WIN, CH + TOK :] = onehot(
                first - MARGIN, KEYS + WIN, side_from, side_to
            )
        vals[:, CH:] = jnp.ones((EXT, CH), BF16)
        at = iota((TOK, ATOMS), 1).astype(F32)
        member[...] = jnp.where(
            (at >= starts_column) & (at < ends_column), 1.0, 0.0
        ).astype(BF16)

        weights[0].wait()
        w32 = bias_weights()
        side_moments(w32)

        @pl.loop(0, TOK // OWN_UNROLL)
        def _(k):
            for u in range(OWN_UNROLL // STEP):
                own_copy(k * (OWN_UNROLL // STEP) + u).wait()
            for u in range(OWN_UNROLL):
                i = k * OWN_UNROLL + u
                moments(own_pair[i], i, 0, w32)

        for w in weights[2:]:
            w.wait()
        mine.wait()
        pl.semaphore_wait(barrier, greetings)

        @pl.when(to_next)
        def _():
            edge_copy(True, r + 1).start()

        @pl.when(to_prev)
        def _():
            edge_copy(False, r - 1).start()

        own_atoms.wait()
        near_first = row_peers[::-1]
        for col in near_first[:EARLY]:
            atom_copy(col).wait_recv()
        own_bias = [value.astype(BF16) for value in head_bias(0, TOK)]
        main_side = head_bias(8 * TOK, HALF)
        for h in range(HEADS):
            for k in range(ATOMS // 256):
                first = k * 256
                rows = mm(
                    rhs[MARGIN + first : MARGIN + first + 256, CH : CH + TOK], own_bias[h]
                ).astype(BF16)
                for w in range(256 // WIN):
                    start = (first + w * WIN) * HEADS + h * WIN
                    picked[start : start + WIN, :] = rows[w * WIN : (w + 1) * WIN]

        def keys_values(start, count):
            span = pl.ds(start, count)
            norm = layer_norm(atoms[span, :].astype(F32)).astype(BF16)
            projected = mm(norm, wp[...])
            rhs[span, 0:CH] = projected[:, CH : 2 * CH].astype(BF16)
            vals[span, 0:CH] = projected[:, 2 * CH : 3 * CH].astype(BF16)
            return projected

        def project(col):
            projected = keys_values(pl.multiple_of(MARGIN + col * OWN, 16), OWN)
            span = pl.ds(pl.multiple_of(col * OWN, OWN), OWN)
            gate[span, :] = 0.5 + 0.5 * jnp.tanh(0.5 * projected[:, 3 * CH :])
            queries[span, :] = (projected[:, 0:CH] * (CH // HEADS) ** -0.5).astype(BF16)

        for col in [c] + near_first[:EARLY]:
            project(col)

        @pl.when(has_helper)
        def _():
            side_copy().wait_recv()

        @pl.when(jnp.logical_not(has_helper))
        def _():
            side_in[...] = jnp.zeros(side_in.shape, F32)

        low_lanes = iota((HALF, TOK), 1) < SPLIT
        mask_lane = iota((TOK, TOK), 1) == MASK_LANE
        for h in range(HEADS):
            theirs = side_in[h]
            ahead = jnp.where(on_main_next, main_side[h], theirs)
            behind = jnp.where(on_main_next, theirs, main_side[h])
            ahead_rolled = pltpu.roll(ahead, SPLIT, 1)
            behind_rolled = pltpu.roll(behind, SPLIT, 1)
            none = jnp.zeros((HALF, TOK), F32)
            gap = TOK - REACH - HALF
            upper_rows = jnp.concatenate([none, none[:gap], ahead, ahead_rolled], axis=0)
            lower_rows = jnp.concatenate([behind_rolled, behind, none, none[:gap]], axis=0)
            both = jnp.where(iota((TOK, TOK), 1) < SPLIT, upper_rows, lower_rows)
            both = jnp.where(mask_lane, -1e30, both).astype(BF16)
            for k, first in enumerate((0, ATOMS - 2 * WIN)):
                rows = mm(
                    rhs[MARGIN + first : MARGIN + first + 2 * WIN, CH : CH + TOK], both
                ).astype(BF16)
                for w in range(2):
                    start = ((2 * k + w) * HEADS + h) * WIN
                    picked_side[start : start + WIN, :] = rows[w * WIN : (w + 1) * WIN]

        for col in near_first[EARLY:]:
            atom_copy(col).wait_recv()

        @pl.when(has_prev)
        def _():
            edge_copy(True, r).wait_recv()

        @pl.when(jnp.logical_not(has_prev))
        def _():
            atoms[0:MARGIN, :] = jnp.zeros((MARGIN, CH), BF16)

        @pl.when(has_next)
        def _():
            edge_copy(False, r).wait_recv()

        @pl.when(jnp.logical_not(has_next))
        def _():
            atoms[MARGIN + ATOMS :, :] = jnp.zeros((MARGIN, CH), BF16)

        for col in near_first[EARLY:]:
            project(col)
        keys_values(0, MARGIN)
        keys_values(MARGIN + ATOMS, MARGIN)

        head_of = iota((WIN, CH), 1) // (CH // HEADS)

        def attend(q, bias, keys, extra, values, opened):
            split = [jnp.where(head_of == h, q, jnp.zeros_like(q)) for h in range(HEADS)]
            parts = [jnp.concatenate(split, axis=0), bias]
            if extra is not None:
                parts.append(extra)
            scores = nt(jnp.concatenate(parts, axis=1), keys)
            top = jnp.max(scores, -1, keepdims=True)
            weight = jnp.exp(scores - top).astype(BF16)
            total = mm(weight, values)
            above = total[0:WIN, 0:CH]
            below = total[0:WIN, CH:]
            for h in range(1, HEADS):
                here = head_of == h
                above = jnp.where(here, total[h * WIN : (h + 1) * WIN, 0:CH], above)
                below = jnp.where(here, total[h * WIN : (h + 1) * WIN, CH:], below)
            return (above * opened / below).astype(BF16)

        for n, w in enumerate(EDGES):
            span = slice(w * WIN, (w + 1) * WIN)
            keys = slice(w * WIN, w * WIN + KEYS)
            block = slice(w * WIN * HEADS, (w + 1) * WIN * HEADS)
            gated[span, :] = attend(
                queries[span, :],
                picked[block, :],
                rhs[keys, :],
                picked_side[n * WIN * HEADS : (n + 1) * WIN * HEADS, :],
                vals[keys, :],
                gate[span, :],
            )

        @pl.loop(2, ATOMS // WIN - 2, unroll=ATTEND_UNROLL)
        def _(w):
            start = pl.multiple_of(w * WIN, WIN)
            span = pl.ds(start, WIN)
            keys = pl.ds(start, KEYS)
            block = pl.ds(pl.multiple_of(w * WIN * HEADS, WIN * HEADS), WIN * HEADS)
            gated[span, :] = attend(
                queries[span, :],
                picked[block, :],
                rhs[keys, 0 : CH + TOK],
                None,
                vals[keys, :],
                gate[span, :],
            )

        for k in range(ATOMS // 256):
            span = slice(k * 256, (k + 1) * 256)
            ext = slice(MARGIN + k * 256, MARGIN + (k + 1) * 256)
            resid[span, :] = (atoms[ext, :].astype(F32) + mm(gated[span, :], wo[...])).astype(BF16)
        for p in range(4):
            resid_send(p).start()
        for k in range(ATOMS // PART):
            span = slice(k * PART, (k + 1) * PART)
            final[span, :] = transition(resid[span, :])
        terms = jnp.zeros((TOK, CH), F32)
        for q in range(3):
            part = slice(q * CH, (q + 1) * CH)
            for k in range(ATOMS // 256):
                span = slice(k * 256, (k + 1) * 256)
                emitted[span, part] = jnp.maximum(mm(final[span, :], wk[:, part]), 0.0).astype(BF16)
            totals = mm(member[...], emitted[:, part])
            single = (totals / counts_column).astype(BF16)
            single_out[q] = single
            for p in tree[0][1]:
                single_send(p, q).start()
            terms = terms + mm(single, wc[part, :])
        col_out[pl.ds(pl.multiple_of(odd * TOK, TOK), TOK), :] = terms.astype(BF16)
        for p in range(7):
            col_send(p).start()
        resid_in[0:OWN, :] = resid[pl.ds(pl.multiple_of(c * OWN, OWN), OWN), :]

    @pl.when(not_main)
    def _():
        for w in receiver_weights:
            w.wait()

    @pl.when(passes_atoms)
    def _():
        resid_send(1).wait_recv()
        resid_in[...] = transition(resid_in[...])
        atom_pass().start()
        atom_out[...] = resid_in[pl.ds(pl.multiple_of(x_hi * OWN, OWN), OWN), :]

    @pl.when(across & (ahead_of_home == 0))
    def _():
        resid_send(0).wait_recv()

    @pl.when(ahead_of_home == 0)
    def _():
        atom_out[...] = transition(resid_in[0:OWN, :])

    for role, copies in tree[1:]:

        @pl.when(role)
        def _():
            for k in range(3):
                single_send(0, k).wait_recv()
                for p in copies:
                    single_send(p, k).start()

    @pl.when(not_main)
    def _():
        col_send(0).wait_recv()

    col_forward().start()

    @pl.when(not_main & jnp.logical_not(relays))
    def _():
        for k in range(3):
            single_send(0, k).wait_recv()

    row_out[...] = sum(mm(single_out[q], wr[q * CH : (q + 1) * CH, :]) for q in range(3))
    col_forward().wait_recv()
    col_forward().wait_send()

    @pl.when(passes_atoms)
    def _():
        atom_pass().wait_send()

    @pl.when(across & (ahead_of_home != 0))
    def _():
        atom_pass().wait_recv()

    @pl.when(is_main)
    def _():
        for p in range(4):
            resid_send(p).wait_send()
        for p in range(7):
            col_send(p).wait_send()

    for role, copies in tree:

        @pl.when(role)
        def _():
            for k in range(3):
                for p in copies:
                    single_send(p, k).wait_send()

    @pl.when(not_main)
    def _():
        atom_copy(c).wait_send()

    @pl.when(to_next)
    def _():
        edge_copy(True, r + 1).wait_send()

    @pl.when(to_prev)
    def _():
        edge_copy(False, r - 1).wait_send()


def update_kernel(pair, row, col, atom, single, new_pair, atom_out, single_out, result, sem):
    small = [
        pltpu.make_async_copy(atom, atom_out, sem.at[0]),
    ] + [
        pltpu.make_async_copy(single.at[q], single_out.at[:, pl.ds(q * CH, CH)], sem.at[1 + q])
        for q in range(3)
    ]
    for copy in small:
        copy.start()
    width = col.shape[0]
    column = col[...]

    def out_copy(k):
        rows = pl.ds(k * BLOCK, BLOCK)
        return pltpu.make_async_copy(result.at[rows], new_pair.at[rows], sem.at[4 + k])

    @pl.loop(0, TOK // BLOCK)
    def _(k):
        terms = row[pl.ds(pl.multiple_of(k * BLOCK, BLOCK), BLOCK), :]
        for u in range(BLOCK):
            term = jnp.broadcast_to(terms[u : u + 1], (16, CH)).astype(BF16)
            term = jnp.concatenate([term] * (width // 16), axis=0)
            i = k * BLOCK + u
            result[i] = pair[i] + (column + term)
        out_copy(k).start()

    for copy in small:
        copy.wait()
    for k in range(TOK // BLOCK):
        out_copy(k).wait()


def shards(
    pair, counts, atom_single, w_bias, w_project, w_out, w_trans_in, w_trans_out, w_token, w_row, w_col
):
    any_ = pl.BlockSpec(memory_space=pl.ANY)
    vmem = pltpu.VMEM
    in_hbm = lambda a: pltpu.with_memory_space_constraint(a, pltpu.HBM)
    weights = (w_bias.T, w_project, w_out, w_trans_in, w_trans_out, w_token, w_row, w_col)
    in_vmem = pl.BlockSpec(memory_space=vmem)
    atom, single, row, col = pl.pallas_call(
        exchange_kernel,
        out_shape=(
            jax.ShapeDtypeStruct((OWN, CH), BF16),
            jax.ShapeDtypeStruct((3, TOK, CH), BF16),
            jax.ShapeDtypeStruct((TOK, CH), F32),
            jax.ShapeDtypeStruct((2 * TOK, CH), BF16),
        ),
        in_specs=[any_] * (3 + len(weights)),
        out_specs=(in_vmem,) * 4,
        scratch_shapes=[
            vmem((TOK, TOK, CH), BF16),
            vmem((HALF, TOK, CH), BF16),
            vmem(counts.shape, jnp.int32),
            *[vmem(w.shape, w.dtype) for w in weights],
            vmem((8 * (TOK + HALF), TOK), F32),
            vmem((8 * (TOK + HALF), TOK), F32),
            vmem((HEADS, HALF, TOK), F32),
            vmem((HEADS, HALF, TOK), F32),
            vmem((EXT, CH), BF16),
            vmem((ATOMS, CH), BF16),
            vmem((ATOMS * HEADS, TOK), BF16),
            vmem((len(EDGES) * WIN * HEADS, TOK), BF16),
            vmem((EXT, CH + 2 * TOK), BF16),
            vmem((EXT, 2 * CH), BF16),
            vmem((ATOMS, CH), F32),
            vmem((ATOMS, CH), BF16),
            vmem((ATOMS, CH), BF16),
            vmem((2 * OWN, CH), BF16),
            vmem((OWN, CH), BF16),
            vmem((ATOMS, CH), BF16),
            vmem((ATOMS, 3 * CH), BF16),
            vmem((TOK, ATOMS), BF16),
            pltpu.SemaphoreType.DMA((TOK // STEP,)),
            pltpu.SemaphoreType.DMA((2,)),
            pltpu.SemaphoreType.DMA((1 + len(weights),)),
            pltpu.SemaphoreType.DMA((2,)),
            pltpu.SemaphoreType.DMA((32,)),
            pltpu.SemaphoreType.DMA((N_COL + 10,)),
        ],
        compiler_params=pltpu.CompilerParams(
            collective_id=0, has_side_effects=True, vmem_limit_bytes=40 * 2**20
        ),
    )(*[in_hbm(a) for a in (pair, atom_single, counts, *weights)])
    new_pair, atom_out, token_single = pl.pallas_call(
        update_kernel,
        out_shape=(
            jax.ShapeDtypeStruct(pair.shape, BF16),
            jax.ShapeDtypeStruct(atom.shape, BF16),
            jax.ShapeDtypeStruct((TOK, 3 * CH), BF16),
        ),
        in_specs=[in_vmem] * 5,
        out_specs=(any_,) * 3,
        scratch_shapes=[
            vmem(pair.shape, BF16),
            pltpu.SemaphoreType.DMA((4 + TOK // BLOCK,)),
        ],
        compiler_params=pltpu.CompilerParams(vmem_limit_bytes=UPDATE_VMEM * 2**20),
    )(pltpu.with_memory_space_constraint(pair, pltpu.VMEM), row, col, atom, single)
    return atom_out, token_single, new_pair


def solution(mesh):
    return jax.shard_map(
        shards,
        mesh=mesh,
        in_specs=(P("row", "col", None), P(), P(("row", "col"), None)) + (P(),) * 8,
        out_specs=(P(("row", "col"), None), P("row", None), P("row", "col", None)),
        check_vma=False,
    )
```

```python
import functools

import jax
import jax.numpy as jnp
from jax import lax
from jax.experimental import pallas as pl
from jax.experimental.pallas import tpu as pltpu
from jax.sharding import PartitionSpec as P

MESH = pl.DeviceIdType.MESH
F32 = jnp.float32
BF16 = jnp.bfloat16
N_ROW, N_COL = 16, 8
TOK = 128
CH = 128
HEADS = 4
WIN = 32
KEYS = 128
ATOMS = 1024
MARGIN = (KEYS - WIN) // 2
EXT = ATOMS + 2 * MARGIN
OWN = ATOMS // N_COL
STEP = 16
BLOCK = 8
UPDATE_VMEM = 20
REACH = 80
HALF = REACH // 2
EARLY = 4
EDGES = (0, 1, 30, 31)
MASK_LANE = 56
ATTEND_UNROLL = 28
OWN_UNROLL = 64
SIDE_UNROLL = 40
PART = 256
SPLIT = 64


def nt(a, b):
    return lax.dot_general(a, b, (((1,), (1,)), ((), ())), preferred_element_type=F32)


def mm(a, b):
    return jnp.dot(a, b, preferred_element_type=F32)


def layer_norm(x):
    average = jnp.mean(x, -1, keepdims=True)
    centred = x - average
    spread = jnp.mean(centred * centred, -1, keepdims=True)
    return centred * lax.rsqrt(spread + 1e-05)


def iota(shape, axis):
    return lax.broadcasted_iota(jnp.int32, shape, axis)


def exchange_kernel(
    pair_hbm,
    atom_hbm,
    counts_hbm,
    wb_hbm,
    wp_hbm,
    wo_hbm,
    wi_hbm,
    wt_hbm,
    wk_hbm,
    wr_hbm,
    wc_hbm,
    atom_out,
    single_out,
    row_out,
    col_out,
    own_pair,
    side_pair,
    counts,
    wb,
    wp,
    wo,
    wi,
    wt,
    wk,
    wr,
    wc,
    stat,
    diag,
    side,
    side_in,
    atoms,
    queries,
    picked,
    picked_side,
    rhs,
    vals,
    gate,
    gated,
    resid,
    resid_in,
    mine_in,
    final,
    emitted,
    member,
    own_sem,
    side_pair_sem,
    w_sem,
    local_sem,
    send_sem,
    recv_sem,
):
    r, c = lax.axis_index("row"), lax.axis_index("col")
    odd = lax.rem(r, 2)
    home = r // 2
    is_main = c == home
    not_main = jnp.logical_not(is_main)
    helper_col = home - 1 + 2 * odd
    has_helper = (helper_col >= 0) & (helper_col < N_COL)
    is_helper = c == helper_col
    has_prev, has_next = r > 0, r < N_ROW - 1
    z, x_hi = c // 2, lax.rem(c, 2)
    y, x_lo = r // 4, lax.rem(r // 2, 2)
    sibling = r + 1 - 2 * odd
    partner = c + 1 - 2 * x_hi
    home_side = x_hi == x_lo
    row_peers = [
        (lax.rem(z + dz, 4) * 2 + (1 - x_hi if dx else x_hi))
        for dz, dx in ((2, 1), (1, 1), (3, 1), (2, 0), (0, 1), (1, 0), (3, 0))
    ]
    col_peers = [
        (lax.rem(y + dy, 4) * 2 + (1 - x_lo if dx else x_lo)) * 2 + odd
        for dy, dx in ((2, 1), (1, 1), (3, 1), (2, 0), (1, 0), (3, 0), (0, 1))
    ]
    own_start = pl.multiple_of(odd * TOK, TOK)
    on_main_next = odd == 0
    side_is_next = on_main_next == is_main
    side_rows = jnp.where(side_is_next, TOK - REACH, 0)
    side_start = pl.multiple_of((1 - odd) * TOK + jnp.where(side_is_next, 0, SPLIT), SPLIT)

    def own_copy(k):
        rows = pl.ds(k * STEP, STEP)
        return pltpu.make_async_copy(
            pair_hbm.at[rows, pl.ds(own_start, TOK)], own_pair.at[rows], own_sem.at[k]
        )

    def side_pair_copy(k):
        return pltpu.make_async_copy(
            pair_hbm.at[pl.ds(side_rows + k * HALF, HALF), pl.ds(side_start, SPLIT)],
            side_pair.at[:, pl.ds(k * SPLIT, SPLIT)],
            side_pair_sem.at[k],
        )

    weights = [
        pltpu.make_async_copy(a, b, w_sem.at[i])
        for i, (a, b) in enumerate(
            [
                (wb_hbm, wb),
                (counts_hbm, counts),
                (wp_hbm, wp),
                (wo_hbm, wo),
                (wi_hbm, wi),
                (wt_hbm, wt),
                (wk_hbm, wk),
                (wr_hbm, wr),
                (wc_hbm, wc),
            ]
        )
    ]
    receiver_weights = [weights[4], weights[5], weights[7]]
    steps = TOK // STEP

    own_atoms = pltpu.make_async_copy(
        atom_hbm, atoms.at[pl.ds(MARGIN + c * OWN, OWN)], local_sem.at[0]
    )
    mine = pltpu.make_async_copy(atom_hbm, mine_in, local_sem.at[1])
    mine.start()
    barrier = pltpu.get_barrier_semaphore()

    def hello(row, col):
        pl.semaphore_signal(barrier, inc=1, device_id=(row, col), device_id_type=MESH)

    to_next = (c == N_COL - 1) & has_next
    to_prev = (c == 0) & has_prev

    across = jnp.logical_not(home_side)
    ahead_of_home = lax.rem(z - y + 4, 4)
    relays = not_main & ((home_side & (ahead_of_home != 2)) | (across & (ahead_of_home == 0)))
    passes_atoms = not_main & home_side
    @pl.when(is_main)
    def _():
        for col in row_peers:
            hello(r, col)

        @pl.when(has_prev)
        def _():
            hello(r - 1, N_COL - 1)

        @pl.when(has_next)
        def _():
            hello(r + 1, 0)

    @pl.when(not_main)
    def _():
        hello(r, home)

    for n in range(2):

        @pl.when(r != 2 * c + n)
        def _():
            hello(2 * c + n, c)

    def one(flag):
        return jnp.where(flag, 1, 0)

    greetings = (
        one(is_main) * (N_COL - 1 + N_ROW - 1)
        + one(not_main)
        + one(to_next)
        + one(to_prev)
    )

    @pl.when(is_main)
    def _():
        weights[1].start()
        own_atoms.start()
        weights[0].start()
        for k in range(2):
            side_pair_copy(k).start()
        for k in range(steps):
            own_copy(k).start()
        for w in weights[2:]:
            w.start()

    @pl.when(not_main)
    def _():
        @pl.when(is_helper)
        def _():
            weights[0].start()
            for k in range(2):
                side_pair_copy(k).start()

        for w in receiver_weights:
            w.start()

    def atom_copy(col):
        return pltpu.make_async_remote_copy(
            src_ref=mine_in,
            dst_ref=atoms.at[pl.ds(MARGIN + col * OWN, OWN)],
            send_sem=send_sem.at[0],
            recv_sem=recv_sem.at[col],
            device_id=(r, home),
            device_id_type=MESH,
        )

    def edge_copy(forward, row):
        start = OWN - MARGIN if forward else 0
        return pltpu.make_async_remote_copy(
            src_ref=mine_in.at[pl.ds(start, MARGIN)],
            dst_ref=atoms.at[pl.ds(0 if forward else MARGIN + ATOMS, MARGIN)],
            send_sem=send_sem.at[1 if forward else 2],
            recv_sem=recv_sem.at[N_COL + (0 if forward else 1)],
            device_id=(row, row // 2),
            device_id_type=MESH,
        )

    def side_copy():
        return pltpu.make_async_remote_copy(
            src_ref=side,
            dst_ref=side_in,
            send_sem=send_sem.at[3],
            recv_sem=recv_sem.at[N_COL + 2],
            device_id=(r, home),
            device_id_type=MESH,
        )


    lane = iota((8, TOK), 1)
    sub = iota((8, TOK), 0)
    block_of = lane // 8
    on_diag = lax.rem(lane, 8) == sub

    def bias_weights():
        w = wb[...]
        w = w - jnp.mean(w, -1, keepdims=True)
        high = w.astype(BF16)
        rest = w - high.astype(F32)
        mid = rest.astype(BF16)
        low = (rest - mid.astype(F32)).astype(BF16)
        ones = jnp.ones((1, CH), BF16)
        zeros = jnp.zeros((12, CH), BF16)
        return jnp.concatenate(
            [high, ones, zeros[:3], mid, zeros[:4], low, zeros], axis=0
        )

    def moments(x, i, first, w32):
        t = nt(jnp.concatenate([w32, x], axis=0), x)
        d = jnp.zeros((8, TOK), F32)
        for k in range(TOK // 8):
            d = jnp.where(block_of == k, t[32 + 8 * k : 40 + 8 * k], d)
        rows = pl.ds(pl.multiple_of(first + i * 8, 8), 8)
        stat[rows, :] = t[0:8] + t[8:16] + t[16:24]
        diag[rows, :] = jnp.where(on_diag, d, 0.0)

    def side_moments(w32):
        for k in range(2):
            side_pair_copy(k).wait()

        @pl.loop(0, HALF, unroll=SIDE_UNROLL)
        def _(i):
            moments(side_pair[i], i, 8 * TOK, w32)

    def head_bias(first, count):
        def part(ref, s):
            return ref[pl.ds(first + s, count, stride=8), :]

        s1 = part(stat, 4)
        s2 = part(diag, 0)
        for s in range(1, 8):
            s2 = s2 + part(diag, s)
        near = (s1 * (1 / CH)).astype(BF16).astype(F32)
        offset = s1 * (1 / CH) - near
        moment = (s2 - 2 * near * s1) + CH * (near * near)
        spread = jnp.maximum(moment * (1 / CH) - offset * offset, 0.0)
        scale = lax.rsqrt(spread + 1e-05)
        return [part(stat, h) * scale for h in range(HEADS)]

    def transition(x):
        residual = x.astype(F32)
        second = layer_norm(residual).astype(BF16)
        doubled = mm(second, wi[...])
        swish = doubled[:, 0 : 2 * CH]
        hidden = swish * (0.5 + 0.5 * jnp.tanh(0.5 * swish)) * doubled[:, 2 * CH :]
        return (residual + mm(hidden.astype(BF16), wt[...])).astype(BF16)

    @pl.when(not_main)
    def _():
        mine.wait()
        pl.semaphore_wait(barrier, greetings)
        atom_copy(c).start()

    @pl.when(to_next & not_main)
    def _():
        edge_copy(True, r + 1).start()

    @pl.when(to_prev & not_main)
    def _():
        edge_copy(False, r - 1).start()

    @pl.when(is_helper)
    def _():
        weights[0].wait()
        side_moments(bias_weights())
        side[...] = jnp.concatenate(head_bias(8 * TOK, HALF), axis=0).astype(BF16)

    @pl.when(is_helper)
    def _():
        side_copy().start()
        side_copy().wait_send()

    def send(src, dst, slot, recv, row, col):
        return pltpu.make_async_remote_copy(
            src_ref=src,
            dst_ref=dst,
            send_sem=send_sem.at[slot],
            recv_sem=recv_sem.at[recv],
            device_id=(row, col),
            device_id_type=MESH,
        )

    base = N_COL + 3

    def resid_send(p):
        col = (partner, row_peers[5], row_peers[6], row_peers[3])[p]
        count = OWN if p == 0 else 2 * OWN
        first = col if p == 0 else col // 2 * 2
        return send(
            resid.at[pl.ds(pl.multiple_of(first * OWN, OWN), count)],
            resid_in.at[pl.ds(0, count)],
            4 + p,
            base,
            r,
            col,
        )

    def atom_pass():
        return send(
            resid_in.at[pl.ds(pl.multiple_of((1 - x_hi) * OWN, OWN), OWN)],
            atom_out,
            8,
            base + 6,
            r,
            partner,
        )

    def single_send(p, k):
        piece = single_out.at[k]
        col = (row_peers[5], row_peers[6], partner, row_peers[3])[p]
        return send(piece, piece, 12 + 4 * k + p, base + (1, 4, 5)[k], r, col)

    tree = (
        (is_main, (0, 1, 2)),
        (home_side & (ahead_of_home == 1), (0, 2)),
        (home_side & (ahead_of_home == 3), (2,)),
        (across & (ahead_of_home == 0), (3,)),
    )

    own_half = col_out.at[pl.ds(pl.multiple_of(odd * TOK, TOK), TOK)]

    def col_send(p):
        return send(own_half, own_half, 24 + p, base + 2, col_peers[p], c)

    def col_forward():
        return send(own_half, own_half, 31, base + 3, sibling, c)

    @pl.when(is_main)
    def _():
        weights[1].wait()
        own_counts = counts[pl.ds(r, 1), :].astype(F32)
        prev_counts = counts[pl.ds(jnp.maximum(r - 1, 0), 1), :].astype(F32)
        next_counts = counts[pl.ds(jnp.minimum(r + 1, N_ROW - 1), 1), :].astype(F32)
        stacked = jnp.concatenate(
            [own_counts, prev_counts, next_counts, jnp.zeros((5, TOK), F32)], axis=0
        )
        upper = (iota((TOK, TOK), 0) <= iota((TOK, TOK), 1)).astype(F32).astype(BF16)
        lower = (iota((TOK, TOK), 0) >= iota((TOK, TOK), 1)).astype(F32).astype(BF16)
        stacked_low = stacked.astype(BF16)
        ends = mm(stacked_low, upper)
        starts = ends - stacked
        ends_column = nt(lower, stacked_low)[:, 0:1]
        eye = (iota((TOK, TOK), 0) == iota((TOK, TOK), 1)).astype(F32).astype(BF16)
        counts_column = nt(eye, stacked_low)[:, 0:1]
        starts_column = ends_column - counts_column
        far = 1e9
        one_lane = iota((1, TOK), 1)
        after = one_lane < SPLIT
        side_from = jnp.where(
            after,
            jnp.where(has_next, starts[2:3] + ATOMS, far),
            jnp.where(has_prev, starts[1:2] - ATOMS, far),
        )
        side_to = jnp.where(
            after,
            jnp.where(has_next, ends[2:3] + ATOMS, far),
            jnp.where(has_prev, ends[1:2] - ATOMS, far),
        )
        masked = one_lane == MASK_LANE
        low_mask = jnp.where(has_prev, far, -float(MARGIN))
        mask_from = jnp.where(has_next, low_mask, float(ATOMS))
        mask_to = jnp.where(
            has_next, jnp.where(has_prev, far, 0.0), float(ATOMS + MARGIN)
        )
        side_from = jnp.where(masked, mask_from, side_from)
        side_to = jnp.where(masked, mask_to, side_to)

        def onehot(first, count, lo, hi):
            at = (iota((count, TOK), 0) + first).astype(F32)
            return jnp.where((at >= lo) & (at < hi), 1.0, 0.0).astype(BF16)

        rhs[:, CH : CH + TOK] = onehot(-MARGIN, EXT, starts[0:1], ends[0:1])
        for first in (0, ATOMS - 2 * MARGIN + WIN):
            rhs[first : first + KEYS + WIN, CH + TOK :] = onehot(
                first - MARGIN, KEYS + WIN, side_from, side_to
            )
        vals[:, CH:] = jnp.ones((EXT, CH), BF16)
        at = iota((TOK, ATOMS), 1).astype(F32)
        member[...] = jnp.where(
            (at >= starts_column) & (at < ends_column), 1.0, 0.0
        ).astype(BF16)

        weights[0].wait()
        w32 = bias_weights()
        side_moments(w32)

        @pl.loop(0, TOK // OWN_UNROLL)
        def _(k):
            for u in range(OWN_UNROLL // STEP):
                own_copy(k * (OWN_UNROLL // STEP) + u).wait()
            for u in range(OWN_UNROLL):
                i = k * OWN_UNROLL + u
                moments(own_pair[i], i, 0, w32)

        for w in weights[2:]:
            w.wait()
        mine.wait()
        pl.semaphore_wait(barrier, greetings)

        @pl.when(to_next)
        def _():
            edge_copy(True, r + 1).start()

        @pl.when(to_prev)
        def _():
            edge_copy(False, r - 1).start()

        own_atoms.wait()
        near_first = row_peers[::-1]
        for col in near_first[:EARLY]:
            atom_copy(col).wait_recv()
        own_bias = [value.astype(BF16) for value in head_bias(0, TOK)]
        main_side = head_bias(8 * TOK, HALF)
        for h in range(HEADS):
            for k in range(ATOMS // 256):
                first = k * 256
                rows = mm(
                    rhs[MARGIN + first : MARGIN + first + 256, CH : CH + TOK], own_bias[h]
                ).astype(BF16)
                for w in range(256 // WIN):
                    start = (first + w * WIN) * HEADS + h * WIN
                    picked[start : start + WIN, :] = rows[w * WIN : (w + 1) * WIN]

        def keys_values(start, count):
            span = pl.ds(start, count)
            norm = layer_norm(atoms[span, :].astype(F32)).astype(BF16)
            projected = mm(norm, wp[...])
            rhs[span, 0:CH] = projected[:, CH : 2 * CH].astype(BF16)
            vals[span, 0:CH] = projected[:, 2 * CH : 3 * CH].astype(BF16)
            return projected

        def project(col):
            projected = keys_values(pl.multiple_of(MARGIN + col * OWN, 16), OWN)
            span = pl.ds(pl.multiple_of(col * OWN, OWN), OWN)
            gate[span, :] = 0.5 + 0.5 * jnp.tanh(0.5 * projected[:, 3 * CH :])
            queries[span, :] = (projected[:, 0:CH] * (CH // HEADS) ** -0.5).astype(BF16)

        for col in [c] + near_first[:EARLY]:
            project(col)

        for col in near_first[EARLY:]:
            atom_copy(col).wait_recv()

        @pl.when(has_prev)
        def _():
            edge_copy(True, r).wait_recv()

        @pl.when(jnp.logical_not(has_prev))
        def _():
            atoms[0:MARGIN, :] = jnp.zeros((MARGIN, CH), BF16)

        @pl.when(has_next)
        def _():
            edge_copy(False, r).wait_recv()

        @pl.when(jnp.logical_not(has_next))
        def _():
            atoms[MARGIN + ATOMS :, :] = jnp.zeros((MARGIN, CH), BF16)

        @pl.when(has_helper)
        def _():
            side_copy().wait_recv()

        @pl.when(jnp.logical_not(has_helper))
        def _():
            side_in[...] = jnp.zeros(side_in.shape, BF16)

        for col in near_first[EARLY:]:
            project(col)
        keys_values(0, MARGIN)
        keys_values(MARGIN + ATOMS, MARGIN)

        helped = side_in[...].astype(F32)
        mask_lane = iota((TOK, TOK), 1) == MASK_LANE
        for h in range(HEADS):
            theirs = helped[h * HALF : (h + 1) * HALF]
            ahead = jnp.where(on_main_next, main_side[h], theirs)
            behind = jnp.where(on_main_next, theirs, main_side[h])
            ahead_rolled = pltpu.roll(ahead, SPLIT, 1)
            behind_rolled = pltpu.roll(behind, SPLIT, 1)
            none = jnp.zeros((HALF, TOK), F32)
            gap = TOK - REACH - HALF
            upper_rows = jnp.concatenate([none, none[:gap], ahead, ahead_rolled], axis=0)
            lower_rows = jnp.concatenate([behind_rolled, behind, none, none[:gap]], axis=0)
            both = jnp.where(iota((TOK, TOK), 1) < SPLIT, upper_rows, lower_rows)
            both = jnp.where(mask_lane, -1e30, both).astype(BF16)
            for k, first in enumerate((0, ATOMS - 2 * WIN)):
                rows = mm(
                    rhs[MARGIN + first : MARGIN + first + 2 * WIN, CH : CH + TOK], both
                ).astype(BF16)
                for w in range(2):
                    start = ((2 * k + w) * HEADS + h) * WIN
                    picked_side[start : start + WIN, :] = rows[w * WIN : (w + 1) * WIN]

        head_of = iota((WIN, CH), 1) // (CH // HEADS)

        def attend(q, bias, keys, extra, values, opened):
            split = [jnp.where(head_of == h, q, jnp.zeros_like(q)) for h in range(HEADS)]
            parts = [jnp.concatenate(split, axis=0), bias]
            if extra is not None:
                parts.append(extra)
            scores = nt(jnp.concatenate(parts, axis=1), keys)
            top = jnp.max(scores, -1, keepdims=True)
            weight = jnp.exp(scores - top).astype(BF16)
            total = mm(weight, values)
            above = total[0:WIN, 0:CH]
            below = total[0:WIN, CH:]
            for h in range(1, HEADS):
                here = head_of == h
                above = jnp.where(here, total[h * WIN : (h + 1) * WIN, 0:CH], above)
                below = jnp.where(here, total[h * WIN : (h + 1) * WIN, CH:], below)
            return (above * opened / below).astype(BF16)

        for n, w in enumerate(EDGES):
            span = slice(w * WIN, (w + 1) * WIN)
            keys = slice(w * WIN, w * WIN + KEYS)
            block = slice(w * WIN * HEADS, (w + 1) * WIN * HEADS)
            gated[span, :] = attend(
                queries[span, :],
                picked[block, :],
                rhs[keys, :],
                picked_side[n * WIN * HEADS : (n + 1) * WIN * HEADS, :],
                vals[keys, :],
                gate[span, :],
            )

        @pl.loop(2, ATOMS // WIN - 2, unroll=ATTEND_UNROLL)
        def _(w):
            start = pl.multiple_of(w * WIN, WIN)
            span = pl.ds(start, WIN)
            keys = pl.ds(start, KEYS)
            block = pl.ds(pl.multiple_of(w * WIN * HEADS, WIN * HEADS), WIN * HEADS)
            gated[span, :] = attend(
                queries[span, :],
                picked[block, :],
                rhs[keys, 0 : CH + TOK],
                None,
                vals[keys, :],
                gate[span, :],
            )

        for k in range(ATOMS // 256):
            span = slice(k * 256, (k + 1) * 256)
            ext = slice(MARGIN + k * 256, MARGIN + (k + 1) * 256)
            resid[span, :] = (atoms[ext, :].astype(F32) + mm(gated[span, :], wo[...])).astype(BF16)
        for p in range(4):
            resid_send(p).start()
        for k in range(ATOMS // PART):
            span = slice(k * PART, (k + 1) * PART)
            final[span, :] = transition(resid[span, :])
        terms = jnp.zeros((TOK, CH), F32)
        for q in range(3):
            part = slice(q * CH, (q + 1) * CH)
            for k in range(ATOMS // 256):
                span = slice(k * 256, (k + 1) * 256)
                emitted[span, part] = jnp.maximum(mm(final[span, :], wk[:, part]), 0.0).astype(BF16)
            totals = mm(member[...], emitted[:, part])
            single = (totals / counts_column).astype(BF16)
            single_out[q] = single
            for p in tree[0][1]:
                single_send(p, q).start()
            terms = terms + mm(single, wc[part, :])
        col_out[pl.ds(pl.multiple_of(odd * TOK, TOK), TOK), :] = terms.astype(BF16)
        for p in range(7):
            col_send(p).start()
        resid_in[0:OWN, :] = resid[pl.ds(pl.multiple_of(c * OWN, OWN), OWN), :]

    @pl.when(not_main)
    def _():
        for w in receiver_weights:
            w.wait()

    @pl.when(passes_atoms)
    def _():
        resid_send(1).wait_recv()
        resid_in[...] = transition(resid_in[...])
        atom_pass().start()
        atom_out[...] = resid_in[pl.ds(pl.multiple_of(x_hi * OWN, OWN), OWN), :]

    @pl.when(across & (ahead_of_home == 0))
    def _():
        resid_send(0).wait_recv()

    @pl.when(ahead_of_home == 0)
    def _():
        atom_out[...] = transition(resid_in[0:OWN, :])

    for role, copies in tree[1:]:

        @pl.when(role)
        def _():
            for k in range(3):
                single_send(0, k).wait_recv()
                for p in copies:
                    single_send(p, k).start()

    @pl.when(not_main)
    def _():
        col_send(0).wait_recv()

    col_forward().start()

    @pl.when(not_main & jnp.logical_not(relays))
    def _():
        for k in range(3):
            single_send(0, k).wait_recv()

    row_out[...] = sum(mm(single_out[q], wr[q * CH : (q + 1) * CH, :]) for q in range(3))
    col_forward().wait_recv()
    col_forward().wait_send()

    @pl.when(passes_atoms)
    def _():
        atom_pass().wait_send()

    @pl.when(across & (ahead_of_home != 0))
    def _():
        atom_pass().wait_recv()

    @pl.when(is_main)
    def _():
        for p in range(4):
            resid_send(p).wait_send()
        for p in range(7):
            col_send(p).wait_send()

    for role, copies in tree:

        @pl.when(role)
        def _():
            for k in range(3):
                for p in copies:
                    single_send(p, k).wait_send()

    @pl.when(not_main)
    def _():
        atom_copy(c).wait_send()

    @pl.when(to_next)
    def _():
        edge_copy(True, r + 1).wait_send()

    @pl.when(to_prev)
    def _():
        edge_copy(False, r - 1).wait_send()


def update_kernel(pair, row, col, atom, single, new_pair, atom_out, single_out, result, sem):
    small = [
        pltpu.make_async_copy(atom, atom_out, sem.at[0]),
    ] + [
        pltpu.make_async_copy(single.at[q], single_out.at[:, pl.ds(q * CH, CH)], sem.at[1 + q])
        for q in range(3)
    ]
    for copy in small:
        copy.start()
    width = col.shape[0]
    column = col[...]

    def out_copy(k):
        rows = pl.ds(k * BLOCK, BLOCK)
        return pltpu.make_async_copy(result.at[rows], new_pair.at[rows], sem.at[4 + k])

    @pl.loop(0, TOK // BLOCK)
    def _(k):
        terms = row[pl.ds(pl.multiple_of(k * BLOCK, BLOCK), BLOCK), :]
        for u in range(BLOCK):
            term = jnp.broadcast_to(terms[u : u + 1], (16, CH)).astype(BF16)
            term = jnp.concatenate([term] * (width // 16), axis=0)
            i = k * BLOCK + u
            result[i] = pair[i] + (column + term)
        out_copy(k).start()

    for copy in small:
        copy.wait()
    for k in range(TOK // BLOCK):
        out_copy(k).wait()


def shards(
    pair, counts, atom_single, w_bias, w_project, w_out, w_trans_in, w_trans_out, w_token, w_row, w_col
):
    any_ = pl.BlockSpec(memory_space=pl.ANY)
    vmem = pltpu.VMEM
    in_hbm = lambda a: pltpu.with_memory_space_constraint(a, pltpu.HBM)
    weights = (w_bias.T, w_project, w_out, w_trans_in, w_trans_out, w_token, w_row, w_col)
    in_vmem = pl.BlockSpec(memory_space=vmem)
    atom, single, row, col = pl.pallas_call(
        exchange_kernel,
        out_shape=(
            jax.ShapeDtypeStruct((OWN, CH), BF16),
            jax.ShapeDtypeStruct((3, TOK, CH), BF16),
            jax.ShapeDtypeStruct((TOK, CH), F32),
            jax.ShapeDtypeStruct((2 * TOK, CH), BF16),
        ),
        in_specs=[any_] * (3 + len(weights)),
        out_specs=(in_vmem,) * 4,
        scratch_shapes=[
            vmem((TOK, TOK, CH), BF16),
            vmem((HALF, TOK, CH), BF16),
            vmem(counts.shape, jnp.int32),
            *[vmem(w.shape, w.dtype) for w in weights],
            vmem((8 * (TOK + HALF + 1), TOK), F32),
            vmem((8 * (TOK + HALF + 1), TOK), F32),
            vmem((HEADS * HALF, TOK), BF16),
            vmem((HEADS * HALF, TOK), BF16),
            vmem((EXT, CH), BF16),
            vmem((ATOMS, CH), BF16),
            vmem((ATOMS * HEADS, TOK), BF16),
            vmem((len(EDGES) * WIN * HEADS, TOK), BF16),
            vmem((EXT, CH + 2 * TOK), BF16),
            vmem((EXT, 2 * CH), BF16),
            vmem((ATOMS, CH), F32),
            vmem((ATOMS, CH), BF16),
            vmem((ATOMS, CH), BF16),
            vmem((2 * OWN, CH), BF16),
            vmem((OWN, CH), BF16),
            vmem((ATOMS, CH), BF16),
            vmem((ATOMS, 3 * CH), BF16),
            vmem((TOK, ATOMS), BF16),
            pltpu.SemaphoreType.DMA((TOK // STEP,)),
            pltpu.SemaphoreType.DMA((2,)),
            pltpu.SemaphoreType.DMA((1 + len(weights),)),
            pltpu.SemaphoreType.DMA((2,)),
            pltpu.SemaphoreType.DMA((32,)),
            pltpu.SemaphoreType.DMA((N_COL + 10,)),
        ],
        compiler_params=pltpu.CompilerParams(
            collective_id=0, has_side_effects=True, vmem_limit_bytes=40 * 2**20
        ),
    )(*[in_hbm(a) for a in (pair, atom_single, counts, *weights)])
    new_pair, atom_out, token_single = pl.pallas_call(
        update_kernel,
        out_shape=(
            jax.ShapeDtypeStruct(pair.shape, BF16),
            jax.ShapeDtypeStruct(atom.shape, BF16),
            jax.ShapeDtypeStruct((TOK, 3 * CH), BF16),
        ),
        in_specs=[in_vmem] * 5,
        out_specs=(any_,) * 3,
        scratch_shapes=[
            vmem(pair.shape, BF16),
            pltpu.SemaphoreType.DMA((4 + TOK // BLOCK,)),
        ],
        compiler_params=pltpu.CompilerParams(vmem_limit_bytes=UPDATE_VMEM * 2**20),
    )(pltpu.with_memory_space_constraint(pair, pltpu.VMEM), row, col, atom, single)
    return atom_out, token_single, new_pair


def solution(mesh):
    return jax.shard_map(
        shards,
        mesh=mesh,
        in_specs=(P("row", "col", None), P(), P(("row", "col"), None)) + (P(),) * 8,
        out_specs=(P(("row", "col"), None), P("row", None), P("row", "col", None)),
        check_vma=False,
    )
```

```python
import functools

import jax
import jax.numpy as jnp
from jax import lax
from jax.experimental import pallas as pl
from jax.experimental.pallas import tpu as pltpu
from jax.sharding import PartitionSpec as P

MESH = pl.DeviceIdType.MESH
F32 = jnp.float32
BF16 = jnp.bfloat16
N_ROW, N_COL = 16, 8
TOK = 128
CH = 128
HEADS = 4
WIN = 32
KEYS = 128
ATOMS = 1024
MARGIN = (KEYS - WIN) // 2
EXT = ATOMS + 2 * MARGIN
OWN = ATOMS // N_COL
STEP = 16
BLOCK = 8
UPDATE_VMEM = 20
PARTS = 2
REACH = 80
HALF = REACH // 2
EARLY = 6
EDGES = (0, 1, 30, 31)
MASK_LANE = 56
ATTEND_UNROLL = 28
OWN_UNROLL = 64
SIDE_UNROLL = 40
PART = 256
SPLIT = 64


def nt(a, b):
    return lax.dot_general(a, b, (((1,), (1,)), ((), ())), preferred_element_type=F32)


def mm(a, b):
    return jnp.dot(a, b, preferred_element_type=F32)


def layer_norm(x):
    average = jnp.mean(x, -1, keepdims=True)
    centred = x - average
    spread = jnp.mean(centred * centred, -1, keepdims=True)
    return centred * lax.rsqrt(spread + 1e-05)


def iota(shape, axis):
    return lax.broadcasted_iota(jnp.int32, shape, axis)


def exchange_kernel(
    pair_hbm,
    atom_hbm,
    counts_hbm,
    wb_hbm,
    wp_hbm,
    wo_hbm,
    wi_hbm,
    wt_hbm,
    wk_hbm,
    wr_hbm,
    wc_hbm,
    atom_out,
    single_out,
    row_out,
    col_out,
    own_pair,
    side_pair,
    counts,
    wb,
    wp,
    wo,
    wi,
    wt,
    wk,
    wr,
    wc,
    stat,
    diag,
    side,
    side_in,
    atoms,
    queries,
    picked,
    picked_side,
    rhs,
    vals,
    gate,
    gated,
    resid,
    resid_in,
    mine_in,
    final,
    emitted,
    member,
    own_sem,
    side_pair_sem,
    w_sem,
    local_sem,
    send_sem,
    recv_sem,
):
    r, c = lax.axis_index("row"), lax.axis_index("col")
    odd = lax.rem(r, 2)
    home = r // 2
    is_main = c == home
    not_main = jnp.logical_not(is_main)
    helper_col = home - 1 + 2 * odd
    has_helper = (helper_col >= 0) & (helper_col < N_COL)
    is_helper = c == helper_col
    has_prev, has_next = r > 0, r < N_ROW - 1
    z, x_hi = c // 2, lax.rem(c, 2)
    y, x_lo = r // 4, lax.rem(r // 2, 2)
    sibling = r + 1 - 2 * odd
    partner = c + 1 - 2 * x_hi
    home_side = x_hi == x_lo
    row_peers = [
        (lax.rem(z + dz, 4) * 2 + (1 - x_hi if dx else x_hi))
        for dz, dx in ((2, 1), (1, 1), (3, 1), (2, 0), (0, 1), (1, 0), (3, 0))
    ]
    col_peers = [
        (lax.rem(y + dy, 4) * 2 + (1 - x_lo if dx else x_lo)) * 2 + odd
        for dy, dx in ((2, 1), (1, 1), (3, 1), (2, 0), (1, 0), (3, 0), (0, 1))
    ]
    own_start = pl.multiple_of(odd * TOK, TOK)
    on_main_next = odd == 0
    side_is_next = on_main_next == is_main
    side_rows = jnp.where(side_is_next, TOK - REACH, 0)
    side_start = pl.multiple_of((1 - odd) * TOK + jnp.where(side_is_next, 0, SPLIT), SPLIT)

    def own_copy(k):
        rows = pl.ds(k * STEP, STEP)
        return pltpu.make_async_copy(
            pair_hbm.at[rows, pl.ds(own_start, TOK)], own_pair.at[rows], own_sem.at[k]
        )

    def side_pair_copy(k):
        return pltpu.make_async_copy(
            pair_hbm.at[pl.ds(side_rows + k * HALF, HALF), pl.ds(side_start, SPLIT)],
            side_pair.at[:, pl.ds(k * SPLIT, SPLIT)],
            side_pair_sem.at[k],
        )

    weights = [
        pltpu.make_async_copy(a, b, w_sem.at[i])
        for i, (a, b) in enumerate(
            [
                (wb_hbm, wb),
                (counts_hbm, counts),
                (wp_hbm, wp),
                (wo_hbm, wo),
                (wi_hbm, wi),
                (wt_hbm, wt),
                (wk_hbm, wk),
                (wr_hbm, wr),
                (wc_hbm, wc),
            ]
        )
    ]
    receiver_weights = [weights[4], weights[5], weights[7]]
    steps = TOK // STEP

    own_atoms = pltpu.make_async_copy(
        atom_hbm, atoms.at[pl.ds(MARGIN + c * OWN, OWN)], local_sem.at[0]
    )
    mine = pltpu.make_async_copy(atom_hbm, mine_in, local_sem.at[1])
    barrier = pltpu.get_barrier_semaphore()

    def hello(row, col):
        pl.semaphore_signal(barrier, inc=1, device_id=(row, col), device_id_type=MESH)

    to_next = (c == N_COL - 1) & has_next
    to_prev = (c == 0) & has_prev

    across = jnp.logical_not(home_side)
    ahead_of_home = lax.rem(z - y + 4, 4)
    relays = not_main & ((home_side & (ahead_of_home != 2)) | (across & (ahead_of_home == 0)))
    passes_atoms = not_main & home_side
    @pl.when(is_main)
    def _():
        for col in row_peers:
            hello(r, col)

        @pl.when(has_prev)
        def _():
            hello(r - 1, N_COL - 1)

        @pl.when(has_next)
        def _():
            hello(r + 1, 0)

    @pl.when(not_main)
    def _():
        hello(r, home)

    for n in range(2):

        @pl.when(r != 2 * c + n)
        def _():
            hello(2 * c + n, c)

    def one(flag):
        return jnp.where(flag, 1, 0)

    mine.start()
    greetings = (
        one(is_main) * (N_COL - 1 + N_ROW - 1)
        + one(not_main)
        + one(to_next)
        + one(to_prev)
    )

    @pl.when(is_main)
    def _():
        weights[1].start()
        own_atoms.start()
        weights[0].start()
        for k in range(2):
            side_pair_copy(k).start()
        for k in range(steps):
            own_copy(k).start()
        for w in weights[2:]:
            w.start()

    @pl.when(not_main)
    def _():
        @pl.when(is_helper)
        def _():
            weights[0].start()
            for k in range(2):
                side_pair_copy(k).start()

        for w in receiver_weights:
            w.start()

    def atom_copy(col):
        return pltpu.make_async_remote_copy(
            src_ref=mine_in,
            dst_ref=atoms.at[pl.ds(MARGIN + col * OWN, OWN)],
            send_sem=send_sem.at[0],
            recv_sem=recv_sem.at[col],
            device_id=(r, home),
            device_id_type=MESH,
        )

    def edge_copy(forward, row):
        start = OWN - MARGIN if forward else 0
        return pltpu.make_async_remote_copy(
            src_ref=mine_in.at[pl.ds(start, MARGIN)],
            dst_ref=atoms.at[pl.ds(0 if forward else MARGIN + ATOMS, MARGIN)],
            send_sem=send_sem.at[1 if forward else 2],
            recv_sem=recv_sem.at[N_COL + (0 if forward else 1)],
            device_id=(row, row // 2),
            device_id_type=MESH,
        )

    def side_copy():
        return pltpu.make_async_remote_copy(
            src_ref=side,
            dst_ref=side_in,
            send_sem=send_sem.at[3],
            recv_sem=recv_sem.at[N_COL + 2],
            device_id=(r, home),
            device_id_type=MESH,
        )


    lane = iota((8, TOK), 1)
    sub = iota((8, TOK), 0)
    block_of = lane // 8
    on_diag = lax.rem(lane, 8) == sub

    def bias_weights():
        w = wb[...]
        w = w - jnp.mean(w, -1, keepdims=True)
        high = w.astype(BF16)
        rest = w - high.astype(F32)
        mid = rest.astype(BF16)
        low = (rest - mid.astype(F32)).astype(BF16)
        ones = jnp.ones((1, CH), BF16)
        zeros = jnp.zeros((12, CH), BF16)
        return jnp.concatenate(
            [high, ones, zeros[:3], mid, zeros[:4], low, zeros], axis=0
        )

    def moments(x, i, first, w32):
        t = nt(jnp.concatenate([w32, x], axis=0), x)
        d = jnp.zeros((8, TOK), F32)
        for k in range(TOK // 8):
            d = jnp.where(block_of == k, t[32 + 8 * k : 40 + 8 * k], d)
        rows = pl.ds(pl.multiple_of(first + i * 8, 8), 8)
        stat[rows, :] = t[0:8] + t[8:16] + t[16:24]
        diag[rows, :] = jnp.where(on_diag, d, 0.0)

    def side_moments(w32):
        for k in range(2):
            side_pair_copy(k).wait()

        @pl.loop(0, HALF, unroll=SIDE_UNROLL)
        def _(i):
            moments(side_pair[i], i, 8 * TOK, w32)

    def head_bias(first, count):
        def part(ref, s):
            return ref[pl.ds(first + s, count, stride=8), :]

        s1 = part(stat, 4)
        s2 = part(diag, 0)
        for s in range(1, 8):
            s2 = s2 + part(diag, s)
        near = (s1 * (1 / CH)).astype(BF16).astype(F32)
        offset = s1 * (1 / CH) - near
        moment = (s2 - 2 * near * s1) + CH * (near * near)
        spread = jnp.maximum(moment * (1 / CH) - offset * offset, 0.0)
        scale = lax.rsqrt(spread + 1e-05)
        return [part(stat, h) * scale for h in range(HEADS)]

    def transition(x):
        residual = x.astype(F32)
        second = layer_norm(residual).astype(BF16)
        doubled = mm(second, wi[...])
        swish = doubled[:, 0 : 2 * CH]
        hidden = swish * (0.5 + 0.5 * jnp.tanh(0.5 * swish)) * doubled[:, 2 * CH :]
        return (residual + mm(hidden.astype(BF16), wt[...])).astype(BF16)

    @pl.when(not_main)
    def _():
        mine.wait()
        pl.semaphore_wait(barrier, greetings)
        atom_copy(c).start()

    @pl.when(to_next & not_main)
    def _():
        edge_copy(True, r + 1).start()

    @pl.when(to_prev & not_main)
    def _():
        edge_copy(False, r - 1).start()

    @pl.when(is_helper)
    def _():
        weights[0].wait()
        side_moments(bias_weights())
        side[...] = jnp.concatenate(head_bias(8 * TOK, HALF), axis=0).astype(BF16)

    @pl.when(is_helper)
    def _():
        side_copy().start()
        side_copy().wait_send()

    def send(src, dst, slot, recv, row, col):
        return pltpu.make_async_remote_copy(
            src_ref=src,
            dst_ref=dst,
            send_sem=send_sem.at[slot],
            recv_sem=recv_sem.at[recv],
            device_id=(row, col),
            device_id_type=MESH,
        )

    base = N_COL + 3

    def resid_send(p):
        col = (partner, row_peers[5], row_peers[6], row_peers[3])[p]
        count = OWN if p == 0 else 2 * OWN
        first = col if p == 0 else col // 2 * 2
        return send(
            resid.at[pl.ds(pl.multiple_of(first * OWN, OWN), count)],
            resid_in.at[pl.ds(0, count)],
            4 + p,
            base,
            r,
            col,
        )

    def atom_pass():
        return send(
            resid_in.at[pl.ds(pl.multiple_of((1 - x_hi) * OWN, OWN), OWN)],
            atom_out,
            8,
            base + 1,
            r,
            partner,
        )

    def single_send(p, k):
        piece = single_out.at[k // PARTS, pl.ds(k % PARTS * (TOK // PARTS), TOK // PARTS)]
        col = (row_peers[5], row_peers[6], partner, row_peers[3])[p]
        return send(piece, piece, 12 + 4 * k + p, base + 6 + k, r, col)

    tree = (
        (is_main, (2, 0, 1)),
        (home_side & (ahead_of_home == 1), (0, 2)),
        (home_side & (ahead_of_home == 3), (2,)),
        (across & (ahead_of_home == 0), (3,)),
    )

    own_half = col_out.at[pl.ds(pl.multiple_of(odd * TOK, TOK), TOK)]

    def col_send(p):
        return send(own_half, own_half, 12 + 12 * PARTS + p, base + 2, col_peers[p], c)

    def col_forward():
        return send(own_half, own_half, 9, base + 3, sibling, c)

    @pl.when(is_main)
    def _():
        weights[1].wait()
        own_counts = counts[pl.ds(r, 1), :].astype(F32)
        prev_counts = counts[pl.ds(jnp.maximum(r - 1, 0), 1), :].astype(F32)
        next_counts = counts[pl.ds(jnp.minimum(r + 1, N_ROW - 1), 1), :].astype(F32)
        stacked = jnp.concatenate(
            [own_counts, prev_counts, next_counts, jnp.zeros((5, TOK), F32)], axis=0
        )
        upper = (iota((TOK, TOK), 0) <= iota((TOK, TOK), 1)).astype(F32).astype(BF16)
        lower = (iota((TOK, TOK), 0) >= iota((TOK, TOK), 1)).astype(F32).astype(BF16)
        stacked_low = stacked.astype(BF16)
        ends = mm(stacked_low, upper)
        starts = ends - stacked
        ends_column = nt(lower, stacked_low)[:, 0:1]
        eye = (iota((TOK, TOK), 0) == iota((TOK, TOK), 1)).astype(F32).astype(BF16)
        counts_column = nt(eye, stacked_low)[:, 0:1]
        starts_column = ends_column - counts_column
        far = 1e9
        one_lane = iota((1, TOK), 1)
        after = one_lane < SPLIT
        side_from = jnp.where(
            after,
            jnp.where(has_next, starts[2:3] + ATOMS, far),
            jnp.where(has_prev, starts[1:2] - ATOMS, far),
        )
        side_to = jnp.where(
            after,
            jnp.where(has_next, ends[2:3] + ATOMS, far),
            jnp.where(has_prev, ends[1:2] - ATOMS, far),
        )
        masked = one_lane == MASK_LANE
        low_mask = jnp.where(has_prev, far, -float(MARGIN))
        mask_from = jnp.where(has_next, low_mask, float(ATOMS))
        mask_to = jnp.where(
            has_next, jnp.where(has_prev, far, 0.0), float(ATOMS + MARGIN)
        )
        side_from = jnp.where(masked, mask_from, side_from)
        side_to = jnp.where(masked, mask_to, side_to)

        def onehot(first, count, lo, hi):
            at = (iota((count, TOK), 0) + first).astype(F32)
            return jnp.where((at >= lo) & (at < hi), 1.0, 0.0).astype(BF16)

        rhs[:, CH : CH + TOK] = onehot(-MARGIN, EXT, starts[0:1], ends[0:1])
        for first in (0, ATOMS - 2 * MARGIN + WIN):
            rhs[first : first + KEYS + WIN, CH + TOK :] = onehot(
                first - MARGIN, KEYS + WIN, side_from, side_to
            )
        vals[:, CH:] = jnp.ones((EXT, CH), BF16)
        at = iota((TOK, ATOMS), 1).astype(F32)
        member[...] = jnp.where(
            (at >= starts_column) & (at < ends_column), 1.0, 0.0
        ).astype(BF16)

        weights[0].wait()
        w32 = bias_weights()
        side_moments(w32)

        @pl.loop(0, TOK // OWN_UNROLL)
        def _(k):
            for u in range(OWN_UNROLL // STEP):
                own_copy(k * (OWN_UNROLL // STEP) + u).wait()
            for u in range(OWN_UNROLL):
                i = k * OWN_UNROLL + u
                moments(own_pair[i], i, 0, w32)

        for w in weights[2:]:
            w.wait()
        mine.wait()
        pl.semaphore_wait(barrier, greetings)

        @pl.when(to_next)
        def _():
            edge_copy(True, r + 1).start()

        @pl.when(to_prev)
        def _():
            edge_copy(False, r - 1).start()

        own_atoms.wait()
        near_first = row_peers[::-1]
        for col in near_first[:EARLY]:
            atom_copy(col).wait_recv()
        own_bias = [value.astype(BF16) for value in head_bias(0, TOK)]
        main_side = head_bias(8 * TOK, HALF)
        for h in range(HEADS):
            for k in range(ATOMS // 256):
                first = k * 256
                rows = mm(
                    rhs[MARGIN + first : MARGIN + first + 256, CH : CH + TOK], own_bias[h]
                ).astype(BF16)
                for w in range(256 // WIN):
                    start = (first + w * WIN) * HEADS + h * WIN
                    picked[start : start + WIN, :] = rows[w * WIN : (w + 1) * WIN]

        def keys_values(start, count):
            span = pl.ds(start, count)
            norm = layer_norm(atoms[span, :].astype(F32)).astype(BF16)
            projected = mm(norm, wp[...])
            rhs[span, 0:CH] = projected[:, CH : 2 * CH].astype(BF16)
            vals[span, 0:CH] = projected[:, 2 * CH : 3 * CH].astype(BF16)
            return projected

        def project(col):
            projected = keys_values(pl.multiple_of(MARGIN + col * OWN, 16), OWN)
            span = pl.ds(pl.multiple_of(col * OWN, OWN), OWN)
            gate[span, :] = 0.5 + 0.5 * jnp.tanh(0.5 * projected[:, 3 * CH :])
            queries[span, :] = (projected[:, 0:CH] * (CH // HEADS) ** -0.5).astype(BF16)

        for col in [c] + near_first[:EARLY]:
            project(col)

        for col in near_first[EARLY:]:
            atom_copy(col).wait_recv()

        @pl.when(has_prev)
        def _():
            edge_copy(True, r).wait_recv()

        @pl.when(jnp.logical_not(has_prev))
        def _():
            atoms[0:MARGIN, :] = jnp.zeros((MARGIN, CH), BF16)

        @pl.when(has_next)
        def _():
            edge_copy(False, r).wait_recv()

        @pl.when(jnp.logical_not(has_next))
        def _():
            atoms[MARGIN + ATOMS :, :] = jnp.zeros((MARGIN, CH), BF16)

        @pl.when(has_helper)
        def _():
            side_copy().wait_recv()

        @pl.when(jnp.logical_not(has_helper))
        def _():
            side_in[...] = jnp.zeros(side_in.shape, BF16)

        for col in near_first[EARLY:]:
            project(col)
        keys_values(0, MARGIN)
        keys_values(MARGIN + ATOMS, MARGIN)

        helped = side_in[...].astype(F32)
        mask_lane = iota((TOK, TOK), 1) == MASK_LANE
        for h in range(HEADS):
            theirs = helped[h * HALF : (h + 1) * HALF]
            ahead = jnp.where(on_main_next, main_side[h], theirs)
            behind = jnp.where(on_main_next, theirs, main_side[h])
            ahead_rolled = pltpu.roll(ahead, SPLIT, 1)
            behind_rolled = pltpu.roll(behind, SPLIT, 1)
            none = jnp.zeros((HALF, TOK), F32)
            gap = TOK - REACH - HALF
            upper_rows = jnp.concatenate([none, none[:gap], ahead, ahead_rolled], axis=0)
            lower_rows = jnp.concatenate([behind_rolled, behind, none, none[:gap]], axis=0)
            both = jnp.where(iota((TOK, TOK), 1) < SPLIT, upper_rows, lower_rows)
            both = jnp.where(mask_lane, -1e30, both).astype(BF16)
            for k, first in enumerate((0, ATOMS - 2 * WIN)):
                rows = mm(
                    rhs[MARGIN + first : MARGIN + first + 2 * WIN, CH : CH + TOK], both
                ).astype(BF16)
                for w in range(2):
                    start = ((2 * k + w) * HEADS + h) * WIN
                    picked_side[start : start + WIN, :] = rows[w * WIN : (w + 1) * WIN]

        head_of = iota((WIN, CH), 1) // (CH // HEADS)

        def attend(q, bias, keys, extra, values, opened):
            split = [jnp.where(head_of == h, q, jnp.zeros_like(q)) for h in range(HEADS)]
            parts = [jnp.concatenate(split, axis=0), bias]
            if extra is not None:
                parts.append(extra)
            scores = nt(jnp.concatenate(parts, axis=1), keys)
            top = jnp.max(scores, -1, keepdims=True)
            weight = jnp.exp(scores - top).astype(BF16)
            total = mm(weight, values)
            above = total[0:WIN, 0:CH]
            below = total[0:WIN, CH:]
            for h in range(1, HEADS):
                here = head_of == h
                above = jnp.where(here, total[h * WIN : (h + 1) * WIN, 0:CH], above)
                below = jnp.where(here, total[h * WIN : (h + 1) * WIN, CH:], below)
            return (above * opened / below).astype(BF16)

        for n, w in enumerate(EDGES):
            span = slice(w * WIN, (w + 1) * WIN)
            keys = slice(w * WIN, w * WIN + KEYS)
            block = slice(w * WIN * HEADS, (w + 1) * WIN * HEADS)
            gated[span, :] = attend(
                queries[span, :],
                picked[block, :],
                rhs[keys, :],
                picked_side[n * WIN * HEADS : (n + 1) * WIN * HEADS, :],
                vals[keys, :],
                gate[span, :],
            )

        @pl.loop(2, ATOMS // WIN - 2, unroll=ATTEND_UNROLL)
        def _(w):
            start = pl.multiple_of(w * WIN, WIN)
            span = pl.ds(start, WIN)
            keys = pl.ds(start, KEYS)
            block = pl.ds(pl.multiple_of(w * WIN * HEADS, WIN * HEADS), WIN * HEADS)
            gated[span, :] = attend(
                queries[span, :],
                picked[block, :],
                rhs[keys, 0 : CH + TOK],
                None,
                vals[keys, :],
                gate[span, :],
            )

        for k in range(ATOMS // 256):
            span = slice(k * 256, (k + 1) * 256)
            ext = slice(MARGIN + k * 256, MARGIN + (k + 1) * 256)
            resid[span, :] = (atoms[ext, :].astype(F32) + mm(gated[span, :], wo[...])).astype(BF16)
        for p in range(4):
            resid_send(p).start()
        for k in range(ATOMS // PART):
            span = slice(k * PART, (k + 1) * PART)
            final[span, :] = transition(resid[span, :])
        terms = jnp.zeros((TOK, CH), F32)
        for q in range(3):
            part = slice(q * CH, (q + 1) * CH)
            for k in range(ATOMS // 256):
                span = slice(k * 256, (k + 1) * 256)
                emitted[span, part] = jnp.maximum(mm(final[span, :], wk[:, part]), 0.0).astype(BF16)
            totals = mm(member[...], emitted[:, part])
            single = (totals / counts_column).astype(BF16)
            single_out[q] = single
            for k in range(q * PARTS, (q + 1) * PARTS):
                for p in tree[0][1]:
                    single_send(p, k).start()
            terms = terms + mm(single, wc[part, :])
        col_out[pl.ds(pl.multiple_of(odd * TOK, TOK), TOK), :] = terms.astype(BF16)
        for p in range(7):
            col_send(p).start()
        resid_in[0:OWN, :] = resid[pl.ds(pl.multiple_of(c * OWN, OWN), OWN), :]

    @pl.when(not_main)
    def _():
        for w in receiver_weights:
            w.wait()

    @pl.when(passes_atoms)
    def _():
        resid_send(1).wait_recv()
        resid_in[...] = transition(resid_in[...])
        atom_pass().start()
        atom_out[...] = resid_in[pl.ds(pl.multiple_of(x_hi * OWN, OWN), OWN), :]

    @pl.when(across & (ahead_of_home == 0))
    def _():
        resid_send(0).wait_recv()

    @pl.when(ahead_of_home == 0)
    def _():
        atom_out[...] = transition(resid_in[0:OWN, :])

    for role, copies in tree[1:]:

        @pl.when(role)
        def _():
            for k in range(3 * PARTS):
                single_send(0, k).wait_recv()
                for p in copies:
                    single_send(p, k).start()

    @pl.when(not_main)
    def _():
        col_send(0).wait_recv()

    col_forward().start()

    @pl.when(not_main & jnp.logical_not(relays))
    def _():
        for k in range(3 * PARTS):
            single_send(0, k).wait_recv()

    row_out[...] = sum(mm(single_out[q], wr[q * CH : (q + 1) * CH, :]) for q in range(3))
    col_forward().wait_recv()
    col_forward().wait_send()

    @pl.when(passes_atoms)
    def _():
        atom_pass().wait_send()

    @pl.when(across & (ahead_of_home != 0))
    def _():
        atom_pass().wait_recv()

    @pl.when(is_main)
    def _():
        for p in range(4):
            resid_send(p).wait_send()
        for p in range(7):
            col_send(p).wait_send()

    for role, copies in tree:

        @pl.when(role)
        def _():
            for k in range(3 * PARTS):
                for p in copies:
                    single_send(p, k).wait_send()

    @pl.when(not_main)
    def _():
        atom_copy(c).wait_send()

    @pl.when(to_next)
    def _():
        edge_copy(True, r + 1).wait_send()

    @pl.when(to_prev)
    def _():
        edge_copy(False, r - 1).wait_send()


def update_kernel(pair, row, col, atom, single, new_pair, atom_out, single_out, result, sem):
    small = [
        pltpu.make_async_copy(atom, atom_out, sem.at[0]),
    ] + [
        pltpu.make_async_copy(single.at[q], single_out.at[:, pl.ds(q * CH, CH)], sem.at[1 + q])
        for q in range(3)
    ]
    for copy in small:
        copy.start()
    width = col.shape[0]
    column = col[...]

    def out_copy(k):
        rows = pl.ds(k * BLOCK, BLOCK)
        return pltpu.make_async_copy(result.at[rows], new_pair.at[rows], sem.at[4 + k])

    @pl.loop(0, TOK // BLOCK)
    def _(k):
        terms = row[pl.ds(pl.multiple_of(k * BLOCK, BLOCK), BLOCK), :]
        for u in range(BLOCK):
            term = jnp.broadcast_to(terms[u : u + 1], (16, CH)).astype(BF16)
            term = jnp.concatenate([term] * (width // 16), axis=0)
            i = k * BLOCK + u
            result[i] = pair[i] + (column + term)
        out_copy(k).start()

    for copy in small:
        copy.wait()
    for k in range(TOK // BLOCK):
        out_copy(k).wait()


def shards(
    pair, counts, atom_single, w_bias, w_project, w_out, w_trans_in, w_trans_out, w_token, w_row, w_col
):
    any_ = pl.BlockSpec(memory_space=pl.ANY)
    vmem = pltpu.VMEM
    in_hbm = lambda a: pltpu.with_memory_space_constraint(a, pltpu.HBM)
    weights = (w_bias.T, w_project, w_out, w_trans_in, w_trans_out, w_token, w_row, w_col)
    in_vmem = pl.BlockSpec(memory_space=vmem)
    atom, single, row, col = pl.pallas_call(
        exchange_kernel,
        out_shape=(
            jax.ShapeDtypeStruct((OWN, CH), BF16),
            jax.ShapeDtypeStruct((3, TOK, CH), BF16),
            jax.ShapeDtypeStruct((TOK, CH), F32),
            jax.ShapeDtypeStruct((2 * TOK, CH), BF16),
        ),
        in_specs=[any_] * (3 + len(weights)),
        out_specs=(in_vmem,) * 4,
        scratch_shapes=[
            vmem((TOK, TOK, CH), BF16),
            vmem((HALF, TOK, CH), BF16),
            vmem(counts.shape, jnp.int32),
            *[vmem(w.shape, w.dtype) for w in weights],
            vmem((8 * (TOK + HALF + 1), TOK), F32),
            vmem((8 * (TOK + HALF + 1), TOK), F32),
            vmem((HEADS * HALF, TOK), BF16),
            vmem((HEADS * HALF, TOK), BF16),
            vmem((EXT, CH), BF16),
            vmem((ATOMS, CH), BF16),
            vmem((ATOMS * HEADS, TOK), BF16),
            vmem((len(EDGES) * WIN * HEADS, TOK), BF16),
            vmem((EXT, CH + 2 * TOK), BF16),
            vmem((EXT, 2 * CH), BF16),
            vmem((ATOMS, CH), F32),
            vmem((ATOMS, CH), BF16),
            vmem((ATOMS, CH), BF16),
            vmem((2 * OWN, CH), BF16),
            vmem((OWN, CH), BF16),
            vmem((ATOMS, CH), BF16),
            vmem((ATOMS, 3 * CH), BF16),
            vmem((TOK, ATOMS), BF16),
            pltpu.SemaphoreType.DMA((TOK // STEP,)),
            pltpu.SemaphoreType.DMA((2,)),
            pltpu.SemaphoreType.DMA((1 + len(weights),)),
            pltpu.SemaphoreType.DMA((2,)),
            pltpu.SemaphoreType.DMA((12 + 12 * PARTS + 7,)),
            pltpu.SemaphoreType.DMA((N_COL + 9 + 3 * PARTS,)),
        ],
        compiler_params=pltpu.CompilerParams(
            collective_id=0, has_side_effects=True, vmem_limit_bytes=40 * 2**20
        ),
    )(*[in_hbm(a) for a in (pair, atom_single, counts, *weights)])
    new_pair, atom_out, token_single = pl.pallas_call(
        update_kernel,
        out_shape=(
            jax.ShapeDtypeStruct(pair.shape, BF16),
            jax.ShapeDtypeStruct(atom.shape, BF16),
            jax.ShapeDtypeStruct((TOK, 3 * CH), BF16),
        ),
        in_specs=[in_vmem] * 5,
        out_specs=(any_,) * 3,
        scratch_shapes=[
            vmem(pair.shape, BF16),
            pltpu.SemaphoreType.DMA((4 + TOK // BLOCK,)),
        ],
        compiler_params=pltpu.CompilerParams(vmem_limit_bytes=UPDATE_VMEM * 2**20),
    )(pltpu.with_memory_space_constraint(pair, pltpu.VMEM), row, col, atom, single)
    return atom_out, token_single, new_pair


def solution(mesh):
    return jax.shard_map(
        shards,
        mesh=mesh,
        in_specs=(P("row", "col", None), P(), P(("row", "col"), None)) + (P(),) * 8,
        out_specs=(P(("row", "col"), None), P("row", None), P("row", "col", None)),
        check_vma=False,
    )
```
